128 devices in a mesh: dp: 4 (over y_lo, core), ctx: 32 (over y_hi, x, z).
Axes of the slice: x: 4, y: 4 (y_hi: 2, y_lo: 2; y = y_hi * 2 + y_lo), z: 4, core: 2. Of those that a mesh axis runs over, the one named last changes fastest.
Arguments:
- tokens: bfloat16 [4, 4096, 960], P('dp', 'ctx'), may hold values from -6 to 6
- positions: int32 [4, 4096], P('dp', 'ctx'), may hold values from 0 to 4095, as said below
- w_query: bfloat16 [960, 960], P('dp'), may hold values from -0.1875 to 0.1875
- key_weight: bfloat16 [960, 320], P('dp'), may hold values from -0.1875 to 0.1875
- value_weight: bfloat16 [960, 320], P('dp'), may hold values from -0.1875 to 0.1875
- w_output: bfloat16 [960, 960], P('dp'), may hold values from -2 to 2
- gain_attn: bfloat16 [960], P('dp'), may hold values from 0.5 to 1.5
- w_gate: bfloat16 [960, 2560], P('dp'), may hold values from -0.1875 to 0.1875
- w_up: bfloat16 [960, 2560], P('dp'), may hold values from -0.1875 to 0.1875
- w_down: bfloat16 [2560, 960], P('dp'), may hold values from -0.125 to 0.125
- gain_mlp: bfloat16 [960], P('dp'), may hold values from 0.5 to 1.5
- cotangent: bfloat16 [4, 4096, 960], P('dp', 'ctx'), may hold values from -6 to 6
Outputs:
- output: bfloat16 [4, 4096, 960], P('dp', 'ctx')
- grad_input: bfloat16 [4, 4096, 960], P('dp', 'ctx')
- grad_query: float32 [960, 960], P('dp')
- grad_key: float32 [960, 320], P('dp')
- grad_value: float32 [960, 320], P('dp')
- grad_output: float32 [960, 960], P('dp')
- grad_gain_attn: float32 [960], P('dp')
- grad_gate: float32 [960, 2560], P('dp')
- grad_up: float32 [960, 2560], P('dp')
- grad_down: float32 [2560, 960], P('dp')
- grad_gain_mlp: float32 [960], P('dp')
The draws below stay inside these ranges and needn't reach their ends.
Inputs may be any that keep to these rules, and one draw needn't show every extreme that they name: Each row holds every position 0 to 4095 exactly once; the 128 stored tokens of each device form two runs of 64 consecutive positions, ascending within a run.
All inputs are finite; a program needn't handle non-finite values.
Results may differ from the reference program's by a relative error of at most 0.035.
Values may be sent and summed in bfloat16 or wider, within the bound.
A program may use at most 192 MiB of HBM per device.

```python
import math
import jax
import jax.numpy as jnp
from jax import lax

MODEL_WIDTH = 960
HQ = 15
KEY_VALUE_HEADS = 5
HEAD_SIZE = 64
FF = 2560
TOK_DEV = 128
QUERY_PER_KV = 3
SEQS = 4
LENGTH = 4096


def draw_positions(key, part):
    key = jax.random.fold_in(key, 7)
    half_size = TOK_DEV // 2
    run_count = LENGTH // half_size
    seq_keys = jax.random.split(key, SEQS)
    orders = jax.vmap(lambda one_key: jax.random.permutation(one_key, run_count))(seq_keys)
    inside = jnp.arange(half_size, dtype=jnp.int32)
    placed = orders.astype(jnp.int32)[:, :, None] * half_size + inside[None, None, :]
    return placed.reshape(SEQS, LENGTH).astype(jnp.int32)


def steps_of(stream_key, extent, pieces, smallest, largest):
    level = 1.0
    for dim, blocks in pieces:
        heights = jax.random.uniform(jax.random.fold_in(jax.random.fold_in(stream_key, 6), dim), (blocks,), jnp.float32, smallest / len(pieces), largest / len(pieces))
        level = level * jnp.repeat(jnp.exp(heights), extent[dim] // blocks).reshape((-1,) + (1,) * (len(extent) - 1 - dim))
    return level


def centred(key, shape, deviation, reach, cuts=(), held_as=jnp.bfloat16):
    drawn = jax.random.normal(key, shape, jnp.float32) * deviation
    if len(cuts) > 0:
        drawn = steps_of(key, shape, cuts, -0.22, 0.18) * drawn
    return jnp.clip(drawn, min=-reach, max=reach).astype(held_as)


def setup_inputs(seed: int = 0) -> dict:
    splits = jax.random.split(jax.random.key(seed), 13)
    tokens = centred(splits[0], (SEQS, LENGTH, MODEL_WIDTH), 1.0, 6.0, ((0, 4), (1, 32)))
    positions = draw_positions(jax.random.fold_in(splits[12], 71), 0)
    w_query = centred(splits[2], (MODEL_WIDTH, HQ * HEAD_SIZE), MODEL_WIDTH ** -0.5, 0.1875, ((0, 4),))
    key_weight = centred(splits[3], (MODEL_WIDTH, KEY_VALUE_HEADS * HEAD_SIZE), MODEL_WIDTH ** -0.5, 0.1875, ((0, 4),))
    value_weight = centred(splits[4], (MODEL_WIDTH, KEY_VALUE_HEADS * HEAD_SIZE), MODEL_WIDTH ** -0.5, 0.1875, ((0, 4),))
    w_output = centred(splits[5], (HQ * HEAD_SIZE, MODEL_WIDTH), (HQ * HEAD_SIZE // 120) ** -0.5, 2.0, ((0, 4),))
    gain_attn = jnp.clip(1.0 + 0.1 * jax.random.normal(splits[6], (MODEL_WIDTH,), jnp.float32), 0.5, 1.5).astype(jnp.bfloat16)
    w_gate = centred(splits[7], (MODEL_WIDTH, FF), MODEL_WIDTH ** -0.5, 0.1875, ((0, 4),))
    w_up = centred(splits[8], (MODEL_WIDTH, FF), MODEL_WIDTH ** -0.5, 0.1875, ((0, 4),))
    w_down = centred(splits[9], (FF, MODEL_WIDTH), FF ** -0.5, 0.125, ((0, 4),))
    gain_mlp = jnp.clip(1.0 + 0.1 * jax.random.normal(splits[10], (MODEL_WIDTH,), jnp.float32), 0.5, 1.5).astype(jnp.bfloat16)
    cotangent = centred(splits[11], (SEQS, LENGTH, MODEL_WIDTH), 1.0, 6.0, ((0, 4), (1, 32)))
    return {"tokens": tokens, "positions": positions, "w_query": w_query, "key_weight": key_weight, "value_weight": value_weight, "w_output": w_output, "gain_attn": gain_attn, "w_gate": w_gate, "w_up": w_up, "w_down": w_down, "gain_mlp": gain_mlp, "cotangent": cotangent}


@jax.custom_vjp
def reduced_precision(v):
    return lax.optimization_barrier(v.astype(jnp.bfloat16)).astype(jnp.float32)

@jax.custom_vjp
def low_back(v):
    return v

def low_keep(v):
    return (reduced_precision(v), None)

def low_pass(kept, grad):
    return (grad,)

def back_keep(v):
    return (v, None)

def back_low(kept, grad):
    return (reduced_precision(grad),)
reduced_precision.defvjp(low_keep, low_pass)
low_back.defvjp(back_keep, back_low)

def apply_rotary(values, position_list, head_count):
    half_size = HEAD_SIZE // 2
    frequency = 100000.0 ** (-(jnp.arange(half_size, dtype=jnp.float32) * 2.0 / HEAD_SIZE))
    angles = position_list.astype(jnp.float32)[:, None] * frequency[None, :]
    cosine = jnp.cos(angles)[:, None, :]
    sine = jnp.sin(angles)[:, None, :]
    shaped = values.reshape(values.shape[0], head_count, HEAD_SIZE)
    first = shaped[..., :half_size]
    second = shaped[..., half_size:]
    turned = jnp.concatenate([first * cosine - second * sine, second * cosine + first * sine], axis=-1)
    return turned.reshape(values.shape[0], head_count * HEAD_SIZE)

def attention(rotated_queries, rotated_keys, value_reduced, position_list):
    length_tokens = rotated_queries.shape[0]
    block_index = math.gcd(length_tokens, 512)
    score_scale = 1.0 / math.sqrt(HEAD_SIZE)
    query_block_list = rotated_queries.reshape(length_tokens // block_index, block_index, KEY_VALUE_HEADS, QUERY_PER_KV, HEAD_SIZE)
    place_blocks = position_list.reshape(length_tokens // block_index, block_index)
    grouped_keys = rotated_keys.reshape(length_tokens, KEY_VALUE_HEADS, HEAD_SIZE)
    grouped_values = value_reduced.reshape(length_tokens, KEY_VALUE_HEADS, HEAD_SIZE)

    def one_block(pair_in):
        query_block, block_places = pair_in
        scores = jnp.einsum('tgjd,kgd->gjtk', query_block, grouped_keys, precision=lax.Precision.HIGHEST) * score_scale
        scores = low_back(scores)
        visible = block_places[:, None] >= position_list[None, :]
        masked = jnp.where(visible, scores, -1e+30)
        peak = lax.optimization_barrier(jnp.max(masked, axis=-1, keepdims=True))
        weights_exp = jnp.where(visible, jnp.exp(masked - peak), 0.0)
        total = lax.optimization_barrier(jnp.sum(weights_exp, axis=-1, keepdims=True))
        summed = low_back(jnp.einsum('gjtk,kgd->gjtd', reduced_precision(weights_exp), grouped_values, precision=lax.Precision.HIGHEST))
        return jnp.transpose(summed / total, (2, 0, 1, 3))
    blocks_out = lax.map(jax.checkpoint(one_block), (query_block_list, place_blocks))
    return blocks_out.reshape(length_tokens, HQ * HEAD_SIZE)

def matrix_product(left, right):
    return jnp.dot(left, right, precision=lax.Precision.HIGHEST)

def forward(inputs, position_list, w_query, key_weight, value_weight, w_output, gain_attn, w_gate, w_up, w_down, gain_mlp):
    inverse_one = lax.rsqrt(lax.optimization_barrier(jnp.mean(inputs * inputs, axis=-1)) + 1e-05)
    normed_one = reduced_precision(inputs * inverse_one[:, None] * gain_attn)
    query_raw = low_back(matrix_product(normed_one, w_query))
    unrotated_keys = low_back(matrix_product(normed_one, key_weight))
    value_reduced = reduced_precision(low_back(matrix_product(normed_one, value_weight)))
    rotated_queries = reduced_precision(apply_rotary(query_raw, position_list, HQ))
    rotated_keys = reduced_precision(apply_rotary(unrotated_keys, position_list, KEY_VALUE_HEADS))
    attended = reduced_precision(attention(rotated_queries, rotated_keys, value_reduced, position_list))
    middle = inputs + low_back(matrix_product(attended, w_output))
    inverse_two = lax.rsqrt(lax.optimization_barrier(jnp.mean(middle * middle, axis=-1)) + 1e-05)
    normed_two = reduced_precision(middle * inverse_two[:, None] * gain_mlp)
    gate = low_back(matrix_product(normed_two, w_gate))
    upper = low_back(matrix_product(normed_two, w_up))
    hidden = reduced_precision(jax.nn.silu(gate) * upper)
    return middle + low_back(matrix_product(hidden, w_down))

def reference(tokens, positions, w_query, key_weight, value_weight, w_output, gain_attn, w_gate, w_up, w_down, gain_mlp, cotangent):
    weight_list = tuple((w.astype(jnp.float32) for w in (w_query, key_weight, value_weight, w_output, gain_attn, w_gate, w_up, w_down, gain_mlp)))

    def per_sequence(totals, entry):
        seq_tokens, seq_places, seq_cotangent = entry

        def wrapped(inputs, *weights):
            return forward(inputs, seq_places, *weights)
        result, pull = jax.vjp(wrapped, seq_tokens.astype(jnp.float32), *weight_list)
        grads = pull(seq_cotangent.astype(jnp.float32))
        totals = tuple((left + right for left, right in zip(totals, grads[1:])))
        return (totals, (result.astype(jnp.bfloat16), grads[0].astype(jnp.bfloat16)))
    starting = tuple((jnp.zeros(w.shape, jnp.float32) for w in weight_list))
    totals, (results, input_grads) = lax.scan(per_sequence, starting, (tokens, positions, cotangent))
    return (results, input_grads, totals[0], totals[1], totals[2], totals[3], totals[4], totals[5], totals[6], totals[7], totals[8])
```

```python
import functools
import itertools
import math

import jax
import jax.numpy as jnp
from jax import lax
from jax.experimental import pallas as pl
from jax.experimental.pallas import tpu as pltpu
from jax.sharding import PartitionSpec as P

HQ = 15
KEY_VALUE_HEADS = 5
HEAD_SIZE = 64
QUERY_PER_KV = 3
MESH = pl.DeviceIdType.MESH
VMEM_LIMIT = 60 * 2**20
F32 = jnp.float32
BF16 = jnp.bfloat16
ROWS3 = 384


def coords():
    dp = lax.axis_index("dp")
    ctx = lax.axis_index("ctx")
    return dict(yl=dp // 2, c=dp % 2, yh=ctx // 16, x=(ctx // 4) % 4, z=ctx % 4)


def flip(t):
    return t + 1 - 2 * (t % 2)


def partner(co, d):
    new = dict(co)
    if d == "core":
        new["c"] = 1 - co["c"]
    elif d == "x1":
        new["x"] = flip(co["x"])
    elif d == "x3":
        new["x"] = 3 - co["x"]
    elif d == "z1":
        new["z"] = flip(co["z"])
    elif d == "z3":
        new["z"] = 3 - co["z"]
    else:
        if d in ("y1", "y3"):
            new["yl"] = 1 - co["yl"]
        if d in ("y2", "y3"):
            new["yh"] = 1 - co["yh"]
    return new


def device(co):
    return (co["yl"] * 2 + co["c"], co["yh"] * 16 + co["x"] * 4 + co["z"])


def spans(state, t):
    if state == "all":
        return [(0, 4)]
    if state == "both":
        return [(0, 2)]
    if state == "pair":
        return [(t - t % 2, 2)]
    if state == "anti":
        return [(t, 1), (3 - t, 1)]
    return [(t, 1)]


WIDTH = {"all": 4, "both": 2, "pair": 2, "anti": 2, "one": 1}


def less(state, d):
    new = dict(state)
    axis = d[0]
    if axis == "y":
        new["y"] = "one"
    elif state[axis] == "all":
        new[axis] = "anti" if d[1] == "1" else "pair"
    else:
        new[axis] = "one"
    return new


def more(state, d):
    new = dict(state)
    axis = d[0]
    if axis == "y":
        new["y"] = "both"
    elif state[axis] == "one":
        new[axis] = "pair" if d[1] == "1" else "anti"
    else:
        new[axis] = "all"
    return new


def boxes(state, co, ykey):
    out = []
    place_y = 0
    for ys, yn in spans(state["y"], co[ykey]):
        place_x = 0
        for xs, xn in spans(state["x"], co["x"]):
            place_z = 0
            for zs, zn in spans(state["z"], co["z"]):
                out.append(
                    (
                        (pl.ds(ys, yn), pl.ds(xs, xn), pl.ds(zs, zn)),
                        (pl.ds(place_y, yn), pl.ds(place_x, xn), pl.ds(place_z, zn)),
                        (yn, xn, zn),
                    )
                )
                place_z += zn
            place_x += xn
        place_y += yn
    return out


FULL = dict(y="both", x="all", z="all")
SINGLE = dict(y="one", x="one", z="one")


def order(ydim, part):
    dims = ["x1", "x3", "z1", "z3", ydim]
    return dims[part:] + dims[:part]


def rs_states(ydim, part):
    states = []
    state = FULL
    for d in order(ydim, part):
        state = less(state, d)
        states.append(state)
    return states


def rs_shapes(ydim, block):
    return [
        (WIDTH[s["y"]], WIDTH[s["x"]], WIDTH[s["z"]]) + block
        for part in range(5)
        for s in rs_states(ydim, part)
    ]


class Sems:
    def __init__(self, send, recv):
        self.send, self.recv, self.count = send, recv, 0

    def take(self):
        i = self.count
        self.count += 1
        return self.send.at[i], self.recv.at[i]

    def copy(self, src, dst, co):
        s, r = self.take()
        cp = pltpu.make_async_remote_copy(
            src_ref=src, dst_ref=dst, send_sem=s, recv_sem=r,
            device_id=device(co), device_id_type=MESH,
        )
        cp.start()
        return cp


def greet(co, dims):
    barrier = pltpu.get_barrier_semaphore()
    for d in dims:
        pl.semaphore_signal(
            barrier, inc=1, device_id=device(partner(co, d)), device_id_type=MESH
        )
    pl.semaphore_wait(barrier, len(dims))


class ReduceScatter:
    def __init__(self, acc, bufs, sems, co, ydim):
        self.acc, self.bufs, self.sems, self.co, self.ydim = acc, bufs, sems, co, ydim
        self.ykey = "yl" if ydim == "yl" else "yh"
        self.flying = {}
        self.sent = []

    def start(self, part, stage):
        d = order(self.ydim, part)[stage]
        state = rs_states(self.ydim, part)[stage]
        buf = self.bufs[part * 5 + stage]
        out = []
        if d == "yl":
            half = self.acc.shape[-2] // 2
            ways = [("y1", pl.ds(0, half)), ("y3", pl.ds(half, half))]
        else:
            ways = [(d, slice(None))]
        for way, rows in ways:
            to = partner(self.co, way)
            for box, place, _ in boxes(state, to, self.ykey):
                middle = (slice(None),) * (len(self.acc.shape) - 6)
                src = self.acc.at[box + (part,) + middle + (rows, slice(None))]
                dst = buf.at[place + middle + (rows, slice(None))]
                out.append(self.sems.copy(src, dst, to))
        self.flying[part, stage] = out
        self.sent += out

    def finish(self, part, stage):
        for cp in self.flying[part, stage]:
            cp.wait_recv()
        state = rs_states(self.ydim, part)[stage]
        buf = self.bufs[part * 5 + stage]
        for box, place, (yn, xn, zn) in boxes(state, self.co, self.ykey):
            (by, bx, bz), (py, px, pz) = box, place

            def add(i, carry):
                iy, ix, iz = i // (xn * zn), (i // zn) % xn, i % zn
                here = (by.start + iy, bx.start + ix, bz.start + iz, part)
                there = (py.start + iy, px.start + ix, pz.start + iz)
                self.acc[here] = (
                    self.acc[here].astype(F32) + buf[there].astype(F32)
                ).astype(BF16)
                return carry

            count = yn * xn * zn
            if count == 1:
                add(0, 0)
            else:
                lax.fori_loop(0, count, add, 0)

    def drain(self):
        for cp in self.sent:
            cp.wait_send()


class AllGather:
    def __init__(self, buf, sems, co, ydim="y2"):
        self.buf, self.sems, self.co, self.ydim = buf, sems, co, ydim
        self.flying = {}
        self.sent = []

    def start(self, part, stage):
        dims = order(self.ydim, part)
        state = SINGLE
        for d in dims[:stage]:
            state = more(state, d)
        to = partner(self.co, dims[stage])
        out = []
        for box, _, _ in boxes(state, self.co, "yh"):
            ref = self.buf.at[box + (part,)]
            out.append(self.sems.copy(ref, ref, to))
        self.flying[part, stage] = out
        self.sent += out

    def finish(self, part, stage):
        for cp in self.flying[part, stage]:
            cp.wait_recv()

    def drain(self):
        for cp in self.sent:
            cp.wait_send()


class Gather:
    def __init__(self, items, sems, local, co):
        self.items, self.sems, self.local, self.co = items, sems, local, co
        self.waits = []

    def start(self):
        co = self.co
        me = co["yl"] * 2 + co["c"]
        self.stage = []
        for i, (src, dst, n, h) in enumerate(self.items):
            base = pl.multiple_of(me * n, 16)
            cp = pltpu.make_async_copy(src, dst.at[pl.ds(base, n)], self.local.at[i])
            cp.start()
            self.waits.append(cp)
        for src, dst, n, h in self.items:
            base = pl.multiple_of(me * n, 16)
            one = self.sems.copy(
                src.at[pl.ds(0, h)], dst.at[pl.ds(base, h)], partner(co, "y1")
            )
            two = None
            if h < n:
                two = self.sems.copy(
                    src.at[pl.ds(h, n - h)],
                    dst.at[pl.ds(pl.multiple_of(base + h, 16), n - h)],
                    partner(co, "y3"),
                )
            self.stage.append((one, two))
        for src, dst, n, h in self.items:
            base = pl.multiple_of(me * n, 16)
            self.waits.append(
                self.sems.copy(src, dst.at[pl.ds(base, n)], partner(co, "core"))
            )

    def forward(self, i):
        co = self.co
        src, dst, n, h = self.items[i]
        base = ((1 - co["yl"]) * 2 + co["c"]) * n
        for cp, at, size in zip(self.stage[i], (0, h), (h, n - h)):
            if cp is None:
                continue
            cp.wait_recv()
            ref = dst.at[pl.ds(pl.multiple_of(base + at, 16), size)]
            self.waits.append(self.sems.copy(ref, ref, partner(co, "core")))

    def finish(self):
        for one, two in self.stage:
            one.wait_send()
            if two is not None:
                two.wait_send()
        for cp in self.waits:
            cp.wait()


def params(cid):
    return pltpu.CompilerParams(
        collective_id=cid, has_side_effects=True, vmem_limit_bytes=VMEM_LIMIT
    )


def dma_sems(n):
    return pltpu.SemaphoreType.DMA((n,))


ANY = pl.BlockSpec(memory_space=pl.ANY)
INV = pl.BlockSpec(memory_space=pltpu.VMEM)


def first_kernel(w_ref, gain_ref, pos_ref, w_out, gain_out, pos_out, send, recv, local, ps, pr):
    co = coords()
    dp, me = lax.axis_index("dp"), lax.axis_index("ctx")
    barrier = pltpu.get_barrier_semaphore()
    for d in ("core", "y1"):
        pl.semaphore_signal(
            barrier, inc=1, device_id=device(partner(co, d)), device_id_type=MESH
        )

    def hello(i, carry):
        to = (me + 1 + i) % 32
        pl.semaphore_signal(barrier, inc=1, device_id=(dp, to), device_id_type=MESH)
        return carry

    lax.fori_loop(0, 31, hello, 0)
    pl.semaphore_signal(
        barrier, inc=1, device_id=device(partner(co, "y3")), device_id_type=MESH
    )
    pl.semaphore_wait(barrier, 34)
    gather = Gather(
        [(w_ref, w_out, 240, 128), (gain_ref, gain_out, 16, 16)],
        Sems(send, recv), local, co,
    )
    gather.start()

    def put(i, carry):
        to = (me + 1 + i) % 32
        pltpu.make_async_remote_copy(
            src_ref=pos_ref, dst_ref=pos_out.at[me], send_sem=ps, recv_sem=pr,
            device_id=(dp, to), device_id_type=MESH,
        ).start()
        return carry

    lax.fori_loop(0, 31, put, 0)
    own = pltpu.make_async_copy(pos_ref, pos_out.at[me], local.at[2])
    own.start()
    gather.forward(0)
    gather.forward(1)
    gather.finish()
    own.wait()
    block = pos_out.at[pl.ds(0, 31)]
    pltpu.make_async_copy(block, block, ps).wait()
    pltpu.make_async_copy(block, block, pr).wait()


def first_call(w_one, gains, pos):
    return pl.pallas_call(
        first_kernel,
        out_shape=(
            jax.ShapeDtypeStruct((960, 1600), BF16),
            jax.ShapeDtypeStruct((64, 256), BF16),
            jax.ShapeDtypeStruct((32, 8, 128), jnp.int32),
        ),
        in_specs=[ANY] * 3,
        out_specs=[ANY] * 3,
        scratch_shapes=[
            dma_sems(8), dma_sems(8), dma_sems(3),
            pltpu.SemaphoreType.DMA, pltpu.SemaphoreType.DMA,
        ],
        compiler_params=params(1),
        name="gather_first",
    )(w_one, gains, pos)


CHUNK = 512


def over_dim0(left, right):
    return lax.dot_general(
        left, right, (((0,), (0,)), ((), ())), preferred_element_type=F32
    )


def forward_kernel(
    kv_ref, qt_ref, bias_ref, wo_ref, wg_ref, wu_ref, wd_ref,
    kv_all, u_ref, m_ref, l_ref, wo_all, wg_all, wu_all, wd_all,
    scores, send, recv, wsend, wrecv, local,
):
    co = coords()
    greet(co, ("x1", "x3", "z1", "z3", "y2", "core", "y1", "y3"))
    weights = Gather(
        [
            (wo_ref, wo_all, 240, 128),
            (wg_ref, wg_all, 240, 128),
            (wu_ref, wu_all, 240, 128),
            (wd_ref, wd_all, 640, 320),
        ],
        Sems(wsend, wrecv), local, co,
    )
    kv_all[co["yh"], co["x"], co["z"]] = kv_ref[...]
    ag = AllGather(kv_all, Sems(send, recv), co)
    for part in range(5):
        ag.start(part, 0)
    weights.start()
    for stage in range(1, 5):
        for part in range(5):
            ag.finish(part, stage - 1)
            ag.start(part, stage)
    for i in range(2):
        weights.forward(i)

    for g in range(KEY_VALUE_HEADS):
        ag.finish(g, 4)
        qt = qt_ref[g]

        def score(i, top):
            kv = kv_all[i // 4, i % 4, :, g].reshape(CHUNK, 128)
            s = jnp.dot(kv, qt, preferred_element_type=F32)
            b = bias_ref[pl.ds(i * CHUNK, CHUNK)]
            s = s + jnp.concatenate([b, b, b], axis=1)
            scores[pl.ds(i * CHUNK, CHUNK)] = s
            return jnp.maximum(top, jnp.max(s.reshape(CHUNK // 8, 8, ROWS3), axis=0))

        top = lax.fori_loop(0, 8, score, jnp.full((8, ROWS3), -1e30, F32))
        top = jnp.max(top, axis=0, keepdims=True)

        def weigh(i, carry):
            total, u = carry
            kv = kv_all[i // 4, i % 4, :, g].reshape(CHUNK, 128)
            e = jnp.exp(scores[pl.ds(i * CHUNK, CHUNK)] - top)
            total = total + jnp.sum(e.reshape(CHUNK // 8, 8, ROWS3), axis=0)
            return total, u + over_dim0(kv, e.astype(BF16))

        total, u = lax.fori_loop(
            0, 8, weigh, (jnp.zeros((8, ROWS3), F32), jnp.zeros((128, ROWS3), F32))
        )
        u_ref[g] = u
        m_ref[g] = top
        l_ref[g] = jnp.sum(total, axis=0, keepdims=True)
    for i in range(2, 4):
        weights.forward(i)
    ag.drain()
    weights.finish()


def forward_call(kv, qt, bias, wo, wg, wu, wd):
    shape = jax.ShapeDtypeStruct
    return pl.pallas_call(
        forward_kernel,
        out_shape=(
            shape((2, 4, 4, 5, 128, 128), BF16),
            shape((5, 128, ROWS3), F32),
            shape((5, 1, ROWS3), F32),
            shape((5, 1, ROWS3), F32),
            shape((960, 960), BF16),
            shape((960, 2560), BF16),
            shape((960, 2560), BF16),
            shape((2560, 960), BF16),
        ),
        in_specs=[INV] * 3 + [ANY] * 4,
        out_specs=[INV] * 4 + [ANY] * 4,
        scratch_shapes=[
            pltpu.VMEM((4096, ROWS3), F32),
            dma_sems(48), dma_sems(48), dma_sems(20), dma_sems(20), dma_sems(4),
        ],
        compiler_params=params(2),
        name="attention_forward",
    )(kv, qt, bias, wo, wg, wu, wd)


def backward_kernel(
    kv_ref, w_ref, wt_ref, bias_ref, m_ref, delta_ref,
    dq_ref, own_ref, acc, *rest,
):
    bufs, (send, recv) = rest[:25], rest[25:]
    co = coords()
    greet(co, ("x1", "x3", "z1", "z3", "y2"))
    rs = ReduceScatter(acc, bufs, Sems(send, recv), co, "y2")
    for g in range(KEY_VALUE_HEADS):
        w, wt = w_ref[g], wt_ref[g]
        top, delta = m_ref[g], delta_ref[g]

        def step(i, dq):
            kv = kv_ref[i // 4, i % 4, :, g].reshape(CHUNK, 128)
            both = jnp.dot(kv, w, preferred_element_type=F32)
            b = bias_ref[pl.ds(i * CHUNK, CHUNK)]
            s = both[:, :ROWS3] + jnp.concatenate([b, b, b], axis=1)
            e = jnp.exp(s - top)
            ds = (e * (both[:, ROWS3:] - delta)).astype(BF16)
            pair = jnp.concatenate([ds, e.astype(BF16)], axis=1)
            dkv = jnp.dot(pair, wt, preferred_element_type=F32)
            acc[i // 4, i % 4, :, g] = dkv.astype(BF16).reshape(4, 128, 128)
            return dq + over_dim0(kv, ds)

        dq_ref[g] = lax.fori_loop(0, 8, step, jnp.zeros((128, ROWS3), F32))
        rs.start(g, 0)
    for stage in range(5):
        for part in range(5):
            rs.finish(part, stage)
            if stage < 4:
                rs.start(part, stage + 1)
    own_ref[...] = acc[co["yh"], co["x"], co["z"]]
    rs.drain()


def backward_call(kv, w, wt, bias, m, delta):
    shape = jax.ShapeDtypeStruct
    return pl.pallas_call(
        backward_kernel,
        out_shape=(shape((5, 128, ROWS3), F32), shape((5, 128, 128), BF16)),
        in_specs=[INV] * 6,
        out_specs=[INV] * 2,
        scratch_shapes=[pltpu.VMEM((2, 4, 4, 5, 128, 128), BF16)]
        + [pltpu.VMEM(s, BF16) for s in rs_shapes("y2", (128, 128))]
        + [dma_sems(64), dma_sems(64)],
        compiler_params=params(3),
        name="attention_backward",
    )(kv, w, wt, bias, m, delta)


def fold_block(own, got, yl, x, z, p, wide):
    if wide:
        rows = 64 if x < 3 else 48
        lanes = pl.ds(pl.multiple_of(512 * p + 128 * z, 128), 128)
        at = (yl, pl.ds(64 * x, rows), lanes)
        s = own[at].astype(F32) + got[at].astype(F32)
        if x == 3:
            s = jnp.concatenate([s, jnp.zeros((16, 128), F32)], axis=0)
        return s.astype(BF16)
    rows = pl.ds(pl.multiple_of(128 * p + 32 * x, 16), 32)
    halves = []
    for h in range(2):
        first = 256 * z + 128 * h
        count = min(128, 960 - first)
        at = (yl, rows, pl.ds(first, count))
        s = own[at].astype(F32) + got[at].astype(F32)
        if count < 128:
            s = jnp.concatenate([s, jnp.zeros((32, 128 - count), F32)], axis=1)
        halves.append(s)
    return jnp.concatenate(halves, axis=0).astype(BF16)


def slab_rows(wide):
    return 240 if wide else 640


def grads_kernel(kinds, *refs):
    n = len(kinds)
    slabs, (out,) = refs[:n], refs[n:n + 1]
    rest = refs[n + 1:]
    owns, gots = rest[:n], rest[n:2 * n]
    acc = rest[2 * n]
    bufs = rest[2 * n + 1:2 * n + 26]
    last, send, recv, csend, crecv, local = rest[2 * n + 26:]
    co = coords()
    greet(co, ("x1", "x3", "z1", "z3", "y1", "y2", "y3", "core"))
    sems, core = Sems(send, recv), Sems(csend, crecv)
    cores, loads = [], []
    for i, wide in enumerate(kinds):
        rows = slab_rows(wide)
        for yl in range(2):
            other = pl.multiple_of((yl * 2 + 1 - co["c"]) * rows, 16)
            cores.append(
                core.copy(
                    slabs[i].at[pl.ds(other, rows)], gots[i].at[yl], partner(co, "core")
                )
            )
            mine = pl.multiple_of((yl * 2 + co["c"]) * rows, 16)
            cp = pltpu.make_async_copy(
                slabs[i].at[pl.ds(mine, rows)], owns[i].at[yl], local.at[2 * i + yl]
            )
            cp.start()
            loads.append(cp)
    rs = ReduceScatter(acc, bufs, sems, co, "yl")
    for i, wide in enumerate(kinds):
        for yl in range(2):
            loads[2 * i + yl].wait()
            cores[2 * i + yl].wait_recv()

            def fold(p, carry):
                for x in range(4):
                    for z in range(4):
                        acc[yl, x, z, p, i] = fold_block(
                            owns[i], gots[i], yl, x, z, p, wide
                        )
                return carry

            lax.fori_loop(0, 5, fold, 0)
    for part in range(5):
        rs.start(part, 0)
    for stage in range(5):
        for part in range(5):
            rs.finish(part, stage)
            if stage < 4:
                rs.start(part, stage + 1)
    yl, x, z, yh = co["yl"], co["x"], co["z"], co["yh"]
    mine = pl.ds(pl.multiple_of(yh * 32, 32), 32)
    theirs = pl.ds(pl.multiple_of((1 - yh) * 32, 32), 32)
    half = sems.copy(
        acc.at[yl, x, z, :, :, theirs, :], last, partner(co, "y2")
    )
    half.wait_recv()
    for p in range(5):
        out[yh, x, z, p] = (
            acc[yl, x, z, p, :, mine, :].astype(F32) + last[p].astype(F32)
        ).astype(BF16)
    ag = AllGather(out, sems, co)
    for part in range(5):
        ag.start(part, 0)
    for stage in range(5):
        for part in range(5):
            ag.finish(part, stage)
            if stage < 4:
                ag.start(part, stage + 1)
    half.wait_send()
    rs.drain()
    ag.drain()
    for cp in cores:
        cp.wait_send()


def grads_call(slabs, kinds, cid):
    n = len(slabs)
    blocks = [(2, 240, 2560) if wide else (2, 640, 960) for wide in kinds]
    return pl.pallas_call(
        functools.partial(grads_kernel, kinds),
        out_shape=jax.ShapeDtypeStruct((2, 4, 4, 5, n, 32, 128), BF16),
        in_specs=[ANY] * n,
        out_specs=INV,
        scratch_shapes=[pltpu.VMEM(b, BF16) for b in blocks]
        + [pltpu.VMEM(b, BF16) for b in blocks]
        + [pltpu.VMEM((2, 4, 4, 5, n, 64, 128), BF16)]
        + [pltpu.VMEM(s, BF16) for s in rs_shapes("yl", (n, 64, 128))]
        + [pltpu.VMEM((5, n, 32, 128), BF16)]
        + [dma_sems(128), dma_sems(128), dma_sems(2 * n), dma_sems(2 * n), dma_sems(2 * n)],
        compiler_params=params(cid),
        name="grads_" + str(n),
    )(*slabs)


def unpack_kernel(kinds, src, *outs):
    for i, wide in enumerate(kinds):
        def part(p, carry):
            for x in range(4):
                for z in range(4):
                    for yh in range(2):
                        block = src[yh, x, z, p, i].astype(F32)
                        if wide:
                            rows = min(32, 240 - 64 * x - 32 * yh)
                            lanes = pl.ds(pl.multiple_of(512 * p + 128 * z, 128), 128)
                            outs[i][pl.ds(64 * x + 32 * yh, rows), lanes] = block[:rows]
                        else:
                            first = 256 * z + 128 * yh
                            count = min(128, 960 - first)
                            rows = pl.ds(pl.multiple_of(128 * p + 32 * x, 8), 32)
                            outs[i][rows, pl.ds(first, count)] = block[:, :count]
            return carry

        lax.fori_loop(0, 5, part, 0)


def unpack_call(packed, kinds):
    return pl.pallas_call(
        functools.partial(unpack_kernel, kinds),
        out_shape=tuple(
            jax.ShapeDtypeStruct((240, 2560) if wide else (640, 960), F32) for wide in kinds
        ),
        in_specs=[INV],
        out_specs=[INV] * len(kinds),
        compiler_params=pltpu.CompilerParams(vmem_limit_bytes=VMEM_LIMIT),
        name="unpack",
    )(packed)


def rotation(position_list):
    half_size = HEAD_SIZE // 2
    frequency = 100000.0 ** (-(jnp.arange(half_size, dtype=F32) * 2.0 / HEAD_SIZE))
    angles = position_list.astype(F32)[:, None] * frequency[None, :]
    return jnp.cos(angles)[:, None, :], jnp.sin(angles)[:, None, :]


def apply_rotary(values, turn, head_count, backward):
    half_size = HEAD_SIZE // 2
    cosine, sine = turn
    if backward:
        sine = -sine
    shaped = values.reshape(values.shape[0], head_count, HEAD_SIZE)
    first = shaped[..., :half_size]
    second = shaped[..., half_size:]
    turned = jnp.concatenate(
        [first * cosine - second * sine, second * cosine + first * sine], axis=-1
    )
    return turned.reshape(values.shape[0], head_count * HEAD_SIZE)


def rms_inverse(rows_in):
    return lax.rsqrt(jnp.mean(rows_in * rows_in, axis=-1) + 1e-05)


def norm_back(grad_normed, inputs, inverse, gain_row):
    gain_grad = jnp.sum(grad_normed * inputs * inverse[:, None], axis=0)
    scaled = grad_normed * gain_row
    input_grad = inverse[:, None] * scaled - inputs * (inverse**3)[:, None] * jnp.mean(
        scaled * inputs, axis=-1, keepdims=True
    )
    return (input_grad, gain_grad)


def matrix_product(left, right):
    return jnp.dot(left, right, preferred_element_type=F32)


def by_group(rows):
    t = rows.shape[0]
    return (
        rows.reshape(t, KEY_VALUE_HEADS, QUERY_PER_KV, HEAD_SIZE)
        .transpose(1, 2, 0, 3)
        .reshape(KEY_VALUE_HEADS, ROWS3, HEAD_SIZE)
    )


def shards(
    tokens, positions, w_query, key_weight, value_weight, w_output, gain_attn,
    w_gate, w_up, w_down, gain_mlp, cotangent,
):
    t = tokens.shape[1]
    owned_positions = positions[0]
    w_one = jnp.concatenate([w_query, key_weight, value_weight], axis=1)
    gains = jnp.pad(jnp.stack([gain_attn, gain_mlp]), ((0, 14), (0, 16)))
    w_qkv, gains_all, pos_all = first_call(
        w_one, gains, jnp.broadcast_to(owned_positions[None], (8, 128))
    )
    gains_all = gains_all.reshape(4, 16, 256)[:, :2, :240].astype(F32)
    gain_one = gains_all[:, 0].reshape(960)
    gain_two = gains_all[:, 1].reshape(960)
    full_places = pos_all[:, 0, :].reshape(4096)
    bias = jnp.where(
        owned_positions[None, :] >= full_places[:, None], 0.0, -1e30
    ).astype(F32)

    inputs = tokens[0].astype(F32)
    inverse_one = rms_inverse(inputs)
    normed_one = (inputs * inverse_one[:, None] * gain_one).astype(BF16)
    qkv = matrix_product(normed_one, w_qkv)
    turn = rotation(owned_positions)
    queries = apply_rotary(qkv[:, :960], turn, HQ, False).astype(BF16)
    keys = apply_rotary(qkv[:, 960:1280], turn, KEY_VALUE_HEADS, False).astype(BF16)
    values = qkv[:, 1280:].astype(BF16)
    kv_own = jnp.concatenate(
        [keys.reshape(t, 5, 64), values.reshape(t, 5, 64)], axis=-1
    ).transpose(1, 0, 2)
    q_rows = by_group(queries * BF16(0.125))
    q_turned = q_rows.transpose(0, 2, 1)
    qt = jnp.concatenate([q_turned, jnp.zeros_like(q_turned)], axis=1)

    kv_all, u_all, top, total, wo_all, wg_all, wu_all, wd_all = forward_call(
        kv_own, qt, bias, w_output, w_gate, w_up, w_down
    )
    attended = u_all[:, 64:] / total
    attended_rows = (
        attended.reshape(5, 64, 3, t).transpose(3, 0, 2, 1).reshape(t, 960).astype(BF16)
    )
    middle = inputs + matrix_product(attended_rows, wo_all)
    inverse_two = rms_inverse(middle)
    normed_two = (middle * inverse_two[:, None] * gain_two).astype(BF16)
    gate = matrix_product(normed_two, wg_all)
    upper = matrix_product(normed_two, wu_all)
    sigma = jax.nn.sigmoid(gate)
    hidden = (gate * sigma * upper).astype(BF16)
    result = (middle + matrix_product(hidden, wd_all)).astype(BF16)[None]

    grad_low = cotangent[0]
    grad_out = grad_low.astype(F32)
    term_down = matrix_product(hidden.T, grad_low).astype(BF16)
    grad_hidden = matrix_product(grad_low, wd_all.T)
    grad_gate_low = (grad_hidden * upper * sigma * (1.0 + gate * (1.0 - sigma))).astype(BF16)
    grad_upper_low = (grad_hidden * gate * sigma).astype(BF16)
    term_gate = matrix_product(normed_two.T, grad_gate_low).astype(BF16)
    term_up = matrix_product(normed_two.T, grad_upper_low).astype(BF16)
    grad_normed_two = matrix_product(grad_gate_low, wg_all.T) + matrix_product(
        grad_upper_low, wu_all.T
    )
    norm_grad_two, term_gain_two = norm_back(grad_normed_two, middle, inverse_two, gain_two)
    grad_middle = grad_out + norm_grad_two
    branch_gradient = grad_middle.astype(BF16)
    term_output = matrix_product(attended_rows.T, branch_gradient).astype(BF16)
    grad_attended = (
        matrix_product(branch_gradient, wo_all.T)
        .reshape(t, 5, 3, 64)
        .transpose(1, 3, 2, 0)
        .reshape(5, 64, ROWS3)
    )
    du_turned = (grad_attended / total).astype(BF16)
    delta = jnp.sum(grad_attended * attended, axis=1, keepdims=True) / total
    w_back = jnp.concatenate(
        [
            jnp.concatenate([q_turned, jnp.zeros_like(q_turned)], axis=2),
            jnp.concatenate([jnp.zeros_like(du_turned), du_turned], axis=2),
        ],
        axis=1,
    )
    dq_turned, own_pairs = backward_call(
        kv_all, w_back, w_back.transpose(0, 2, 1), bias, top, delta
    )
    query_rows = (
        (dq_turned[:, :64] * 0.125)
        .reshape(5, 64, 3, t)
        .transpose(3, 0, 2, 1)
        .reshape(t, 960)
    )
    pairs = own_pairs.transpose(1, 0, 2)
    grad_query_low = apply_rotary(query_rows, turn, HQ, True).astype(BF16)
    grad_key_low = apply_rotary(
        pairs[..., :64].reshape(t, 320).astype(F32), turn, KEY_VALUE_HEADS, True
    ).astype(BF16)
    grad_value_low = pairs[..., 64:].reshape(t, 320)
    grad_qkv = jnp.concatenate([grad_query_low, grad_key_low, grad_value_low], axis=1)
    term_qkv = matrix_product(normed_one.T, grad_qkv).astype(BF16)
    grad_normed_one = matrix_product(grad_qkv, w_qkv.T)
    norm_grad_one, term_gain_one = norm_back(grad_normed_one, inputs, inverse_one, gain_one)
    grad_input = (grad_middle + norm_grad_one).astype(BF16)[None]

    term_gains = lax.psum(
        jnp.stack([term_gain_one, term_gain_two]), ("dp", "ctx")
    ).reshape(2, 4, 240)
    mine = lax.dynamic_index_in_dim(term_gains, lax.axis_index("dp"), 1, keepdims=False)

    kinds = (True, True, True, False)
    packed = grads_call(
        [jnp.concatenate([term_qkv, term_output], axis=1), term_gate, term_up, term_down],
        kinds, 4,
    )
    first, sum_gate, sum_up, sum_down = unpack_call(packed, kinds)
    return (
        result, grad_input,
        first[:, :960], first[:, 960:1280], first[:, 1280:1600], first[:, 1600:],
        mine[0], sum_gate, sum_up, sum_down, mine[1],
    )


def solution(mesh):
    in_specs = (
        P("dp", "ctx", None), P("dp", "ctx"),
        P("dp", None), P("dp", None), P("dp", None), P("dp", None), P("dp"),
        P("dp", None), P("dp", None), P("dp", None), P("dp"),
        P("dp", "ctx", None),
    )
    out_specs = (
        P("dp", "ctx", None), P("dp", "ctx", None),
        P("dp", None), P("dp", None), P("dp", None), P("dp", None), P("dp"),
        P("dp", None), P("dp", None), P("dp", None), P("dp"),
    )
    return jax.shard_map(shards, mesh=mesh, in_specs=in_specs, out_specs=out_specs, check_vma=False)
```

```python
import functools
import itertools
import math

import jax
import jax.numpy as jnp
from jax import lax
from jax.experimental import pallas as pl
from jax.experimental.pallas import tpu as pltpu
from jax.sharding import PartitionSpec as P

HQ = 15
KEY_VALUE_HEADS = 5
HEAD_SIZE = 64
QUERY_PER_KV = 3
MESH = pl.DeviceIdType.MESH
VMEM_LIMIT = 60 * 2**20
F32 = jnp.float32
BF16 = jnp.bfloat16
ROWS3 = 384


def coords():
    dp = lax.axis_index("dp")
    ctx = lax.axis_index("ctx")
    return dict(yl=dp // 2, c=dp % 2, yh=ctx // 16, x=(ctx // 4) % 4, z=ctx % 4)


def flip(t):
    return t + 1 - 2 * (t % 2)


def partner(co, d):
    new = dict(co)
    if d == "core":
        new["c"] = 1 - co["c"]
    elif d == "x1":
        new["x"] = flip(co["x"])
    elif d == "x3":
        new["x"] = 3 - co["x"]
    elif d == "z1":
        new["z"] = flip(co["z"])
    elif d == "z3":
        new["z"] = 3 - co["z"]
    else:
        if d in ("y1", "y3"):
            new["yl"] = 1 - co["yl"]
        if d in ("y2", "y3"):
            new["yh"] = 1 - co["yh"]
    return new


def device(co):
    return (co["yl"] * 2 + co["c"], co["yh"] * 16 + co["x"] * 4 + co["z"])


def spans(state, t):
    if state == "all":
        return [(0, 4)]
    if state == "both":
        return [(0, 2)]
    if state == "pair":
        return [(t - t % 2, 2)]
    if state == "anti":
        return [(t, 1), (3 - t, 1)]
    return [(t, 1)]


WIDTH = {"all": 4, "both": 2, "pair": 2, "anti": 2, "one": 1}


def less(state, d):
    new = dict(state)
    axis = d[0]
    if axis == "y":
        new["y"] = "one"
    elif state[axis] == "all":
        new[axis] = "anti" if d[1] == "1" else "pair"
    else:
        new[axis] = "one"
    return new


def more(state, d):
    new = dict(state)
    axis = d[0]
    if axis == "y":
        new["y"] = "both"
    elif state[axis] == "one":
        new[axis] = "pair" if d[1] == "1" else "anti"
    else:
        new[axis] = "all"
    return new


def boxes(state, co, ykey):
    out = []
    place_y = 0
    for ys, yn in spans(state["y"], co[ykey]):
        place_x = 0
        for xs, xn in spans(state["x"], co["x"]):
            place_z = 0
            for zs, zn in spans(state["z"], co["z"]):
                out.append(
                    (
                        (pl.ds(ys, yn), pl.ds(xs, xn), pl.ds(zs, zn)),
                        (pl.ds(place_y, yn), pl.ds(place_x, xn), pl.ds(place_z, zn)),
                        (yn, xn, zn),
                    )
                )
                place_z += zn
            place_x += xn
        place_y += yn
    return out


FULL = dict(y="both", x="all", z="all")
SINGLE = dict(y="one", x="one", z="one")


def order(ydim, part):
    dims = ["x1", "x3", "z1", "z3", ydim]
    return dims[part:] + dims[:part]


def rs_states(ydim, part):
    states = []
    state = FULL
    for d in order(ydim, part):
        state = less(state, d)
        states.append(state)
    return states


def rs_shapes(ydim, block):
    return [
        (WIDTH[s["y"]], WIDTH[s["x"]], WIDTH[s["z"]]) + block
        for part in range(5)
        for s in rs_states(ydim, part)
    ]


class Sems:
    def __init__(self, send, recv):
        self.send, self.recv, self.count = send, recv, 0

    def take(self):
        i = self.count
        self.count += 1
        return self.send.at[i], self.recv.at[i]

    def copy(self, src, dst, co):
        s, r = self.take()
        cp = pltpu.make_async_remote_copy(
            src_ref=src, dst_ref=dst, send_sem=s, recv_sem=r,
            device_id=device(co), device_id_type=MESH,
        )
        cp.start()
        return cp


def greet(co, dims):
    barrier = pltpu.get_barrier_semaphore()
    for d in dims:
        pl.semaphore_signal(
            barrier, inc=1, device_id=device(partner(co, d)), device_id_type=MESH
        )
    pl.semaphore_wait(barrier, len(dims))


class ReduceScatter:
    def __init__(self, acc, bufs, sems, co, ydim):
        self.acc, self.bufs, self.sems, self.co, self.ydim = acc, bufs, sems, co, ydim
        self.ykey = "yl" if ydim == "yl" else "yh"
        self.flying = {}
        self.sent = []

    def start(self, part, stage):
        d = order(self.ydim, part)[stage]
        state = rs_states(self.ydim, part)[stage]
        buf = self.bufs[part * 5 + stage]
        out = []
        if d == "yl":
            half = self.acc.shape[-2] // 2
            ways = [("y1", pl.ds(0, half)), ("y3", pl.ds(half, half))]
        else:
            ways = [(d, slice(None))]
        for way, rows in ways:
            to = partner(self.co, way)
            for box, place, _ in boxes(state, to, self.ykey):
                middle = (slice(None),) * (len(self.acc.shape) - 6)
                src = self.acc.at[box + (part,) + middle + (rows, slice(None))]
                dst = buf.at[place + middle + (rows, slice(None))]
                out.append(self.sems.copy(src, dst, to))
        self.flying[part, stage] = out
        self.sent += out

    def finish(self, part, stage):
        for cp in self.flying[part, stage]:
            cp.wait_recv()
        state = rs_states(self.ydim, part)[stage]
        buf = self.bufs[part * 5 + stage]
        for box, place, (yn, xn, zn) in boxes(state, self.co, self.ykey):
            (by, bx, bz), (py, px, pz) = box, place

            def add(i, carry):
                iy, ix, iz = i // (xn * zn), (i // zn) % xn, i % zn
                here = (by.start + iy, bx.start + ix, bz.start + iz, part)
                there = (py.start + iy, px.start + ix, pz.start + iz)
                self.acc[here] = (
                    self.acc[here].astype(F32) + buf[there].astype(F32)
                ).astype(BF16)
                return carry

            count = yn * xn * zn
            if count == 1:
                add(0, 0)
            else:
                lax.fori_loop(0, count, add, 0)

    def drain(self):
        for cp in self.sent:
            cp.wait_send()


class AllGather:
    def __init__(self, buf, sems, co, ydim="y2"):
        self.buf, self.sems, self.co, self.ydim = buf, sems, co, ydim
        self.flying = {}
        self.sent = []

    def start(self, part, stage):
        dims = order(self.ydim, part)
        state = SINGLE
        for d in dims[:stage]:
            state = more(state, d)
        to = partner(self.co, dims[stage])
        out = []
        for box, _, _ in boxes(state, self.co, "yh"):
            ref = self.buf.at[box + (part,)]
            out.append(self.sems.copy(ref, ref, to))
        self.flying[part, stage] = out
        self.sent += out

    def finish(self, part, stage):
        for cp in self.flying[part, stage]:
            cp.wait_recv()

    def drain(self):
        for cp in self.sent:
            cp.wait_send()


class PlaneGather:
    DIMS = ["x1", "x3", "z1", "z3"]

    def __init__(self, buf, sems, co):
        self.buf, self.sems, self.co = buf, sems, co
        self.flying = {}
        self.sent = []

    def first(self):
        co = self.co
        ref = self.buf.at[co["yh"], co["x"], co["z"]]
        self.sent.append(self.sems.copy(ref, ref, partner(co, "y2")))
        self.sent[0].wait_recv()

    def start(self, part, stage):
        dims = self.DIMS[part:] + self.DIMS[:part]
        state = dict(y="both", x="one", z="one")
        for d in dims[:stage]:
            state = more(state, d)
        to = partner(self.co, dims[stage])
        rows = pl.ds(32 * part, 32)
        groups = range(5) if stage == 3 else [slice(None)]
        for g in groups:
            out = []
            for box, _, _ in boxes(state, self.co, "yh"):
                ref = self.buf.at[box + (g, rows)]
                out.append(self.sems.copy(ref, ref, to))
            self.flying[part, stage, g if stage == 3 else 0] = out
            self.sent += out

    def finish(self, part, stage, g=0):
        for cp in self.flying[part, stage, g]:
            cp.wait_recv()

    def drain(self):
        for cp in self.sent:
            cp.wait_send()


class Gather:
    def __init__(self, items, sems, local, co):
        self.items, self.sems, self.local, self.co = items, sems, local, co
        self.waits = []

    def start(self):
        co = self.co
        me = co["yl"] * 2 + co["c"]
        self.stage = []
        for i, (src, dst, n, h) in enumerate(self.items):
            base = pl.multiple_of(me * n, 16)
            cp = pltpu.make_async_copy(src, dst.at[pl.ds(base, n)], self.local.at[i])
            cp.start()
            self.waits.append(cp)
        for src, dst, n, h in self.items:
            base = pl.multiple_of(me * n, 16)
            one = self.sems.copy(
                src.at[pl.ds(0, h)], dst.at[pl.ds(base, h)], partner(co, "y1")
            )
            two = None
            if h < n:
                two = self.sems.copy(
                    src.at[pl.ds(h, n - h)],
                    dst.at[pl.ds(pl.multiple_of(base + h, 16), n - h)],
                    partner(co, "y3"),
                )
            self.stage.append((one, two))
        for src, dst, n, h in self.items:
            base = pl.multiple_of(me * n, 16)
            self.waits.append(
                self.sems.copy(src, dst.at[pl.ds(base, n)], partner(co, "core"))
            )

    def forward(self, i):
        co = self.co
        src, dst, n, h = self.items[i]
        base = ((1 - co["yl"]) * 2 + co["c"]) * n
        for cp, at, size in zip(self.stage[i], (0, h), (h, n - h)):
            if cp is None:
                continue
            cp.wait_recv()
            ref = dst.at[pl.ds(pl.multiple_of(base + at, 16), size)]
            self.waits.append(self.sems.copy(ref, ref, partner(co, "core")))

    def finish(self):
        for one, two in self.stage:
            one.wait_send()
            if two is not None:
                two.wait_send()
        for cp in self.waits:
            cp.wait()


def params(cid):
    return pltpu.CompilerParams(
        collective_id=cid, has_side_effects=True, vmem_limit_bytes=VMEM_LIMIT
    )


def dma_sems(n):
    return pltpu.SemaphoreType.DMA((n,))


ANY = pl.BlockSpec(memory_space=pl.ANY)
INV = pl.BlockSpec(memory_space=pltpu.VMEM)


def first_kernel(w_ref, gain_ref, pos_ref, w_out, gain_out, pos_out, send, recv, local, ps, pr):
    co = coords()
    dp, me = lax.axis_index("dp"), lax.axis_index("ctx")
    barrier = pltpu.get_barrier_semaphore()
    for d in ("core", "y1"):
        pl.semaphore_signal(
            barrier, inc=1, device_id=device(partner(co, d)), device_id_type=MESH
        )

    def hello(i, carry):
        to = (me + 1 + i) % 32
        pl.semaphore_signal(barrier, inc=1, device_id=(dp, to), device_id_type=MESH)
        return carry

    lax.fori_loop(0, 31, hello, 0)
    pl.semaphore_signal(
        barrier, inc=1, device_id=device(partner(co, "y3")), device_id_type=MESH
    )
    pl.semaphore_wait(barrier, 34)
    gather = Gather(
        [(w_ref, w_out, 240, 128), (gain_ref, gain_out, 16, 16)],
        Sems(send, recv), local, co,
    )
    gather.start()

    def put(i, carry):
        to = (me + 1 + i) % 32
        pltpu.make_async_remote_copy(
            src_ref=pos_ref, dst_ref=pos_out.at[me], send_sem=ps, recv_sem=pr,
            device_id=(dp, to), device_id_type=MESH,
        ).start()
        return carry

    lax.fori_loop(0, 31, put, 0)
    own = pltpu.make_async_copy(pos_ref, pos_out.at[me], local.at[2])
    own.start()
    gather.forward(0)
    gather.forward(1)
    gather.finish()
    own.wait()
    block = pos_out.at[pl.ds(0, 31)]
    pltpu.make_async_copy(block, block, ps).wait()
    pltpu.make_async_copy(block, block, pr).wait()


def first_call(w_one, gains, pos):
    return pl.pallas_call(
        first_kernel,
        out_shape=(
            jax.ShapeDtypeStruct((960, 1600), BF16),
            jax.ShapeDtypeStruct((64, 256), BF16),
            jax.ShapeDtypeStruct((32, 8, 128), jnp.int32),
        ),
        in_specs=[INV] * 3,
        out_specs=[ANY] * 3,
        scratch_shapes=[
            dma_sems(8), dma_sems(8), dma_sems(3),
            pltpu.SemaphoreType.DMA, pltpu.SemaphoreType.DMA,
        ],
        compiler_params=params(1),
        name="gather_first",
    )(w_one, gains, pos)


CHUNK = 512


def over_dim0(left, right):
    return lax.dot_general(
        left, right, (((0,), (0,)), ((), ())), preferred_element_type=F32
    )


def forward_kernel(
    kv_ref, qt_ref, bias_ref, wo_ref, wg_ref, wu_ref, wd_ref,
    kv_all, u_ref, m_ref, l_ref, wo_all, wg_all, wu_all, wd_all,
    scores, send, recv, wsend, wrecv, local,
):
    co = coords()
    greet(co, ("x1", "x3", "z1", "z3", "y2", "core", "y1", "y3"))
    weights = Gather(
        [
            (wo_ref, wo_all, 240, 128),
            (wg_ref, wg_all, 240, 128),
            (wu_ref, wu_all, 240, 128),
            (wd_ref, wd_all, 640, 320),
        ],
        Sems(wsend, wrecv), local, co,
    )
    kv_all[co["yh"], co["x"], co["z"]] = kv_ref[...]
    ag = PlaneGather(kv_all, Sems(send, recv), co)
    ag.first()
    for part in range(4):
        ag.start(part, 0)
    weights.start()
    for stage in range(1, 4):
        for part in range(4):
            ag.finish(part, stage - 1)
            ag.start(part, stage)

    for g in range(KEY_VALUE_HEADS):
        for part in range(4):
            ag.finish(part, 3, g)
        if g > 0:
            weights.forward(g - 1)
        qt = qt_ref[g]

        def score(i, top):
            kv = kv_all[i // 4, i % 4, :, g].reshape(CHUNK, 128)
            s = jnp.dot(kv, qt, preferred_element_type=F32)
            b = bias_ref[pl.ds(i * CHUNK, CHUNK)]
            s = s + jnp.concatenate([b, b, b], axis=1)
            scores[pl.ds(i * CHUNK, CHUNK)] = s
            return jnp.maximum(top, jnp.max(s.reshape(CHUNK // 8, 8, ROWS3), axis=0))

        top = lax.fori_loop(0, 8, score, jnp.full((8, ROWS3), -1e30, F32))
        top = jnp.max(top, axis=0, keepdims=True)

        def weigh(i, carry):
            total, u = carry
            kv = kv_all[i // 4, i % 4, :, g].reshape(CHUNK, 128)
            e = jnp.exp(scores[pl.ds(i * CHUNK, CHUNK)] - top)
            total = total + jnp.sum(e.reshape(CHUNK // 8, 8, ROWS3), axis=0)
            return total, u + over_dim0(kv, e.astype(BF16))

        total, u = lax.fori_loop(
            0, 8, weigh, (jnp.zeros((8, ROWS3), F32), jnp.zeros((128, ROWS3), F32))
        )
        u_ref[g] = u
        m_ref[g] = top
        l_ref[g] = jnp.sum(total, axis=0, keepdims=True)
    ag.drain()
    weights.finish()


def forward_call(kv, qt, bias, wo, wg, wu, wd):
    shape = jax.ShapeDtypeStruct
    return pl.pallas_call(
        forward_kernel,
        out_shape=(
            shape((2, 4, 4, 5, 128, 128), BF16),
            shape((5, 128, ROWS3), F32),
            shape((5, 1, ROWS3), F32),
            shape((5, 1, ROWS3), F32),
            shape((960, 960), BF16),
            shape((960, 2560), BF16),
            shape((960, 2560), BF16),
            shape((2560, 960), BF16),
        ),
        in_specs=[INV] * 7,
        out_specs=[INV] * 4 + [ANY] * 4,
        scratch_shapes=[
            pltpu.VMEM((4096, ROWS3), F32),
            dma_sems(96), dma_sems(96), dma_sems(20), dma_sems(20), dma_sems(4),
        ],
        compiler_params=params(2),
        name="attention_forward",
    )(kv, qt, bias, wo, wg, wu, wd)


WIDE, TALL, GAIN = 240, 640, 256


def slab_shape(kind):
    return (640, 960) if kind == TALL else (kind, 2560)


def fold_block(own, got, yl, x, z, p, kind):
    if kind != TALL:
        rows = min(64, kind - 64 * x)
        lanes = pl.ds(pl.multiple_of(512 * p + 128 * z, 128), 128)
        at = (yl, pl.ds(64 * x, rows), lanes)
        s = own[at].astype(F32) + got[at].astype(F32)
        if rows < 64:
            s = jnp.concatenate([s, jnp.zeros((64 - rows, 128), F32)], axis=0)
        return s.astype(BF16)
    rows = pl.ds(pl.multiple_of(128 * p + 32 * x, 16), 32)
    halves = []
    for h in range(2):
        first = 256 * z + 128 * h
        count = min(128, 960 - first)
        at = (yl, rows, pl.ds(first, count))
        s = own[at].astype(F32) + got[at].astype(F32)
        if count < 128:
            s = jnp.concatenate([s, jnp.zeros((32, 128 - count), F32)], axis=1)
        halves.append(s)
    return jnp.concatenate(halves, axis=0).astype(BF16)


GRAD_DIMS = ("x1", "x3", "z1", "z3", "y1", "y2", "y3", "core")


def grad_scratch(kinds):
    n = len(kinds)
    blocks = [(2,) + slab_shape(kind) for kind in kinds]
    return (
        [pltpu.VMEM(b, BF16) for b in blocks]
        + [pltpu.VMEM(b, BF16) for b in blocks]
        + [pltpu.VMEM((2, 4, 4, 5, n, 64, 128), BF16)]
        + [pltpu.VMEM(s, BF16) for s in rs_shapes("yl", (n, 64, 128))]
        + [pltpu.VMEM((5, n, 32, 128), BF16)]
        + [dma_sems(64), dma_sems(64), dma_sems(2 * n), dma_sems(2 * n), dma_sems(2 * n)]
    )


def grad_scratch_count(kinds):
    return 2 * len(kinds) + 32


class GradSum:
    def __init__(self, kinds, slabs, scratch, co):
        n = len(kinds)
        self.kinds, self.slabs, self.co = kinds, slabs, co
        self.owns, self.gots = scratch[:n], scratch[n:2 * n]
        self.acc = scratch[2 * n]
        bufs = scratch[2 * n + 1:2 * n + 26]
        self.last, send, recv, csend, crecv, self.local = scratch[2 * n + 26:]
        self.sems, self.core = Sems(send, recv), Sems(csend, crecv)
        self.rs = ReduceScatter(self.acc, bufs, self.sems, co, "yl")

    def begin(self):
        co = self.co
        self.cores, self.loads = [], []
        for i, kind in enumerate(self.kinds):
            rows = slab_shape(kind)[0]
            for yl in range(2):
                other = pl.multiple_of((yl * 2 + 1 - co["c"]) * rows, 16)
                self.cores.append(
                    self.core.copy(
                        self.slabs[i].at[pl.ds(other, rows)],
                        self.gots[i].at[yl],
                        partner(co, "core"),
                    )
                )
                mine = pl.multiple_of((yl * 2 + co["c"]) * rows, 16)
                cp = pltpu.make_async_copy(
                    self.slabs[i].at[pl.ds(mine, rows)],
                    self.owns[i].at[yl],
                    self.local.at[2 * i + yl],
                )
                cp.start()
                self.loads.append(cp)

    def fold(self):
        for i, kind in enumerate(self.kinds):
            for yl in range(2):
                self.loads[2 * i + yl].wait()
                self.cores[2 * i + yl].wait_recv()

                def step(p, carry):
                    for x in range(4):
                        for z in range(4):
                            self.acc[yl, x, z, p, i] = fold_block(
                                self.owns[i], self.gots[i], yl, x, z, p, kind
                            )
                    return carry

                lax.fori_loop(0, 5, step, 0)
        for part in range(5):
            self.rs.start(part, 0)

    def stage(self, stage):
        for part in range(5):
            self.rs.finish(part, stage)
            if stage < 4:
                self.rs.start(part, stage + 1)

    def halve(self):
        co = self.co
        theirs = pl.ds(pl.multiple_of((1 - co["yh"]) * 32, 32), 32)
        self.half = self.sems.copy(
            self.acc.at[co["yl"], co["x"], co["z"], :, :, theirs, :],
            self.last,
            partner(co, "y2"),
        )

    def result(self, p):
        co = self.co
        mine = pl.ds(pl.multiple_of(co["yh"] * 32, 32), 32)
        own = self.acc[co["yl"], co["x"], co["z"], p, :, mine, :]
        return (own.astype(F32) + self.last[p].astype(F32)).astype(BF16)

    def drain(self):
        self.half.wait_send()
        self.rs.drain()
        for cp in self.cores:
            cp.wait_send()


MLP = (WIDE, WIDE, TALL)


def backward_kernel(
    kv_ref, w_ref, wt_ref, bias_ref, m_ref, delta_ref, gate_ref, up_ref, down_ref,
    dq_ref, own_ref, mlp_ref, acc, *rest,
):
    bufs, (send, recv) = rest[:25], rest[25:27]
    co = coords()
    greet(co, GRAD_DIMS)
    mlp = GradSum(MLP, (gate_ref, up_ref, down_ref), rest[27:], co)
    mlp.begin()
    rs = ReduceScatter(acc, bufs, Sems(send, recv), co, "y2")
    for g in range(KEY_VALUE_HEADS):
        w, wt = w_ref[g], wt_ref[g]
        top, delta = m_ref[g], delta_ref[g]

        def step(i, dq):
            kv = kv_ref[i // 4, i % 4, :, g].reshape(CHUNK, 128)
            both = jnp.dot(kv, w, preferred_element_type=F32)
            b = bias_ref[pl.ds(i * CHUNK, CHUNK)]
            s = both[:, :ROWS3] + jnp.concatenate([b, b, b], axis=1)
            e = jnp.exp(s - top)
            ds = (e * (both[:, ROWS3:] - delta)).astype(BF16)
            pair = jnp.concatenate([ds, e.astype(BF16)], axis=1)
            dkv = jnp.dot(pair, wt, preferred_element_type=F32)
            acc[i // 4, i % 4, :, g] = dkv.astype(BF16).reshape(4, 128, 128)
            return dq + over_dim0(kv, ds)

        dq_ref[g] = lax.fori_loop(0, 8, step, jnp.zeros((128, ROWS3), F32))
        if g == 1:
            mlp.fold()
        if g == 3:
            mlp.stage(0)
        rs.start(g, 0)
    mlp.stage(1)
    for part in range(5):
        rs.finish(part, 0)
        rs.start(part, 1)
    mlp.stage(2)
    for part in range(5):
        rs.finish(part, 1)
        rs.start(part, 2)
    mlp.stage(3)
    for part in range(5):
        rs.finish(part, 2)
        rs.start(part, 3)
    mlp.stage(4)
    mlp.halve()
    for part in range(5):
        rs.finish(part, 3)
        rs.start(part, 4)
    mlp.half.wait_recv()
    for p in range(5):
        mlp_ref[p] = mlp.result(p)
    for part in range(5):
        rs.finish(part, 4)
    own_ref[...] = acc[co["yh"], co["x"], co["z"]]
    rs.drain()
    mlp.drain()


def backward_call(kv, w, wt, bias, m, delta, gate, up, down):
    shape = jax.ShapeDtypeStruct
    return pl.pallas_call(
        backward_kernel,
        out_shape=(
            shape((5, 128, ROWS3), F32),
            shape((5, 128, 128), BF16),
            shape((5, 3, 32, 128), BF16),
        ),
        in_specs=[INV] * 6 + [ANY] * 3,
        out_specs=[INV] * 3,
        scratch_shapes=[pltpu.VMEM((2, 4, 4, 5, 128, 128), BF16)]
        + [pltpu.VMEM(s, BF16) for s in rs_shapes("y2", (128, 128))]
        + [dma_sems(64), dma_sems(64)]
        + grad_scratch(MLP),
        compiler_params=params(3),
        name="attention_backward",
    )(kv, w, wt, bias, m, delta, gate, up, down)


LAST = (GAIN,)


def last_kernel(slab_ref, mlp_ref, out_ref, mlp_out, *rest):
    msend, mrecv, send, recv = rest[:4]
    co = coords()
    greet(co, GRAD_DIMS)
    here = (co["yh"], co["x"], co["z"])
    grad = GradSum(LAST, (slab_ref,), rest[4:], co)
    grad.begin()
    mlp_out[here] = mlp_ref[...]
    mlp = AllGather(mlp_out, Sems(msend, mrecv), co)
    for part in range(5):
        mlp.start(part, 0)

    def mlp_stage(stage):
        for part in range(5):
            mlp.finish(part, stage)
            if stage < 4:
                mlp.start(part, stage + 1)

    grad.fold()
    mlp_stage(0)
    for stage in range(5):
        grad.stage(stage)
        if stage < 4:
            mlp_stage(stage + 1)
    grad.halve()
    grad.half.wait_recv()
    for p in range(5):
        out_ref[here + (p,)] = grad.result(p)
    ag = AllGather(out_ref, Sems(send, recv), co)
    for part in range(5):
        ag.start(part, 0)
    for stage in range(5):
        for part in range(5):
            ag.finish(part, stage)
            if stage < 4:
                ag.start(part, stage + 1)
    grad.drain()
    mlp.drain()
    ag.drain()


def last_call(slab, mlp):
    shape = jax.ShapeDtypeStruct
    return pl.pallas_call(
        last_kernel,
        out_shape=(
            shape((2, 4, 4, 5, 1, 32, 128), BF16),
            shape((2, 4, 4, 5, 3, 32, 128), BF16),
        ),
        in_specs=[ANY, INV],
        out_specs=[INV, INV],
        scratch_shapes=[dma_sems(48)] * 4 + grad_scratch(LAST),
        compiler_params=params(4),
        name="last_gradients",
    )(slab, mlp)


def unpack_kernel(kinds, first, second, *outs):
    for i, kind in enumerate(kinds):
        src, j = (first, i) if i < len(LAST) else (second, i - len(LAST))

        def part(p, carry):
            for x in range(4):
                for z in range(4):
                    for yh in range(2):
                        block = src[yh, x, z, p, j].astype(F32)
                        if kind != TALL:
                            rows = min(32, kind - 64 * x - 32 * yh)
                            lanes = pl.ds(pl.multiple_of(512 * p + 128 * z, 128), 128)
                            outs[i][pl.ds(64 * x + 32 * yh, rows), lanes] = block[:rows]
                        else:
                            at = 256 * z + 128 * yh
                            count = min(128, 960 - at)
                            rows = pl.ds(pl.multiple_of(128 * p + 32 * x, 8), 32)
                            outs[i][rows, pl.ds(at, count)] = block[:, :count]
            return carry

        lax.fori_loop(0, 5, part, 0)


def unpack_call(first, second):
    kinds = LAST + MLP
    return pl.pallas_call(
        functools.partial(unpack_kernel, kinds),
        out_shape=tuple(jax.ShapeDtypeStruct(slab_shape(kind), F32) for kind in kinds),
        in_specs=[INV, INV],
        out_specs=[INV] * len(kinds),
        compiler_params=pltpu.CompilerParams(vmem_limit_bytes=VMEM_LIMIT),
        name="unpack",
    )(first, second)


def rotation(position_list):
    half_size = HEAD_SIZE // 2
    frequency = 100000.0 ** (-(jnp.arange(half_size, dtype=F32) * 2.0 / HEAD_SIZE))
    angles = position_list.astype(F32)[:, None] * frequency[None, :]
    return jnp.cos(angles)[:, None, :], jnp.sin(angles)[:, None, :]


def apply_rotary(values, turn, head_count, backward):
    half_size = HEAD_SIZE // 2
    cosine, sine = turn
    if backward:
        sine = -sine
    shaped = values.reshape(values.shape[0], head_count, HEAD_SIZE)
    first = shaped[..., :half_size]
    second = shaped[..., half_size:]
    turned = jnp.concatenate(
        [first * cosine - second * sine, second * cosine + first * sine], axis=-1
    )
    return turned.reshape(values.shape[0], head_count * HEAD_SIZE)


def rms_inverse(rows_in):
    return lax.rsqrt(jnp.mean(rows_in * rows_in, axis=-1) + 1e-05)


def norm_back(grad_normed, inputs, inverse, gain_row):
    gain_grad = jnp.sum(grad_normed * inputs * inverse[:, None], axis=0)
    scaled = grad_normed * gain_row
    input_grad = inverse[:, None] * scaled - inputs * (inverse**3)[:, None] * jnp.mean(
        scaled * inputs, axis=-1, keepdims=True
    )
    return (input_grad, gain_grad)


def matrix_product(left, right):
    return jnp.dot(left, right, preferred_element_type=F32)


def by_group(rows):
    t = rows.shape[0]
    return (
        rows.reshape(t, KEY_VALUE_HEADS, QUERY_PER_KV, HEAD_SIZE)
        .transpose(1, 2, 0, 3)
        .reshape(KEY_VALUE_HEADS, ROWS3, HEAD_SIZE)
    )


def shards(
    tokens, positions, w_query, key_weight, value_weight, w_output, gain_attn,
    w_gate, w_up, w_down, gain_mlp, cotangent,
):
    t = tokens.shape[1]
    owned_positions = positions[0]
    w_one = jnp.concatenate([w_query, key_weight, value_weight], axis=1)
    gains = jnp.pad(jnp.stack([gain_attn, gain_mlp]), ((0, 14), (0, 16)))
    w_qkv, gains_all, pos_all = first_call(
        w_one, gains, jnp.broadcast_to(owned_positions[None], (8, 128))
    )
    gains_all = gains_all.reshape(4, 16, 256)[:, :2, :240].astype(F32)
    gain_one = gains_all[:, 0].reshape(960)
    gain_two = gains_all[:, 1].reshape(960)
    full_places = pos_all[:, 0, :].reshape(4096)
    bias = jnp.where(
        owned_positions[None, :] >= full_places[:, None], 0.0, -1e30
    ).astype(F32)

    inputs = tokens[0].astype(F32)
    inverse_one = rms_inverse(inputs)
    normed_one = (inputs * inverse_one[:, None] * gain_one).astype(BF16)
    qkv = matrix_product(normed_one, w_qkv)
    turn = rotation(owned_positions)
    queries = apply_rotary(qkv[:, :960], turn, HQ, False).astype(BF16)
    keys = apply_rotary(qkv[:, 960:1280], turn, KEY_VALUE_HEADS, False).astype(BF16)
    values = qkv[:, 1280:].astype(BF16)
    kv_own = jnp.concatenate(
        [keys.reshape(t, 5, 64), values.reshape(t, 5, 64)], axis=-1
    ).transpose(1, 0, 2)
    q_rows = by_group(queries * BF16(0.125))
    q_turned = q_rows.transpose(0, 2, 1)
    qt = jnp.concatenate([q_turned, jnp.zeros_like(q_turned)], axis=1)

    kv_all, u_all, top, total, wo_all, wg_all, wu_all, wd_all = forward_call(
        kv_own, qt, bias, w_output, w_gate, w_up, w_down
    )
    attended = u_all[:, 64:] / total
    attended_rows = (
        attended.reshape(5, 64, 3, t).transpose(3, 0, 2, 1).reshape(t, 960).astype(BF16)
    )
    middle = inputs + matrix_product(attended_rows, wo_all)
    inverse_two = rms_inverse(middle)
    normed_two = (middle * inverse_two[:, None] * gain_two).astype(BF16)
    gate = matrix_product(normed_two, wg_all)
    upper = matrix_product(normed_two, wu_all)
    sigma = jax.nn.sigmoid(gate)
    hidden = (gate * sigma * upper).astype(BF16)
    result = (middle + matrix_product(hidden, wd_all)).astype(BF16)[None]

    grad_low = cotangent[0]
    grad_out = grad_low.astype(F32)
    term_down = matrix_product(hidden.T, grad_low).astype(BF16)
    grad_hidden = matrix_product(grad_low, wd_all.T)
    grad_gate_low = (grad_hidden * upper * sigma * (1.0 + gate * (1.0 - sigma))).astype(BF16)
    grad_upper_low = (grad_hidden * gate * sigma).astype(BF16)
    term_gate = matrix_product(normed_two.T, grad_gate_low).astype(BF16)
    term_up = matrix_product(normed_two.T, grad_upper_low).astype(BF16)
    grad_normed_two = matrix_product(grad_gate_low, wg_all.T) + matrix_product(
        grad_upper_low, wu_all.T
    )
    norm_grad_two, term_gain_two = norm_back(grad_normed_two, middle, inverse_two, gain_two)
    grad_middle = grad_out + norm_grad_two
    branch_gradient = grad_middle.astype(BF16)
    term_output = matrix_product(attended_rows.T, branch_gradient).astype(BF16)
    grad_attended = (
        matrix_product(branch_gradient, wo_all.T)
        .reshape(t, 5, 3, 64)
        .transpose(1, 3, 2, 0)
        .reshape(5, 64, ROWS3)
    )
    du_turned = (grad_attended / total).astype(BF16)
    delta = jnp.sum(grad_attended * attended, axis=1, keepdims=True) / total
    w_back = jnp.concatenate(
        [
            jnp.concatenate([q_turned, jnp.zeros_like(q_turned)], axis=2),
            jnp.concatenate([jnp.zeros_like(du_turned), du_turned], axis=2),
        ],
        axis=1,
    )
    dq_turned, own_pairs, mlp_own = backward_call(
        kv_all, w_back, w_back.transpose(0, 2, 1), bias, top, delta,
        term_gate, term_up, term_down,
    )
    query_rows = (
        (dq_turned[:, :64] * 0.125)
        .reshape(5, 64, 3, t)
        .transpose(3, 0, 2, 1)
        .reshape(t, 960)
    )
    pairs = own_pairs.transpose(1, 0, 2)
    grad_query_low = apply_rotary(query_rows, turn, HQ, True).astype(BF16)
    grad_key_low = apply_rotary(
        pairs[..., :64].reshape(t, 320).astype(F32), turn, KEY_VALUE_HEADS, True
    ).astype(BF16)
    grad_value_low = pairs[..., 64:].reshape(t, 320)
    grad_qkv = jnp.concatenate([grad_query_low, grad_key_low, grad_value_low], axis=1)
    term_qkv = matrix_product(normed_one.T, grad_qkv).astype(BF16)
    grad_normed_one = matrix_product(grad_qkv, w_qkv.T)
    norm_grad_one, term_gain_one = norm_back(grad_normed_one, inputs, inverse_one, gain_one)
    grad_input = (grad_middle + norm_grad_one).astype(BF16)[None]

    term_gains = jnp.stack([term_gain_one, term_gain_two]).astype(BF16)
    gain_rows = jnp.pad(
        term_gains.reshape(2, 4, 240).transpose(1, 0, 2), ((0, 0), (0, 14), (0, 2320))
    )
    slab = jnp.concatenate(
        [jnp.concatenate([term_qkv, term_output], axis=1).reshape(4, 240, 2560), gain_rows],
        axis=1,
    ).reshape(1024, 2560)
    first, sum_gate, sum_up, sum_down = unpack_call(*last_call(slab, mlp_own))
    return (
        result, grad_input,
        first[:240, :960], first[:240, 960:1280], first[:240, 1280:1600], first[:240, 1600:],
        first[240, :240], sum_gate, sum_up, sum_down, first[241, :240],
    )


def solution(mesh):
    in_specs = (
        P("dp", "ctx", None), P("dp", "ctx"),
        P("dp", None), P("dp", None), P("dp", None), P("dp", None), P("dp"),
        P("dp", None), P("dp", None), P("dp", None), P("dp"),
        P("dp", "ctx", None),
    )
    out_specs = (
        P("dp", "ctx", None), P("dp", "ctx", None),
        P("dp", None), P("dp", None), P("dp", None), P("dp", None), P("dp"),
        P("dp", None), P("dp", None), P("dp", None), P("dp"),
    )
    return jax.shard_map(shards, mesh=mesh, in_specs=in_specs, out_specs=out_specs, check_vma=False)
```

```python
import jax
import jax.numpy as jnp
from jax import lax
from jax.experimental import pallas as pl
from jax.experimental.pallas import tpu as pltpu
from jax.sharding import PartitionSpec as P

HQ = 15
KEY_VALUE_HEADS = 5
HEAD_SIZE = 64
QUERY_PER_KV = 3
MESH = pl.DeviceIdType.MESH
VMEM_LIMIT = 60 * 2**20
F32 = jnp.float32
BF16 = jnp.bfloat16
ROWS3 = 384


def coords():
    dp = lax.axis_index("dp")
    ctx = lax.axis_index("ctx")
    return dict(yl=dp // 2, c=dp % 2, yh=ctx // 16, x=(ctx // 4) % 4, z=ctx % 4)


def flip(t):
    return t + 1 - 2 * (t % 2)


def partner(co, d):
    new = dict(co)
    if d == "core":
        new["c"] = 1 - co["c"]
    elif d == "x1":
        new["x"] = flip(co["x"])
    elif d == "x3":
        new["x"] = 3 - co["x"]
    elif d == "z1":
        new["z"] = flip(co["z"])
    elif d == "z3":
        new["z"] = 3 - co["z"]
    else:
        if d in ("y1", "y3"):
            new["yl"] = 1 - co["yl"]
        if d in ("y2", "y3"):
            new["yh"] = 1 - co["yh"]
    return new


def device(co):
    return (co["yl"] * 2 + co["c"], co["yh"] * 16 + co["x"] * 4 + co["z"])


def spans(state, t):
    if state == "all":
        return [(0, 4)]
    if state == "both":
        return [(0, 2)]
    if state == "pair":
        return [(t - t % 2, 2)]
    if state == "anti":
        return [(t, 1), (3 - t, 1)]
    return [(t, 1)]


WIDTH = {"all": 4, "both": 2, "pair": 2, "anti": 2, "one": 1}


def less(state, d):
    new = dict(state)
    axis = d[0]
    if axis == "y":
        new["y"] = "one"
    elif state[axis] == "all":
        new[axis] = "anti" if d[1] == "1" else "pair"
    else:
        new[axis] = "one"
    return new


def more(state, d):
    new = dict(state)
    axis = d[0]
    if axis == "y":
        new["y"] = "both"
    elif state[axis] == "one":
        new[axis] = "pair" if d[1] == "1" else "anti"
    else:
        new[axis] = "all"
    return new


def boxes(state, co, ykey):
    out = []
    place_y = 0
    for ys, yn in spans(state["y"], co[ykey]):
        place_x = 0
        for xs, xn in spans(state["x"], co["x"]):
            place_z = 0
            for zs, zn in spans(state["z"], co["z"]):
                out.append(
                    (
                        (pl.ds(ys, yn), pl.ds(xs, xn), pl.ds(zs, zn)),
                        (pl.ds(place_y, yn), pl.ds(place_x, xn), pl.ds(place_z, zn)),
                        (yn, xn, zn),
                    )
                )
                place_z += zn
            place_x += xn
        place_y += yn
    return out


FULL = dict(y="both", x="all", z="all")
SINGLE = dict(y="one", x="one", z="one")


def order(ydim, part):
    dims = ["x1", "x3", "z1", "z3", ydim]
    return dims[part:] + dims[:part]


def rs_states(ydim, part):
    states = []
    state = FULL
    for d in order(ydim, part):
        state = less(state, d)
        states.append(state)
    return states


def rs_shapes(ydim, block):
    return [
        (WIDTH[s["y"]], WIDTH[s["x"]], WIDTH[s["z"]]) + block
        for part in range(5)
        for s in rs_states(ydim, part)
    ]


class Sems:
    def __init__(self, send, recv):
        self.send, self.recv, self.count = send, recv, 0

    def take(self):
        i = self.count
        self.count += 1
        return self.send.at[i], self.recv.at[i]

    def copy(self, src, dst, co):
        s, r = self.take()
        cp = pltpu.make_async_remote_copy(
            src_ref=src, dst_ref=dst, send_sem=s, recv_sem=r,
            device_id=device(co), device_id_type=MESH,
        )
        cp.start()
        return cp


def greet(co, dims):
    barrier = pltpu.get_barrier_semaphore()
    for d in dims:
        pl.semaphore_signal(
            barrier, inc=1, device_id=device(partner(co, d)), device_id_type=MESH
        )
    pl.semaphore_wait(barrier, len(dims))


def add_boxes(pairs, acc, tail, buf, head):
    for box, place, (yn, xn, zn) in pairs:
        (by, bx, bz), (py, px, pz) = box, place

        def add(i, carry):
            iy, ix = i // xn, i % xn
            here = (by.start + iy, bx.start + ix, bz) + tail
            there = head + (py.start + iy, px.start + ix, pz)
            acc[here] = (acc[here].astype(F32) + buf[there].astype(F32)).astype(BF16)
            return carry

        if yn * xn == 1:
            add(0, 0)
        else:
            lax.fori_loop(0, yn * xn, add, 0)


class PlaneReduce:
    DIMS = ["x1", "x3", "z1", "z3"]

    @classmethod
    def plan(cls, part, y):
        dims = (cls.DIMS[part:] + cls.DIMS[:part])[::-1]
        states = []
        state = dict(y=y, x="all", z="all")
        for d in dims:
            state = less(state, d)
            states.append(state)
        return dims, states

    @classmethod
    def shapes(cls, y, lead, block):
        return [
            lead + (WIDTH[y], WIDTH[s["x"]], WIDTH[s["z"]]) + block
            for part in range(4)
            for s in cls.plan(part, y)[1]
        ]

    def __init__(self, acc, bufs, sems, co, y):
        self.acc, self.bufs, self.sems, self.co, self.y = acc, bufs, sems, co, y
        self.ykey = "yh" if y == "both" else "yl"
        self.quarter = acc.shape[-2] // 4
        self.flying, self.sent = {}, []

    def send(self, tail, lead, part, stage):
        dims, states = self.plan(part, self.y)
        to = partner(self.co, dims[stage])
        rows = pl.ds(self.quarter * part, self.quarter)
        buf = self.bufs[part * 4 + stage]
        out = []
        for box, place, _ in boxes(states[stage], to, self.ykey):
            src = self.acc.at[box + tail + (rows,)]
            out.append(self.sems.copy(src, buf.at[lead + place], to))
        self.flying[lead, part] = out
        self.sent += out

    def step(self, tail, lead, stage):
        for part in range(4):
            if stage > 0:
                for cp in self.flying[lead, part]:
                    cp.wait_recv()
                rows = pl.ds(self.quarter * part, self.quarter)
                add_boxes(
                    boxes(self.plan(part, self.y)[1][stage - 1], self.co, self.ykey),
                    self.acc, tail + (rows,), self.bufs[part * 4 + stage - 1], lead,
                )
            if stage < 4:
                self.send(tail, lead, part, stage)

    def drain(self):
        for cp in self.sent:
            cp.wait_send()


class PairSum:
    def __init__(self, acc, own, last, bufs, sems, co):
        self.acc, self.own, self.last, self.sems, self.co = acc, own, last, sems, co
        self.plane = PlaneReduce(acc, bufs, sems, co, "both")
        self.at, self.halves = {}, {}

    def advance(self, g):
        at = self.at[g] = self.at.get(g, -1) + 1
        co = self.co
        if at < 5:
            self.plane.step((g,), (g,), at)
        if at == 4:
            there = (1 - co["yh"], co["x"], co["z"], g)
            self.halves[g] = self.sems.copy(
                self.acc.at[there], self.last.at[g], partner(co, "y2")
            )
        elif at == 5:
            self.halves[g].wait_recv()
            here = (co["yh"], co["x"], co["z"], g)
            self.own[g] = (
                self.acc[here].astype(F32) + self.last[g].astype(F32)
            ).astype(BF16)

    def drain(self):
        self.plane.drain()
        for cp in self.halves.values():
            cp.wait_send()


class ReduceScatter:
    def __init__(self, acc, bufs, sems, co, ydim):
        self.acc, self.bufs, self.sems, self.co, self.ydim = acc, bufs, sems, co, ydim
        self.ykey = "yl" if ydim == "yl" else "yh"
        self.flying = {}
        self.sent = []

    def start(self, part, stage):
        d = order(self.ydim, part)[stage]
        state = rs_states(self.ydim, part)[stage]
        buf = self.bufs[part * 5 + stage]
        out = []
        if d == "yl":
            half = self.acc.shape[-2] // 2
            ways = [("y1", pl.ds(0, half)), ("y3", pl.ds(half, half))]
        else:
            ways = [(d, slice(None))]
        for way, rows in ways:
            to = partner(self.co, way)
            for box, place, _ in boxes(state, to, self.ykey):
                middle = (slice(None),) * (len(self.acc.shape) - 6)
                src = self.acc.at[box + (part,) + middle + (rows, slice(None))]
                dst = buf.at[place + middle + (rows, slice(None))]
                out.append(self.sems.copy(src, dst, to))
        self.flying[part, stage] = out
        self.sent += out

    def finish(self, part, stage):
        for cp in self.flying[part, stage]:
            cp.wait_recv()
        state = rs_states(self.ydim, part)[stage]
        buf = self.bufs[part * 5 + stage]
        add_boxes(
            boxes(state, self.co, self.ykey), self.acc, (part,), buf, ()
        )

    def drain(self):
        for cp in self.sent:
            cp.wait_send()


class AllGather:
    def __init__(self, buf, sems, co, ydim="y2"):
        self.buf, self.sems, self.co, self.ydim = buf, sems, co, ydim
        self.flying = {}
        self.sent = []

    def start(self, part, stage):
        dims = order(self.ydim, part)
        state = SINGLE
        for d in dims[:stage]:
            state = more(state, d)
        to = partner(self.co, dims[stage])
        out = []
        for box, _, _ in boxes(state, self.co, "yh"):
            ref = self.buf.at[box + (part,)]
            out.append(self.sems.copy(ref, ref, to))
        self.flying[part, stage] = out
        self.sent += out

    def finish(self, part, stage):
        for cp in self.flying[part, stage]:
            cp.wait_recv()

    def drain(self):
        for cp in self.sent:
            cp.wait_send()


class PlaneGather:
    DIMS = ["x1", "x3", "z1", "z3"]

    def __init__(self, buf, places, sems, co):
        self.buf, self.places, self.sems, self.co = buf, places, sems, co
        self.flying, self.sent = {}, []

    def first(self):
        co = self.co
        out = []
        for buf in (self.places, self.buf):
            ref = buf.at[co["yh"], co["x"], co["z"]]
            out.append(self.sems.copy(ref, ref, partner(co, "y2")))
        for cp in out:
            cp.wait_recv()
        self.sent += out

    def start(self, part, stage):
        dims = self.DIMS[part:] + self.DIMS[:part]
        state = dict(y="both", x="one", z="one")
        for d in dims[:stage]:
            state = more(state, d)
        to = partner(self.co, dims[stage])
        rows = pl.ds(32 * part, 32)
        for g in range(5) if stage == 3 else [None]:
            out = []
            for box, _, _ in boxes(state, self.co, "yh"):
                if part == 0 and g in (None, 0):
                    ref = self.places.at[box]
                    out.append(self.sems.copy(ref, ref, to))
                ref = self.buf.at[box + (slice(None) if g is None else g, rows)]
                out.append(self.sems.copy(ref, ref, to))
            self.flying[part, stage, g or 0] = out
            self.sent += out

    def finish(self, part, stage, g=0):
        for cp in self.flying[part, stage, g]:
            cp.wait_recv()

    def drain(self):
        for cp in self.sent:
            cp.wait_send()


class Gather:
    def __init__(self, items, sems, local, co):
        self.items, self.sems, self.local, self.co = items, sems, local, co
        self.waits = []

    def block(self, i, q, first, count):
        src, dst, h, lanes = self.items[i]
        n, width = src.shape
        if lanes:
            where = pl.ds(pl.multiple_of(q * width, 128), width)
            return dst.at[pl.ds(first, count), where]
        return dst.at[pl.ds(pl.multiple_of(q * n + first, 16), count)]

    def start(self):
        co = self.co
        me = co["yl"] * 2 + co["c"]
        self.stage = []
        for i, (src, dst, h, lanes) in enumerate(self.items):
            n = src.shape[0]
            one = self.sems.copy(
                src.at[pl.ds(0, h)], self.block(i, me, 0, h), partner(co, "y1")
            )
            two = None
            if h < n:
                two = self.sems.copy(
                    src.at[pl.ds(h, n - h)], self.block(i, me, h, n - h), partner(co, "y3")
                )
            self.stage.append((one, two))
            whole = self.block(i, me, 0, n)
            self.waits.append(self.sems.copy(src, whole, partner(co, "core")))
            cp = pltpu.make_async_copy(src, whole, self.local.at[i])
            cp.start()
            self.waits.append(cp)

    def forward(self, i):
        co = self.co
        src, dst, h, lanes = self.items[i]
        n = src.shape[0]
        q = (1 - co["yl"]) * 2 + co["c"]
        for cp, first, count in zip(self.stage[i], (0, h), (h, n - h)):
            if cp is None:
                continue
            cp.wait_recv()
            ref = self.block(i, q, first, count)
            self.waits.append(self.sems.copy(ref, ref, partner(co, "core")))

    def finish(self):
        for one, two in self.stage:
            one.wait_send()
            if two is not None:
                two.wait_send()
        for cp in self.waits:
            cp.wait()


def params(cid):
    return pltpu.CompilerParams(
        collective_id=cid, has_side_effects=True, vmem_limit_bytes=VMEM_LIMIT
    )


def dma_sems(n):
    return pltpu.SemaphoreType.DMA((n,))


ANY = pl.BlockSpec(memory_space=pl.ANY)
INV = pl.BlockSpec(memory_space=pltpu.VMEM)


def first_kernel(w_ref, gain_ref, w_out, gain_out, send, recv, local):
    co = coords()
    greet(co, ("core", "y1", "y3"))
    gather = Gather(
        [(gain_ref, gain_out, 240, False), (w_ref, w_out, 128, False)],
        Sems(send, recv), local, co,
    )
    gather.start()
    gather.forward(0)
    gather.forward(1)
    gather.finish()


def first_call(w_one, gains):
    return pl.pallas_call(
        first_kernel,
        out_shape=(
            jax.ShapeDtypeStruct((960, 1600), BF16),
            jax.ShapeDtypeStruct((960, 128), BF16),
        ),
        in_specs=[INV] * 2,
        out_specs=[ANY] * 2,
        scratch_shapes=[dma_sems(8), dma_sems(8), dma_sems(3)],
        compiler_params=params(1),
        name="gather_first",
    )(w_one, gains)


CHUNK = 512


def over_lanes(left, right):
    return lax.dot_general(
        left, right, (((1,), (1,)), ((), ())), preferred_element_type=F32
    )


def over_dim0(left, right):
    return lax.dot_general(
        left, right, (((0,), (0,)), ((), ())), preferred_element_type=F32
    )


def forward_kernel(
    kv_ref, qt_ref, pos_ref, wo_ref, wg_ref, wu_ref, wd_ref,
    kv_all, bias_ref, u_ref, m_ref, l_ref, wo_all, wg_all, wu_all, wd_all,
    scores, places, send, recv, wsend, wrecv, local,
):
    co = coords()
    greet(co, ("x1", "x3", "z1", "z3", "y2", "core", "y1", "y3"))
    weights = Gather(
        [
            (wo_ref, wo_all, 128, False),
            (wg_ref, wg_all, 128, False),
            (wu_ref, wu_all, 128, False),
            (wd_ref, wd_all, 480, True),
        ],
        Sems(wsend, wrecv), local, co,
    )
    here = (co["yh"], co["x"], co["z"])
    kv_all[here] = kv_ref[...]
    places[here] = pos_ref[...]
    ag = PlaneGather(kv_all, places, Sems(send, recv), co)
    ag.first()
    for part in range(4):
        ag.start(part, 0)
    weights.start()
    for stage in range(1, 4):
        for part in range(4):
            ag.finish(part, stage - 1)
            ag.start(part, stage)
    for part in range(4):
        ag.finish(part, 3, 0)
    steps = lax.broadcasted_iota(jnp.int32, (64, 128), 0)

    def mask(i, carry):
        row = places[i // 16, (i // 4) % 4, i % 4][0:1]
        for half in range(2):
            ahead = pos_ref[0:1] - row[:, 64 * half:64 * half + 1]
            bias_ref[pl.ds(pl.multiple_of(i * 128 + 64 * half, 64), 64)] = jnp.where(
                steps <= ahead, 0.0, -1e30
            ).astype(F32)
        return carry

    lax.fori_loop(0, 32, mask, 0)

    for g in range(KEY_VALUE_HEADS):
        qt = qt_ref[g]
        if g > 0:
            for part in range(4):
                ag.finish(part, 3, g)
        if g == 4:
            weights.forward(0)
            weights.forward(1)

        def score(i, top):
            kv = kv_all[i // 4, i % 4, :, g].reshape(CHUNK, 128)
            s = jnp.dot(kv, qt, preferred_element_type=F32)
            b = bias_ref[pl.ds(i * CHUNK, CHUNK)]
            s = s + jnp.concatenate([b, b, b], axis=1)
            scores[pl.ds(i * CHUNK, CHUNK)] = s
            return jnp.maximum(top, jnp.max(s.reshape(CHUNK // 8, 8, ROWS3), axis=0))

        top = lax.fori_loop(0, 8, score, jnp.full((8, ROWS3), -1e30, F32))
        top = jnp.max(top, axis=0, keepdims=True)

        def weigh(i, carry):
            total, u = carry
            kv = kv_all[i // 4, i % 4, :, g].reshape(CHUNK, 128)
            e = jnp.exp(scores[pl.ds(i * CHUNK, CHUNK)] - top)
            total = total + jnp.sum(e.reshape(CHUNK // 8, 8, ROWS3), axis=0)
            return total, u + over_dim0(kv, e.astype(BF16))

        carry = (jnp.zeros((8, ROWS3), F32), jnp.zeros((128, ROWS3), F32))
        total, u = lax.fori_loop(0, 8, weigh, carry)
        u_ref[g] = u
        m_ref[g] = top
        l_ref[g] = jnp.sum(total, axis=0, keepdims=True)
    weights.forward(2)
    weights.forward(3)
    ag.drain()
    weights.finish()


def forward_call(kv, qt, pos, wo, wg, wu, wd):
    shape = jax.ShapeDtypeStruct
    return pl.pallas_call(
        forward_kernel,
        out_shape=(
            shape((2, 4, 4, 5, 128, 128), BF16),
            shape((4096, 128), F32),
            shape((5, 128, ROWS3), F32),
            shape((5, 1, ROWS3), F32),
            shape((5, 1, ROWS3), F32),
            shape((960, 960), BF16),
            shape((960, 2560), BF16),
            shape((960, 2560), BF16),
            shape((960, 2560), BF16),
        ),
        in_specs=[INV] * 7,
        out_specs=[INV] * 5 + [ANY] * 4,
        scratch_shapes=[
            pltpu.VMEM((4096, ROWS3), F32),
            pltpu.VMEM((2, 4, 4, 8, 128), jnp.int32),
            dma_sems(128), dma_sems(128), dma_sems(20), dma_sems(20), dma_sems(4),
        ],
        compiler_params=params(2),
        name="attention_forward",
    )(kv, qt, pos, wo, wg, wu, wd)


WIDE, TALL, GAIN = 240, 640, 256


def slab_shape(kind):
    return (960, 640) if kind == TALL else (kind, 2560)


def term(kind, lhs, rhs, q, p):
    if kind == TALL:
        lanes = pl.ds(pl.multiple_of(640 * q + 128 * p, 128), 128)
        return jnp.dot(lhs[...], rhs[:, lanes], preferred_element_type=F32)
    rows = pl.ds(pl.multiple_of(240 * q, 16), 240)
    lanes = pl.ds(pl.multiple_of(512 * p, 128), 512)
    if kind == GAIN:
        return over_lanes(lhs[rows], rhs[lanes])
    return jnp.dot(lhs[rows], rhs[:, lanes], preferred_element_type=F32)


def part_lanes(kind, p):
    width = 128 if kind == TALL else 512
    return pl.ds(pl.multiple_of(width * p, 128), width)


GRAD_DIMS = ("x1", "x3", "z1", "z3", "y1", "y2", "y3", "core")


def grad_scratch(kinds):
    n = len(kinds)
    blocks = [(2,) + slab_shape(kind) for kind in kinds]
    return (
        [pltpu.VMEM(b, BF16) for b in blocks]
        + [pltpu.VMEM(b, BF16) for b in blocks]
        + [pltpu.VMEM((2, 4, 4, 5, n, 64, 128), BF16)]
        + [pltpu.VMEM(s, BF16) for s in rs_shapes("yl", (n, 64, 128))]
        + [pltpu.VMEM((5, n, 32, 128), BF16)]
        + [dma_sems(64), dma_sems(64), dma_sems(2 * n), dma_sems(2 * n)]
    )


def send_terms(kind, factors, gains, out, got, sems, co):
    lhs, rhs = factors
    copies = []
    for yl in range(2):
        q = yl * 2 + 1 - co["c"]

        def step(p, carry):
            value = term(kind, lhs, rhs, q, p).astype(BF16)
            out[yl, pl.ds(0, value.shape[0]), part_lanes(kind, p)] = value
            return carry

        lax.fori_loop(0, 5, step, 0)
        if kind == GAIN:
            out[yl, 240:256, :] = jnp.zeros((16, 2560), BF16)
            rows = pl.ds(pl.multiple_of(16 * q, 16), 16)
            out[yl, 240:256, 0:256] = gains[rows]
        copies.append(sems.copy(out.at[yl], got.at[yl], partner(co, "core")))
    return copies


def fold_terms(kind, factors, gains, got, copies, put, co):
    lhs, rhs = factors
    for yl in range(2):
        q = yl * 2 + co["c"]
        copies[yl].wait_recv()

        def step(p, carry):
            value = term(kind, lhs, rhs, q, p)
            count = value.shape[0]
            value = value + got[yl, pl.ds(0, count), part_lanes(kind, p)].astype(F32)
            value = value.astype(BF16)
            if count % 64:
                pad = jnp.zeros((64 - count % 64, value.shape[1]), BF16)
                value = jnp.concatenate([value, pad], axis=0)
            for x in range(4):
                for z in range(4):
                    if kind == TALL:
                        first = min(256 * x + 64 * z, 896)
                        block = value[first:first + 64]
                    else:
                        block = value[64 * x:64 * x + 64, 128 * z:128 * z + 128]
                    put(yl, x, z, p, block)
            return carry

        lax.fori_loop(0, 5, step, 0)


class GradSum:
    def __init__(self, kinds, factors, gains, scratch, co):
        n = len(kinds)
        self.kinds, self.factors, self.gains, self.co = kinds, factors, gains, co
        self.outs, self.gots = scratch[:n], scratch[n:2 * n]
        self.acc = scratch[2 * n]
        bufs = scratch[2 * n + 1:2 * n + 26]
        self.last, send, recv, csend, crecv = scratch[2 * n + 26:]
        self.sems, self.core = Sems(send, recv), Sems(csend, crecv)
        self.rs = ReduceScatter(self.acc, bufs, self.sems, co, "yl")
        self.cores = []

    def begin(self, i):
        self.cores += send_terms(
            self.kinds[i], self.factors[i], self.gains, self.outs[i], self.gots[i],
            self.core, self.co,
        )

    def fold(self, i):
        co, kind, got = self.co, self.kinds[i], self.gots[i]

        def put(yl, x, z, p, block):
            self.acc[yl, x, z, p, i] = block

        copies = self.cores[2 * i:2 * i + 2]
        fold_terms(kind, self.factors[i], self.gains, got, copies, put, co)
        if kind == GAIN:
            for yl in range(2):
                q = yl * 2 + co["c"]
                rows = pl.ds(pl.multiple_of(16 * q, 16), 16)
                for z in range(2):
                    lanes = slice(128 * z, 128 * z + 128)
                    self.acc[yl, 3, z, 0, i, 48:64, :] = (
                        self.gains[rows, lanes].astype(F32)
                        + got[yl, 240:256, lanes].astype(F32)
                    ).astype(BF16)

    def launch(self):
        for part in range(5):
            self.rs.start(part, 0)

    def stage(self, stage):
        for part in range(5):
            self.rs.finish(part, stage)
            if stage < 4:
                self.rs.start(part, stage + 1)

    def halve(self):
        co = self.co
        theirs = pl.ds(pl.multiple_of((1 - co["yh"]) * 32, 32), 32)
        self.half = self.sems.copy(
            self.acc.at[co["yl"], co["x"], co["z"], :, :, theirs, :],
            self.last,
            partner(co, "y2"),
        )

    def result(self, p):
        co = self.co
        mine = pl.ds(pl.multiple_of(co["yh"] * 32, 32), 32)
        own = self.acc[co["yl"], co["x"], co["z"], p, :, mine, :]
        return (own.astype(F32) + self.last[p].astype(F32)).astype(BF16)

    def drain(self):
        self.half.wait_send()
        self.rs.drain()
        for cp in self.cores:
            cp.wait_send()


class SlabSum:
    def __init__(self, kind, factors, out_ref, i, scratch, co, late):
        self.late = late
        self.kind, self.factors, self.out_ref, self.i, self.co = kind, factors, out_ref, i, co
        self.out, self.got, self.acc, self.ybuf, self.last = scratch[:5]
        send, recv = scratch[21:]
        self.sems = Sems(send, recv)
        y = "both" if late else "one"
        self.plane = PlaneReduce(self.acc, scratch[5:21], self.sems, co, y)
        self.at = 0

    @staticmethod
    def scratch(kind, late):
        return (
            [pltpu.VMEM((2,) + slab_shape(kind), BF16)] * 2
            + [
                pltpu.VMEM((2, 4, 4, 5, 64, 128), BF16),
                pltpu.VMEM((5, 64, 128) if late else (4, 4, 5, 64, 128), BF16),
                pltpu.VMEM((5, 32, 128), BF16),
            ]
            + [pltpu.VMEM(s, BF16) for s in PlaneReduce.shapes("both" if late else "one", (), (5, 16, 128))]
            + [dma_sems(32), dma_sems(32)]
        )

    def begin(self):
        self.cores = send_terms(
            self.kind, self.factors, None, self.out, self.got, self.sems, self.co
        )

    def fold(self):
        def put(yl, x, z, p, block):
            self.acc[yl, x, z, p] = block

        fold_terms(self.kind, self.factors, None, self.got, self.cores, put, self.co)
        if self.late:
            self.plane.step((slice(None),), (), 0)
        else:
            self.send_y()

    def send_y(self):
        co = self.co
        self.halves = []
        for way, first in (("y1", 0), ("y3", 32)):
            if self.late:
                rows = (slice(None), pl.ds(first, 32))
                src = self.acc.at[(1 - co["yl"], co["x"], co["z"]) + rows]
            else:
                rows = (slice(None),) * 3 + (pl.ds(first, 32),)
                src = self.acc.at[(1 - co["yl"],) + rows]
            self.halves.append(self.sems.copy(src, self.ybuf.at[rows], partner(co, way)))

    def add_y(self):
        co = self.co
        yl = co["yl"]
        for cp in self.halves:
            cp.wait_recv()

        def add(here, there):
            self.acc[(yl,) + here] = (
                self.acc[(yl,) + here].astype(F32) + self.ybuf[there].astype(F32)
            ).astype(BF16)

        if self.late:
            add((co["x"], co["z"]), (slice(None),))
        else:

            def step(i, carry):
                add((i // 4, i % 4), (i // 4, i % 4))
                return carry

            lax.fori_loop(0, 16, step, 0)

    def send_half(self):
        co = self.co
        theirs = pl.ds(pl.multiple_of((1 - co["yh"]) * 32, 32), 32)
        src = self.acc.at[co["yl"], co["x"], co["z"], :, theirs, :]
        self.half = self.sems.copy(src, self.last, partner(co, "y2"))

    def advance(self):
        at, co = self.at, self.co
        self.at += 1
        tail = (slice(None),)
        if self.late:
            if at < 4:
                self.plane.step(tail, (), at + 1)
            if at == 3:
                self.send_y()
            if at == 4:
                self.add_y()
                self.send_half()
        else:
            if at == 0:
                self.add_y()
            if at < 5:
                self.plane.step(tail, (), at)
            if at == 4:
                self.send_half()
        if at == 5:
            self.half.wait_recv()
            mine = pl.ds(pl.multiple_of(co["yh"] * 32, 32), 32)
            own = self.acc[co["yl"], co["x"], co["z"], :, mine, :]
            self.out_ref[:, self.i] = (own.astype(F32) + self.last[...].astype(F32)).astype(BF16)

    def drain(self):
        self.plane.drain()
        self.half.wait_send()
        for cp in self.cores + self.halves:
            cp.wait_send()


MLP = (WIDE, WIDE, TALL)
LATE = (True, False, False)


def backward_kernel(
    kv_ref, w_ref, bias_ref, m_ref, delta_ref, h_ref, dg_ref, dp_ref, dy_ref, z_ref,
    dq_ref, own_ref, mlp_ref, acc, last, *rest,
):
    bufs, (send, recv) = rest[:16], rest[16:18]
    co = coords()
    greet(co, GRAD_DIMS)
    factors = ((h_ref, dg_ref), (h_ref, dp_ref), (dy_ref, z_ref))
    slabs, at = [], 18
    for i, kind in enumerate(MLP):
        count = len(SlabSum.scratch(kind, LATE[i]))
        slabs.append(SlabSum(kind, factors[i], mlp_ref, i, rest[at:at + count], co, LATE[i]))
        at += count
    for slab in slabs:
        slab.begin()
    slabs[0].fold()
    slabs[1].fold()
    pairs = PairSum(acc, own_ref, last, bufs, Sems(send, recv), co)
    starts = (2, 3, 5)
    for g in range(KEY_VALUE_HEADS):
        w = w_ref[g]
        top, delta = m_ref[g], delta_ref[g]

        def step(i, dq):
            kv = kv_ref[i // 4, i % 4, :, g].reshape(CHUNK, 128)
            both = jnp.dot(kv, w, preferred_element_type=F32)
            b = bias_ref[pl.ds(i * CHUNK, CHUNK)]
            s = both[:, :ROWS3] + jnp.concatenate([b, b, b], axis=1)
            e = jnp.exp(s - top)
            ds = (e * (both[:, ROWS3:] - delta)).astype(BF16)
            pair = jnp.concatenate([ds, e.astype(BF16)], axis=1)
            dkv = over_lanes(pair, w)
            acc[i // 4, i % 4, :, g] = dkv.astype(BF16).reshape(4, 128, 128)
            return dq + over_dim0(kv, ds)

        dq = jnp.zeros((128, ROWS3), F32)
        for half in range(2):
            dq = lax.fori_loop(4 * half, 4 * half + 4, step, dq)
            if half == 1:
                dq_ref[g] = dq
                pairs.advance(g)
            now = 2 * g + half
            for early in range(g):
                if pairs.at[early] < (5 if now >= 8 else 3):
                    pairs.advance(early)
            if now == 0:
                slabs[2].fold()
            for slab, start in zip(slabs, starts):
                if now >= start and slab.at < 6:
                    slab.advance()
    for turn in range(5):
        for g in (4, 3, 2, 1, 0):
            if pairs.at[g] < 5:
                pairs.advance(g)
        for slab in slabs:
            if slab.at < 6:
                slab.advance()
    pairs.drain()
    for slab in slabs:
        slab.drain()


def backward_call(*args):
    shape = jax.ShapeDtypeStruct
    return pl.pallas_call(
        backward_kernel,
        out_shape=(
            shape((5, 128, ROWS3), F32),
            shape((5, 128, 128), BF16),
            shape((5, 3, 32, 128), BF16),
        ),
        in_specs=[INV] * 10,
        out_specs=[INV] * 3,
        scratch_shapes=[
            pltpu.VMEM((2, 4, 4, 5, 128, 128), BF16),
            pltpu.VMEM((5, 128, 128), BF16),
        ]
        + [pltpu.VMEM(s, BF16) for s in PlaneReduce.shapes("both", (5,), (32, 128))]
        + [dma_sems(128), dma_sems(128)]
        + [s for kind, late in zip(MLP, LATE) for s in SlabSum.scratch(kind, late)],
        compiler_params=params(3),
        name="attention_backward",
    )(*args)


LAST = (GAIN,)


def last_kernel(lhs_ref, rhs_ref, gain_ref, mlp_ref, out_ref, mlp_out, *rest):
    msend, mrecv, send, recv = rest[:4]
    co = coords()
    greet(co, GRAD_DIMS)
    here = (co["yh"], co["x"], co["z"])
    grad = GradSum(LAST, ((lhs_ref, rhs_ref),), gain_ref, rest[4:], co)
    grad.begin(0)
    mlp_out[here] = mlp_ref[...]
    mlp = AllGather(mlp_out, Sems(msend, mrecv), co)
    for part in range(5):
        mlp.start(part, 0)

    def mlp_stage(stage):
        for part in range(5):
            mlp.finish(part, stage)
            if stage < 4:
                mlp.start(part, stage + 1)

    grad.fold(0)
    grad.launch()
    mlp_stage(0)
    for stage in range(5):
        grad.stage(stage)
        if stage < 4:
            mlp_stage(stage + 1)
    grad.halve()
    grad.half.wait_recv()
    for p in range(5):
        out_ref[here + (p,)] = grad.result(p)
    ag = AllGather(out_ref, Sems(send, recv), co)
    for part in range(5):
        ag.start(part, 0)
    for stage in range(5):
        for part in range(5):
            ag.finish(part, stage)
            if stage < 4:
                ag.start(part, stage + 1)
    grad.drain()
    mlp.drain()
    ag.drain()


def last_call(*args):
    shape = jax.ShapeDtypeStruct
    return pl.pallas_call(
        last_kernel,
        out_shape=(
            shape((2, 4, 4, 5, 1, 32, 128), BF16),
            shape((2, 4, 4, 5, 3, 32, 128), BF16),
        ),
        in_specs=[INV] * 4,
        out_specs=[INV, INV],
        scratch_shapes=[dma_sems(48)] * 4 + grad_scratch(LAST),
        compiler_params=params(4),
        name="last_gradients",
    )(*args)


def unpack_kernel(first, second, q_ref, k_ref, v_ref, o_ref, gain_ref, *outs):
    for x in range(4):
        for yh in range(2):
            at = 64 * x + 32 * yh
            value = jnp.concatenate(
                [first[yh, x, z, p, 0].astype(F32) for p in range(5) for z in range(4)], axis=1
            )
            rows = min(32, 240 - at)
            for ref, lane in ((q_ref, 0), (k_ref, 960), (v_ref, 1280), (o_ref, 1600)):
                ref[at:at + rows] = value[:rows, lane:lane + ref.shape[1]]
            if rows < 32:
                gain_ref[...] = value[rows:, :256]
    for i, kind in enumerate(MLP):

        def part(p, carry):
            for x in range(4):
                for z in range(4):
                    for yh in range(2):
                        block = second[yh, x, z, p, i].astype(F32)
                        if kind != TALL:
                            rows = min(32, kind - 64 * x - 32 * yh)
                            lanes = pl.ds(pl.multiple_of(512 * p + 128 * z, 128), 128)
                            outs[i][pl.ds(64 * x + 32 * yh, rows), lanes] = block[:rows]
                        elif x * 4 + z < 15:
                            lanes = pl.ds(pl.multiple_of(128 * p, 128), 128)
                            outs[i][pl.ds(256 * x + 64 * z + 32 * yh, 32), lanes] = block
            return carry

        lax.fori_loop(0, 5, part, 0)


def unpack_call(first, second):
    shapes = [(240, 960), (240, 320), (240, 320), (240, 960), (16, 256)]
    shapes += [slab_shape(kind) for kind in MLP]
    return pl.pallas_call(
        unpack_kernel,
        out_shape=tuple(jax.ShapeDtypeStruct(s, F32) for s in shapes),
        in_specs=[INV, INV],
        out_specs=[INV] * len(shapes),
        compiler_params=pltpu.CompilerParams(vmem_limit_bytes=VMEM_LIMIT),
        name="unpack",
    )(first, second)


EPS = 1e-05


def turn(value):
    return value.astype(F32).T


def rms_rows(x):
    return lax.rsqrt(jnp.mean(x * x, axis=0, keepdims=True) + EPS)


def norm_back_rows(grad, x, inverse, gain):
    gain_grad = jnp.sum(grad * x * inverse, axis=1, keepdims=True)
    scaled = grad * gain
    mean = jnp.mean(scaled * x, axis=0, keepdims=True)
    return inverse * scaled - x * (inverse * inverse * inverse) * mean, gain_grad


def rotate(rows, cosine, sine):
    a, b = rows[:32], rows[32:]
    return jnp.concatenate([a * cosine - b * sine, b * cosine + a * sine], axis=0)


def head_rows(i):
    return slice(64 * i, 64 * i + 64)


def token_lanes(j):
    return slice(128 * j, 128 * j + 128)


def project_kernel(x_ref, w_ref, gain_ref, cos_ref, sin_ref, qt_ref, kv_ref, h_ref, inv_ref, raw):
    x = x_ref[...].astype(F32)
    inverse = rms_rows(x)
    inv_ref[...] = inverse
    normed = x * inverse * gain_ref[:, 0:1].astype(F32)
    h_ref[...] = normed.astype(BF16)
    rows = turn(normed).astype(BF16)
    for first, count in ((0, 512), (512, 512), (1024, 576)):
        lanes = slice(first, first + count)
        part = jnp.dot(rows, w_ref[:, lanes], preferred_element_type=F32)
        raw[lanes] = part.T
    cosine, sine = cos_ref[...], sin_ref[...]
    for g in range(KEY_VALUE_HEADS):
        for j in range(QUERY_PER_KV):
            q = rotate(raw[head_rows(3 * g + j)], cosine, sine).astype(BF16)
            qt_ref[g, 0:64, token_lanes(j)] = q * BF16(0.125)
        qt_ref[g, 64:128, :] = jnp.zeros((64, ROWS3), BF16)
        k = rotate(raw[head_rows(15 + g)], cosine, sine)
        pair = jnp.concatenate([k, raw[head_rows(20 + g)]], axis=0)
        kv_ref[g] = pair.T.astype(BF16)


def plain_params():
    return pltpu.CompilerParams(vmem_limit_bytes=VMEM_LIMIT)


def project_call(*args):
    shape = jax.ShapeDtypeStruct
    return pl.pallas_call(
        project_kernel,
        out_shape=(
            shape((5, 128, ROWS3), BF16),
            shape((5, 128, 128), BF16),
            shape((960, 128), BF16),
            shape((1, 128), F32),
        ),
        in_specs=[INV] * 5,
        out_specs=[INV] * 4,
        scratch_shapes=[pltpu.VMEM((1600, 128), F32)],
        compiler_params=plain_params(),
        name="project",
    )(*args)


def middle_kernel(
    x_ref, dy_ref, gain_ref, u_ref, l_ref, qt_ref, wo_hbm, wg_hbm, wu_hbm, wd_hbm,
    out_ref, h_ref, dg_ref, dp_ref, z_ref, dx_ref, a_ref, w_ref, delta_ref, ggain_ref,
    wo, wg, wu, wd, attended, sems,
):
    loads = []
    for i, (src, dst) in enumerate(((wo_hbm, wo), (wg_hbm, wg), (wu_hbm, wu), (wd_hbm, wd))):
        cp = pltpu.make_async_copy(src, dst, sems.at[i])
        cp.start()
        loads.append(cp)
    for g in range(KEY_VALUE_HEADS):
        for j in range(QUERY_PER_KV):
            lanes = token_lanes(j)
            attended[head_rows(3 * g + j)] = u_ref[g, 64:128, lanes] / l_ref[g, :, lanes]
    a_ref[...] = attended[...].astype(BF16)
    a_rows = attended[...].T.astype(BF16)
    dy_turned = dy_ref[...].astype(F32)
    dy_rows = dy_turned.T.astype(BF16)
    loads[0].wait()
    branch = jnp.dot(a_rows, wo[...], preferred_element_type=F32)
    x2 = x_ref[...].astype(F32) + branch.T
    inverse = rms_rows(x2)
    gain = gain_ref[:, 64:65].astype(F32)
    normed = x2 * inverse * gain
    h_ref[...] = normed.astype(BF16)
    h_rows = normed.T.astype(BF16)
    for cp in loads[1:]:
        cp.wait()

    def hidden(i, carry):
        lanes = pl.ds(pl.multiple_of(i * 512, 128), 512)
        gate = jnp.dot(h_rows, wg[:, lanes], preferred_element_type=F32)
        upper = jnp.dot(h_rows, wu[:, lanes], preferred_element_type=F32)
        dz = jnp.dot(dy_rows, wd[:, lanes], preferred_element_type=F32)
        sigma = jax.nn.sigmoid(gate)
        silu = gate * sigma
        z_ref[:, lanes] = (silu * upper).astype(BF16)
        dg_ref[:, lanes] = (dz * upper * sigma * (1.0 + gate * (1.0 - sigma))).astype(BF16)
        dp_ref[:, lanes] = (dz * silu).astype(BF16)
        return carry

    lax.fori_loop(0, 5, hidden, 0)

    def back(i, carry):
        out, grad = carry
        lanes = pl.ds(pl.multiple_of(i * 512, 128), 512)
        out = out + over_lanes(wd[:, lanes], z_ref[:, lanes])
        grad = grad + over_lanes(wg[:, lanes], dg_ref[:, lanes])
        grad = grad + over_lanes(wu[:, lanes], dp_ref[:, lanes])
        return out, grad

    out, grad = lax.fori_loop(0, 5, back, (x2, jnp.zeros((960, 128), F32)))
    out_ref[...] = out.astype(BF16)
    change, ggain_ref[...] = norm_back_rows(grad, x2, inverse, gain)
    dx = dy_turned + change
    dx_ref[...] = dx
    da = jnp.dot(wo[...], dx.astype(BF16), preferred_element_type=F32)
    for g in range(KEY_VALUE_HEADS):
        w_ref[g, :, 0:ROWS3] = qt_ref[g]
        w_ref[g, 0:64, ROWS3:] = jnp.zeros((64, ROWS3), BF16)
        for j in range(QUERY_PER_KV):
            lanes = token_lanes(j)
            rows = head_rows(3 * g + j)
            total = l_ref[g, :, lanes]
            w_ref[g, 64:128, ROWS3 + 128 * j:ROWS3 + 128 * j + 128] = (
                da[rows] / total
            ).astype(BF16)
            delta_ref[g, :, lanes] = (
                jnp.sum(da[rows] * attended[rows], axis=0, keepdims=True) / total
            )


def middle_call(*args):
    shape = jax.ShapeDtypeStruct
    return pl.pallas_call(
        middle_kernel,
        out_shape=(
            shape((960, 128), BF16),
            shape((960, 128), BF16),
            shape((128, 2560), BF16),
            shape((128, 2560), BF16),
            shape((128, 2560), BF16),
            shape((960, 128), F32),
            shape((960, 128), BF16),
            shape((5, 128, 2 * ROWS3), BF16),
            shape((5, 1, ROWS3), F32),
            shape((960, 1), F32),
        ),
        in_specs=[INV] * 6 + [ANY] * 4,
        out_specs=[INV] * 10,
        scratch_shapes=[
            pltpu.VMEM((960, 960), BF16),
            pltpu.VMEM((960, 2560), BF16),
            pltpu.VMEM((960, 2560), BF16),
            pltpu.VMEM((960, 2560), BF16),
            pltpu.VMEM((960, 128), F32),
            dma_sems(4),
        ],
        compiler_params=plain_params(),
        name="middle",
    )(*args)


def finish_kernel(
    dq_ref, pair_ref, cos_ref, sin_ref, w_ref, x_ref, inv_ref, gain_ref, h_ref, dx_ref, a_ref,
    out_ref, lhs_ref, rhs_ref, ggain_ref,
):
    cosine, sine = cos_ref[...], -sin_ref[...]
    rhs_ref[0:1600, 128:256] = jnp.zeros((1600, 128), BF16)
    rhs_ref[1600:2560, 0:128] = jnp.zeros((960, 128), BF16)
    dx = dx_ref[...]
    rhs_ref[1600:2560, 128:256] = dx.astype(BF16)
    lhs_ref[:, 0:128] = h_ref[...]
    lhs_ref[:, 128:256] = a_ref[...]
    for g in range(KEY_VALUE_HEADS):
        for j in range(QUERY_PER_KV):
            rows = rotate(dq_ref[g, 0:64, token_lanes(j)] * 0.125, cosine, sine)
            rhs_ref[head_rows(3 * g + j), 0:128] = rows.astype(BF16)
        pair = turn(pair_ref[g])
        rhs_ref[head_rows(15 + g), 0:128] = rotate(pair[:64], cosine, sine).astype(BF16)
        rhs_ref[head_rows(20 + g), 0:128] = pair[64:].astype(BF16)
    grad = jnp.dot(w_ref[...], rhs_ref[0:1600, 0:128], preferred_element_type=F32)
    change, ggain_ref[...] = norm_back_rows(
        grad, x_ref[...].astype(F32), inv_ref[...], gain_ref[:, 0:1].astype(F32)
    )
    out_ref[...] = (dx + change).astype(BF16)


def finish_call(*args):
    shape = jax.ShapeDtypeStruct
    return pl.pallas_call(
        finish_kernel,
        out_shape=(
            shape((960, 128), BF16),
            shape((960, 256), BF16),
            shape((2560, 256), BF16),
            shape((960, 1), F32),
        ),
        in_specs=[INV] * 11,
        out_specs=[INV] * 4,
        compiler_params=plain_params(),
        name="finish",
    )(*args)


def shards(
    tokens, positions, w_query, key_weight, value_weight, w_output, gain_attn,
    w_gate, w_up, w_down, gain_mlp, cotangent,
):
    owned_positions = positions[0]
    w_one = jnp.concatenate([w_query, key_weight, value_weight], axis=1)
    gains = jnp.concatenate(
        [
            jnp.broadcast_to(gain_attn[:, None], (240, 64)),
            jnp.broadcast_to(gain_mlp[:, None], (240, 64)),
        ],
        axis=1,
    )
    w_qkv, gains = first_call(w_one, gains)
    half_size = HEAD_SIZE // 2
    frequency = 100000.0 ** (-(jnp.arange(half_size, dtype=F32) * 2.0 / HEAD_SIZE))
    angles = frequency[:, None] * owned_positions.astype(F32)[None, :]
    cosine, sine = jnp.cos(angles), jnp.sin(angles)
    x_turned = tokens[0].T
    dy_turned = cotangent[0].T

    qt, kv_own, h_one, inverse_one = project_call(x_turned, w_qkv, gains, cosine, sine)
    kv_all, bias, u_all, top, total, wo_all, wg_all, wu_all, wd_turned = forward_call(
        kv_own, qt, jnp.broadcast_to(owned_positions[None], (8, 128)),
        w_output, w_gate, w_up, w_down.T,
    )
    out, h_two, dg, dp, z, dx, a, w_back, delta, gain_two = middle_call(
        x_turned, dy_turned, gains, u_all, total, qt, wo_all, wg_all, wu_all, wd_turned
    )
    dq, own_pairs, mlp_own = backward_call(
        kv_all, w_back, bias, top, delta, h_two, dg, dp, dy_turned, z
    )
    grad_in, lhs, rhs, gain_one = finish_call(
        dq, own_pairs, cosine, sine, w_qkv, x_turned, inverse_one, gains, h_one, dx, a
    )
    term_gains = jnp.concatenate([gain_one, gain_two], axis=1).astype(BF16)
    gain_rows = jnp.pad(
        term_gains.reshape(4, 240, 2).transpose(0, 2, 1), ((0, 0), (0, 14), (0, 16))
    ).reshape(64, 256)
    packed = last_call(lhs, rhs, gain_rows, mlp_own)
    (
        sum_query, sum_key, sum_value, sum_output, sum_gains, sum_gate, sum_up, sum_down
    ) = unpack_call(*packed)
    return (
        out.T[None], grad_in.T[None], sum_query, sum_key, sum_value, sum_output,
        sum_gains[0, :240], sum_gate, sum_up, sum_down.T, sum_gains[1, :240],
    )


def solution(mesh):
    in_specs = (
        P("dp", "ctx", None), P("dp", "ctx"),
        P("dp", None), P("dp", None), P("dp", None), P("dp", None), P("dp"),
        P("dp", None), P("dp", None), P("dp", None), P("dp"),
        P("dp", "ctx", None),
    )
    out_specs = (
        P("dp", "ctx", None), P("dp", "ctx", None),
        P("dp", None), P("dp", None), P("dp", None), P("dp", None), P("dp"),
        P("dp", None), P("dp", None), P("dp", None), P("dp"),
    )
    return jax.shard_map(shards, mesh=mesh, in_specs=in_specs, out_specs=out_specs, check_vma=False)
```

```python
import jax
import jax.numpy as jnp
from jax import lax
from jax.experimental import pallas as pl
from jax.experimental.pallas import tpu as pltpu
from jax.sharding import PartitionSpec as P

HQ = 15
KEY_VALUE_HEADS = 5
HEAD_SIZE = 64
QUERY_PER_KV = 3
MESH = pl.DeviceIdType.MESH
VMEM_LIMIT = 60 * 2**20
F32 = jnp.float32
BF16 = jnp.bfloat16
ROWS3 = 384


def coords():
    dp = lax.axis_index("dp")
    ctx = lax.axis_index("ctx")
    return dict(yl=dp // 2, c=dp % 2, yh=ctx // 16, x=(ctx // 4) % 4, z=ctx % 4)


def flip(t):
    return t + 1 - 2 * (t % 2)


def partner(co, d):
    new = dict(co)
    if d == "core":
        new["c"] = 1 - co["c"]
    elif d == "x1":
        new["x"] = flip(co["x"])
    elif d == "x3":
        new["x"] = 3 - co["x"]
    elif d == "z1":
        new["z"] = flip(co["z"])
    elif d == "z3":
        new["z"] = 3 - co["z"]
    else:
        if d in ("y1", "y3"):
            new["yl"] = 1 - co["yl"]
        if d in ("y2", "y3"):
            new["yh"] = 1 - co["yh"]
    return new


def device(co):
    return (co["yl"] * 2 + co["c"], co["yh"] * 16 + co["x"] * 4 + co["z"])


def spans(state, t):
    if state == "all":
        return [(0, 4)]
    if state == "both":
        return [(0, 2)]
    if state == "pair":
        return [(t - t % 2, 2)]
    if state == "anti":
        return [(t, 1), (3 - t, 1)]
    return [(t, 1)]


WIDTH = {"all": 4, "both": 2, "pair": 2, "anti": 2, "one": 1}


def less(state, d):
    new = dict(state)
    axis = d[0]
    if axis == "y":
        new["y"] = "one"
    elif state[axis] == "all":
        new[axis] = "anti" if d[1] == "1" else "pair"
    else:
        new[axis] = "one"
    return new


def more(state, d):
    new = dict(state)
    axis = d[0]
    if axis == "y":
        new["y"] = "both"
    elif state[axis] == "one":
        new[axis] = "pair" if d[1] == "1" else "anti"
    else:
        new[axis] = "all"
    return new


def boxes(state, co, ykey):
    out = []
    place_y = 0
    for ys, yn in spans(state["y"], co[ykey]):
        place_x = 0
        for xs, xn in spans(state["x"], co["x"]):
            place_z = 0
            for zs, zn in spans(state["z"], co["z"]):
                out.append(
                    (
                        (pl.ds(ys, yn), pl.ds(xs, xn), pl.ds(zs, zn)),
                        (pl.ds(place_y, yn), pl.ds(place_x, xn), pl.ds(place_z, zn)),
                        (yn, xn, zn),
                    )
                )
                place_z += zn
            place_x += xn
        place_y += yn
    return out


FULL = dict(y="both", x="all", z="all")
SINGLE = dict(y="one", x="one", z="one")


def order(ydim, part):
    dims = ["x1", "x3", "z1", "z3", ydim]
    return dims[part:] + dims[:part]


def rs_states(ydim, part):
    states = []
    state = FULL
    for d in order(ydim, part):
        state = less(state, d)
        states.append(state)
    return states


def rs_shapes(ydim, block):
    return [
        (WIDTH[s["y"]], WIDTH[s["x"]], WIDTH[s["z"]]) + block
        for part in range(5)
        for s in rs_states(ydim, part)
    ]


class Sems:
    def __init__(self, send, recv):
        self.send, self.recv, self.count = send, recv, 0

    def take(self):
        i = self.count
        self.count += 1
        return self.send.at[i], self.recv.at[i]

    def copy(self, src, dst, co):
        s, r = self.take()
        cp = pltpu.make_async_remote_copy(
            src_ref=src, dst_ref=dst, send_sem=s, recv_sem=r,
            device_id=device(co), device_id_type=MESH,
        )
        cp.start()
        return cp


def greet(co, dims):
    barrier = pltpu.get_barrier_semaphore()
    for d in dims:
        pl.semaphore_signal(
            barrier, inc=1, device_id=device(partner(co, d)), device_id_type=MESH
        )
    pl.semaphore_wait(barrier, len(dims))


def add_boxes(pairs, acc, tail, buf, head):
    for box, place, (yn, xn, zn) in pairs:
        (by, bx, bz), (py, px, pz) = box, place

        def add(i, carry):
            iy, ix = i // xn, i % xn
            here = (by.start + iy, bx.start + ix, bz) + tail
            there = head + (py.start + iy, px.start + ix, pz)
            acc[here] = acc[here] + buf[there]
            return carry

        if yn * xn == 1:
            add(0, 0)
        else:
            lax.fori_loop(0, yn * xn, add, 0)


class PlaneReduce:
    DIMS = ["x1", "x3", "z1", "z3"]

    @classmethod
    def plan(cls, part, y):
        dims = (cls.DIMS[part:] + cls.DIMS[:part])[::-1]
        states = []
        state = dict(y=y, x="all", z="all")
        for d in dims:
            state = less(state, d)
            states.append(state)
        return dims, states

    @classmethod
    def shapes(cls, y, lead, block):
        return [
            lead + (WIDTH[y], WIDTH[s["x"]], WIDTH[s["z"]]) + block
            for part in range(4)
            for s in cls.plan(part, y)[1]
        ]

    def __init__(self, acc, bufs, sems, co, y):
        self.acc, self.bufs, self.sems, self.co, self.y = acc, bufs, sems, co, y
        self.ykey = "yh" if y == "both" else "yl"
        self.quarter = acc.shape[-2] // 4
        self.flying, self.sent = {}, []

    def send(self, tail, lead, part, stage):
        dims, states = self.plan(part, self.y)
        to = partner(self.co, dims[stage])
        rows = pl.ds(self.quarter * part, self.quarter)
        buf = self.bufs[part * 4 + stage]
        out = []
        for box, place, _ in boxes(states[stage], to, self.ykey):
            src = self.acc.at[box + tail + (rows,)]
            out.append(self.sems.copy(src, buf.at[lead + place], to))
        self.flying[lead, part] = out
        self.sent += out

    def step(self, tail, lead, stage):
        for part in range(4):
            if stage > 0:
                for cp in self.flying[lead, part]:
                    cp.wait_recv()
                rows = pl.ds(self.quarter * part, self.quarter)
                add_boxes(
                    boxes(self.plan(part, self.y)[1][stage - 1], self.co, self.ykey),
                    self.acc, tail + (rows,), self.bufs[part * 4 + stage - 1], lead,
                )
            if stage < 4:
                self.send(tail, lead, part, stage)

    def drain(self):
        for cp in self.sent:
            cp.wait_send()


class PairSum:
    def __init__(self, acc, own, last, bufs, sems, co):
        self.acc, self.own, self.last, self.sems, self.co = acc, own, last, sems, co
        self.plane = PlaneReduce(acc, bufs, sems, co, "both")
        self.at, self.halves = {}, {}

    def advance(self, g):
        at = self.at[g] = self.at.get(g, -1) + 1
        co = self.co
        if at < 5:
            self.plane.step((g,), (g,), at)
        if at == 4:
            there = (1 - co["yh"], co["x"], co["z"], g)
            self.halves[g] = self.sems.copy(
                self.acc.at[there], self.last.at[g], partner(co, "y2")
            )
        elif at == 5:
            self.halves[g].wait_recv()
            here = (co["yh"], co["x"], co["z"], g)
            self.own[g] = (
                self.acc[here].astype(F32) + self.last[g].astype(F32)
            ).astype(BF16)

    def drain(self):
        self.plane.drain()
        for cp in self.halves.values():
            cp.wait_send()


class ReduceScatter:
    def __init__(self, acc, bufs, sems, co, ydim):
        self.acc, self.bufs, self.sems, self.co, self.ydim = acc, bufs, sems, co, ydim
        self.ykey = "yl" if ydim == "yl" else "yh"
        self.flying = {}
        self.sent = []

    def start(self, part, stage):
        d = order(self.ydim, part)[stage]
        state = rs_states(self.ydim, part)[stage]
        buf = self.bufs[part * 5 + stage]
        out = []
        if d == "yl":
            half = self.acc.shape[-2] // 2
            ways = [("y1", pl.ds(0, half)), ("y3", pl.ds(half, half))]
        else:
            ways = [(d, slice(None))]
        for way, rows in ways:
            to = partner(self.co, way)
            for box, place, _ in boxes(state, to, self.ykey):
                middle = (slice(None),) * (len(self.acc.shape) - 6)
                src = self.acc.at[box + (part,) + middle + (rows, slice(None))]
                dst = buf.at[place + middle + (rows, slice(None))]
                out.append(self.sems.copy(src, dst, to))
        self.flying[part, stage] = out
        self.sent += out

    def finish(self, part, stage):
        for cp in self.flying[part, stage]:
            cp.wait_recv()
        state = rs_states(self.ydim, part)[stage]
        buf = self.bufs[part * 5 + stage]
        add_boxes(
            boxes(state, self.co, self.ykey), self.acc, (part,), buf, ()
        )

    def drain(self):
        for cp in self.sent:
            cp.wait_send()


class AllGather:
    def __init__(self, buf, sems, co, ydim="y2"):
        self.buf, self.sems, self.co, self.ydim = buf, sems, co, ydim
        self.flying = {}
        self.sent = []

    def start(self, part, stage, pick=slice(None)):
        dims = order(self.ydim, part)
        state = SINGLE
        for d in dims[:stage]:
            state = more(state, d)
        to = partner(self.co, dims[stage])
        out = []
        for box, _, _ in boxes(state, self.co, "yh"):
            ref = self.buf.at[box + (part, pick)]
            out.append(self.sems.copy(ref, ref, to))
        self.flying.setdefault((part, stage), []).extend(out)
        self.sent += out

    def finish(self, part, stage):
        for cp in self.flying[part, stage]:
            cp.wait_recv()

    def drain(self):
        for cp in self.sent:
            cp.wait_send()


class PlaneGather:
    DIMS = ["x1", "x3", "z1", "z3"]

    def __init__(self, buf, places, sems, co):
        self.buf, self.places, self.sems, self.co = buf, places, sems, co
        self.flying, self.sent = {}, []

    def first(self):
        co = self.co
        out = []
        for buf in (self.places, self.buf):
            ref = buf.at[co["yh"], co["x"], co["z"]]
            out.append(self.sems.copy(ref, ref, partner(co, "y2")))
        for cp in out:
            cp.wait_recv()
        self.sent += out

    def start(self, part, stage):
        dims = self.DIMS[part:] + self.DIMS[:part]
        state = dict(y="both", x="one", z="one")
        for d in dims[:stage]:
            state = more(state, d)
        to = partner(self.co, dims[stage])
        rows = pl.ds(32 * part, 32)
        for g in range(5) if stage == 3 else [None]:
            out = []
            for box, _, _ in boxes(state, self.co, "yh"):
                if part == 0 and g in (None, 0):
                    ref = self.places.at[box]
                    out.append(self.sems.copy(ref, ref, to))
                ref = self.buf.at[box + (slice(None) if g is None else g, rows)]
                out.append(self.sems.copy(ref, ref, to))
            self.flying[part, stage, g or 0] = out
            self.sent += out

    def finish(self, part, stage, g=0):
        for cp in self.flying[part, stage, g]:
            cp.wait_recv()

    def drain(self):
        for cp in self.sent:
            cp.wait_send()


class Gather:
    def __init__(self, items, sems, local, co):
        self.items, self.sems, self.local, self.co = items, sems, local, co
        self.waits = []

    def block(self, i, q, first, count):
        src, dst, h, lanes = self.items[i]
        n, width = src.shape
        if lanes:
            where = pl.ds(pl.multiple_of(q * width, 128), width)
            return dst.at[pl.ds(first, count), where]
        return dst.at[pl.ds(pl.multiple_of(q * n + first, 16), count)]

    def start(self):
        co = self.co
        me = co["yl"] * 2 + co["c"]
        self.stage = []
        for i, (src, dst, h, lanes) in enumerate(self.items):
            n = src.shape[0]
            one = self.sems.copy(
                src.at[pl.ds(0, h)], self.block(i, me, 0, h), partner(co, "y1")
            )
            two = None
            if h < n:
                two = self.sems.copy(
                    src.at[pl.ds(h, n - h)], self.block(i, me, h, n - h), partner(co, "y3")
                )
            self.stage.append((one, two))

    def share_own(self):
        co = self.co
        me = co["yl"] * 2 + co["c"]
        for i, (src, dst, h, lanes) in enumerate(self.items):
            whole = self.block(i, me, 0, src.shape[0])
            self.waits.append(self.sems.copy(src, whole, partner(co, "core")))
            cp = pltpu.make_async_copy(src, whole, self.local.at[i])
            cp.start()
            self.waits.append(cp)

    def forward(self, i):
        co = self.co
        src, dst, h, lanes = self.items[i]
        n = src.shape[0]
        q = (1 - co["yl"]) * 2 + co["c"]
        for cp, first, count in zip(self.stage[i], (0, h), (h, n - h)):
            if cp is None:
                continue
            cp.wait_recv()
            ref = self.block(i, q, first, count)
            self.waits.append(self.sems.copy(ref, ref, partner(co, "core")))

    def finish(self):
        for one, two in self.stage:
            one.wait_send()
            if two is not None:
                two.wait_send()
        for cp in self.waits:
            cp.wait()


class Spread:
    CUTS = ((0, 128), (128, 112))

    def __init__(self, src, dst, lanes, axis, sems, local, co):
        self.src, self.dst, self.lanes, self.axis = src, dst, lanes, axis
        self.sems, self.local, self.co = sems, local, co
        self.waits = []

    def piece(self, q, t, first, count):
        rows = (t if self.lanes else q) * 240 + first
        lanes = (q if self.lanes else t) * 640
        return self.dst.at[
            pl.ds(pl.multiple_of(rows, 16), count), pl.ds(pl.multiple_of(lanes, 128), 640)
        ]

    def own(self, t, first, count):
        if self.lanes:
            return self.src.at[pl.ds(pl.multiple_of(240 * t + first, 16), count)]
        return self.src.at[pl.ds(first, count), pl.ds(pl.multiple_of(640 * t, 128), 640)]

    def block(self, q):
        if self.lanes:
            return self.dst.at[:, pl.ds(pl.multiple_of(640 * q, 128), 640)]
        return self.dst.at[pl.ds(pl.multiple_of(240 * q, 16), 240)]

    def start(self):
        co = self.co
        me, t = co["yl"] * 2 + co["c"], co[self.axis]
        self.flying = [
            self.sems.copy(self.own(t, *cut), self.piece(me, t, *cut), partner(co, way))
            for way, cut in zip(("y1", "y3"), self.CUTS)
        ]
        self.sent = list(self.flying)

    def share_own(self):
        co = self.co
        whole = self.block(co["yl"] * 2 + co["c"])
        self.waits.append(self.sems.copy(self.src, whole, partner(co, "core")))
        cp = pltpu.make_async_copy(self.src, whole, self.local)
        cp.start()
        self.waits.append(cp)

    def share(self, step):
        co = self.co
        t = co[self.axis]
        q = (1 - co["yl"]) * 2 + co["c"]
        for cp in self.flying:
            cp.wait_recv()
        self.flying = []
        for cut, edges, other in zip(self.CUTS, ("13", "31"), (flip(t), 3 - t)):
            to = partner(co, self.axis + edges[step])
            for at in (t, other)[:step + 1]:
                ref = self.piece(q, at, *cut)
                self.flying.append(self.sems.copy(ref, ref, to))
        self.sent += self.flying

    def forward(self):
        co = self.co
        for cp in self.flying:
            cp.wait_recv()
        ref = self.block((1 - co["yl"]) * 2 + co["c"])
        self.waits.append(self.sems.copy(ref, ref, partner(co, "core")))

    def finish(self):
        for cp in self.sent:
            cp.wait_send()
        for cp in self.waits:
            cp.wait()


def params(cid):
    return pltpu.CompilerParams(
        collective_id=cid, has_side_effects=True, vmem_limit_bytes=VMEM_LIMIT
    )


def dma_sems(n):
    return pltpu.SemaphoreType.DMA((n,))


ANY = pl.BlockSpec(memory_space=pl.ANY)
INV = pl.BlockSpec(memory_space=pltpu.VMEM)


def first_kernel(w_ref, gain_ref, w_out, gain_out, send, recv, local):
    co = coords()
    greet(co, ("core", "y1", "y3"))
    gather = Gather(
        [(gain_ref, gain_out, 240, False), (w_ref, w_out, 128, False)],
        Sems(send, recv), local, co,
    )
    gather.share_own()
    gather.start()
    gather.forward(0)
    gather.forward(1)
    gather.finish()


def first_call(w_one, gains):
    return pl.pallas_call(
        first_kernel,
        out_shape=(
            jax.ShapeDtypeStruct((960, 1600), BF16),
            jax.ShapeDtypeStruct((960, 128), BF16),
        ),
        in_specs=[INV] * 2,
        out_specs=[ANY] * 2,
        scratch_shapes=[dma_sems(8), dma_sems(8), dma_sems(3)],
        compiler_params=params(1),
        name="gather_first",
    )(w_one, gains)


CHUNK = 512


def over_lanes(left, right):
    return lax.dot_general(
        left, right, (((1,), (1,)), ((), ())), preferred_element_type=F32
    )


def over_dim0(left, right):
    return lax.dot_general(
        left, right, (((0,), (0,)), ((), ())), preferred_element_type=F32
    )


def forward_kernel(
    kv_ref, qt_ref, pos_ref, wo_ref, wg_ref, wu_ref, wd_ref,
    kv_all, bias_ref, u_ref, m_ref, l_ref, wo_all, wg_all, wu_all, wd_all,
    scores, places, send, recv, wsend, wrecv, local,
):
    co = coords()
    greet(co, ("x1", "x3", "z1", "z3", "y2", "core", "y1", "y3"))
    wsems = Sems(wsend, wrecv)
    weights = Gather(
        [
            (wo_ref, wo_all, 128, False),
            (wg_ref, wg_all, 128, False),
        ],
        wsems, local, co,
    )
    spreads = (
        Spread(wu_ref, wu_all, False, "x", wsems, local.at[2], co),
        Spread(wd_ref, wd_all, True, "z", wsems, local.at[3], co),
    )
    here = (co["yh"], co["x"], co["z"])
    kv_all[here] = kv_ref[...]
    places[here] = pos_ref[...]
    ag = PlaneGather(kv_all, places, Sems(send, recv), co)
    for item in (weights,) + spreads:
        item.share_own()
    ag.first()
    for part in range(4):
        ag.start(part, 0)
    for spread in spreads:
        spread.start()
    weights.start()
    for stage in range(1, 4):
        if stage == 3:
            for spread in spreads:
                spread.share(0)
        for part in range(4):
            ag.finish(part, stage - 1)
            ag.start(part, stage)
    for part in range(4):
        ag.finish(part, 3, 0)
    steps = lax.broadcasted_iota(jnp.int32, (64, 128), 0)

    def mask(i, carry):
        row = places[i // 16, (i // 4) % 4, i % 4][0:1]
        for half in range(2):
            ahead = pos_ref[0:1] - row[:, 64 * half:64 * half + 1]
            bias_ref[pl.ds(pl.multiple_of(i * 128 + 64 * half, 64), 64)] = jnp.where(
                steps <= ahead, 0.0, -1e30
            ).astype(F32)
        return carry

    lax.fori_loop(0, 32, mask, 0)

    for g in range(KEY_VALUE_HEADS):
        qt = qt_ref[g]
        if g > 0:
            for part in range(4):
                ag.finish(part, 3, g)
        if g == 1:
            for spread in spreads:
                spread.share(1)
        if g == 4:
            weights.forward(0)
            weights.forward(1)

        def score(i, top):
            kv = kv_all[i // 4, i % 4, :, g].reshape(CHUNK, 128)
            s = jnp.dot(kv, qt, preferred_element_type=F32)
            b = bias_ref[pl.ds(i * CHUNK, CHUNK)]
            s = s + jnp.concatenate([b, b, b], axis=1)
            scores[pl.ds(i * CHUNK, CHUNK)] = s
            return jnp.maximum(top, jnp.max(s.reshape(CHUNK // 8, 8, ROWS3), axis=0))

        top = lax.fori_loop(
            0, 8, score, jnp.full((8, ROWS3), -1e30, F32), unroll=8
        )
        top = jnp.max(top, axis=0, keepdims=True)

        def weigh(i, carry):
            total, u = carry
            kv = kv_all[i // 4, i % 4, :, g].reshape(CHUNK, 128)
            e = jnp.exp(scores[pl.ds(i * CHUNK, CHUNK)] - top)
            total = total + jnp.sum(e.reshape(CHUNK // 8, 8, ROWS3), axis=0)
            return total, u + over_dim0(kv, e.astype(BF16))

        carry = (jnp.zeros((8, ROWS3), F32), jnp.zeros((128, ROWS3), F32))
        total, u = lax.fori_loop(0, 8, weigh, carry, unroll=8)
        u_ref[g] = u
        m_ref[g] = top
        l_ref[g] = jnp.sum(total, axis=0, keepdims=True)
    for spread in spreads:
        spread.forward()
    ag.drain()
    weights.finish()
    for spread in spreads:
        spread.finish()


def forward_call(kv, qt, pos, wo, wg, wu, wd):
    shape = jax.ShapeDtypeStruct
    return pl.pallas_call(
        forward_kernel,
        out_shape=(
            shape((2, 4, 4, 5, 128, 128), BF16),
            shape((4096, 128), F32),
            shape((5, 128, ROWS3), F32),
            shape((5, 1, ROWS3), F32),
            shape((5, 1, ROWS3), F32),
            shape((960, 960), BF16),
            shape((960, 2560), BF16),
            shape((960, 2560), BF16),
            shape((960, 2560), BF16),
        ),
        in_specs=[INV] * 7,
        out_specs=[INV] * 5 + [ANY] * 4,
        scratch_shapes=[
            pltpu.VMEM((4096, ROWS3), F32),
            pltpu.VMEM((2, 4, 4, 8, 128), jnp.int32),
            dma_sems(128), dma_sems(128), dma_sems(32), dma_sems(32), dma_sems(4),
        ],
        compiler_params=params(2),
        name="attention_forward",
    )(kv, qt, pos, wo, wg, wu, wd)


WIDE, TALL, GAIN = 240, 640, 256


def slab_shape(kind):
    return (960, 640) if kind == TALL else (kind, 2560)


def term(kind, lhs, rhs, q, p):
    if kind == TALL:
        lanes = pl.ds(pl.multiple_of(640 * q + 128 * p, 128), 128)
        return jnp.dot(lhs[...], rhs[:, lanes], preferred_element_type=F32)
    rows = pl.ds(pl.multiple_of(240 * q, 16), 240)
    lanes = pl.ds(pl.multiple_of(512 * p, 128), 512)
    if kind == GAIN:
        return over_lanes(lhs[rows], rhs[lanes])
    return jnp.dot(lhs[rows], rhs[:, lanes], preferred_element_type=F32)


def part_lanes(kind, p):
    width = 128 if kind == TALL else 512
    return pl.ds(pl.multiple_of(width * p, 128), width)


GRAD_DIMS = ("x1", "x3", "z1", "z3", "y1", "y2", "y3", "core")


def grad_scratch(kinds):
    n = len(kinds)
    blocks = [(2,) + slab_shape(kind) for kind in kinds]
    return (
        [pltpu.VMEM(b, BF16) for b in blocks]
        + [pltpu.VMEM(b, BF16) for b in blocks]
        + [pltpu.VMEM((2, 4, 4, 5, n, 64, 128), BF16)]
        + [pltpu.VMEM(s, BF16) for s in rs_shapes("yl", (n, 64, 128))]
        + [pltpu.VMEM((5, n, 32, 128), BF16)]
        + [dma_sems(64), dma_sems(64), dma_sems(2 * n), dma_sems(2 * n)]
    )


def send_terms(kind, factors, gains, out, got, sems, co):
    lhs, rhs = factors
    copies = []
    for yl in range(2):
        q = yl * 2 + 1 - co["c"]

        def step(p, carry):
            value = term(kind, lhs, rhs, q, p).astype(BF16)
            out[yl, pl.ds(0, value.shape[0]), part_lanes(kind, p)] = value
            return carry

        lax.fori_loop(0, 5, step, 0, unroll=5)
        if kind == GAIN:
            out[yl, 240:256, :] = jnp.zeros((16, 2560), BF16)
            rows = pl.ds(pl.multiple_of(16 * q, 16), 16)
            out[yl, 240:256, 0:256] = gains[rows]
        copies.append(sems.copy(out.at[yl], got.at[yl], partner(co, "core")))
    return copies


def fold_terms(kind, factors, gains, got, copies, put, co):
    lhs, rhs = factors
    for yl in range(2):
        q = yl * 2 + co["c"]
        copies[yl].wait_recv()

        def step(p, carry):
            value = term(kind, lhs, rhs, q, p)
            count = value.shape[0]
            value = value + got[yl, pl.ds(0, count), part_lanes(kind, p)].astype(F32)
            value = value.astype(BF16)
            if count % 64:
                pad = jnp.zeros((64 - count % 64, value.shape[1]), BF16)
                value = jnp.concatenate([value, pad], axis=0)
            for x in range(4):
                for z in range(4):
                    if kind == TALL:
                        first = min(256 * x + 64 * z, 896)
                        block = value[first:first + 64]
                    else:
                        block = value[64 * x:64 * x + 64, 128 * z:128 * z + 128]
                    put(yl, x, z, p, block)
            return carry

        lax.fori_loop(0, 5, step, 0, unroll=5)


class GradSum:
    def __init__(self, kinds, factors, gains, scratch, co):
        n = len(kinds)
        self.kinds, self.factors, self.gains, self.co = kinds, factors, gains, co
        self.outs, self.gots = scratch[:n], scratch[n:2 * n]
        self.acc = scratch[2 * n]
        bufs = scratch[2 * n + 1:2 * n + 26]
        self.last, send, recv, csend, crecv = scratch[2 * n + 26:]
        self.sems, self.core = Sems(send, recv), Sems(csend, crecv)
        self.rs = ReduceScatter(self.acc, bufs, self.sems, co, "yl")
        self.cores = []

    def begin(self, i):
        self.cores += send_terms(
            self.kinds[i], self.factors[i], self.gains, self.outs[i], self.gots[i],
            self.core, self.co,
        )

    def fold(self, i):
        co, kind, got = self.co, self.kinds[i], self.gots[i]

        def put(yl, x, z, p, block):
            self.acc[yl, x, z, p, i] = block

        copies = self.cores[2 * i:2 * i + 2]
        fold_terms(kind, self.factors[i], self.gains, got, copies, put, co)
        if kind == GAIN:
            for yl in range(2):
                q = yl * 2 + co["c"]
                rows = pl.ds(pl.multiple_of(16 * q, 16), 16)
                for z in range(2):
                    lanes = slice(128 * z, 128 * z + 128)
                    self.acc[yl, 3, z, 0, i, 48:64, :] = (
                        self.gains[rows, lanes].astype(F32)
                        + got[yl, 240:256, lanes].astype(F32)
                    ).astype(BF16)

    def launch(self):
        for part in range(5):
            self.rs.start(part, 0)

    def stage(self, stage):
        for part in range(5):
            self.rs.finish(part, stage)
            if stage < 4:
                self.rs.start(part, stage + 1)

    def halve(self):
        co = self.co
        theirs = pl.ds(pl.multiple_of((1 - co["yh"]) * 32, 32), 32)
        self.half = self.sems.copy(
            self.acc.at[co["yl"], co["x"], co["z"], :, :, theirs, :],
            self.last,
            partner(co, "y2"),
        )

    def result(self, p):
        co = self.co
        mine = pl.ds(pl.multiple_of(co["yh"] * 32, 32), 32)
        own = self.acc[co["yl"], co["x"], co["z"], p, :, mine, :]
        return (own.astype(F32) + self.last[p].astype(F32)).astype(BF16)

    def drain(self):
        self.half.wait_send()
        self.rs.drain()
        for cp in self.cores:
            cp.wait_send()


class SlabSum:
    def __init__(self, kind, factors, out_ref, i, scratch, co, late):
        self.late = late
        self.kind, self.factors, self.out_ref, self.i, self.co = kind, factors, out_ref, i, co
        self.out, self.got, self.acc, self.ybuf, self.last = scratch[:5]
        send, recv = scratch[21:]
        self.sems = Sems(send, recv)
        y = "both" if late else "one"
        self.plane = PlaneReduce(self.acc, scratch[5:21], self.sems, co, y)
        self.at = 0

    @staticmethod
    def scratch(kind, late):
        return (
            [pltpu.VMEM((2,) + slab_shape(kind), BF16)] * 2
            + [
                pltpu.VMEM((2, 4, 4, 5, 64, 128), BF16),
                pltpu.VMEM((5, 64, 128) if late else (4, 4, 5, 64, 128), BF16),
                pltpu.VMEM((5, 32, 128), BF16),
            ]
            + [pltpu.VMEM(s, BF16) for s in PlaneReduce.shapes("both" if late else "one", (), (5, 16, 128))]
            + [dma_sems(32), dma_sems(32)]
        )

    def begin(self):
        self.cores = send_terms(
            self.kind, self.factors, None, self.out, self.got, self.sems, self.co
        )

    def fold(self):
        def put(yl, x, z, p, block):
            self.acc[yl, x, z, p] = block

        fold_terms(self.kind, self.factors, None, self.got, self.cores, put, self.co)
        if self.late:
            self.plane.step((slice(None),), (), 0)
        else:
            self.send_y()

    def send_y(self):
        co = self.co
        self.halves = []
        for way, first in (("y1", 0), ("y3", 32)):
            if self.late:
                rows = (slice(None), pl.ds(first, 32))
                src = self.acc.at[(1 - co["yl"], co["x"], co["z"]) + rows]
            else:
                rows = (slice(None),) * 3 + (pl.ds(first, 32),)
                src = self.acc.at[(1 - co["yl"],) + rows]
            self.halves.append(self.sems.copy(src, self.ybuf.at[rows], partner(co, way)))

    def add_y(self):
        co = self.co
        yl = co["yl"]
        for cp in self.halves:
            cp.wait_recv()

        def add(here, there):
            self.acc[(yl,) + here] = self.acc[(yl,) + here] + self.ybuf[there]

        if self.late:
            add((co["x"], co["z"]), (slice(None),))
        else:

            def step(i, carry):
                add((i // 4, i % 4), (i // 4, i % 4))
                return carry

            lax.fori_loop(0, 16, step, 0)

    def send_half(self):
        co = self.co
        theirs = pl.ds(pl.multiple_of((1 - co["yh"]) * 32, 32), 32)
        src = self.acc.at[co["yl"], co["x"], co["z"], :, theirs, :]
        self.half = self.sems.copy(src, self.last, partner(co, "y2"))

    def advance(self):
        at, co = self.at, self.co
        self.at += 1
        tail = (slice(None),)
        if self.late:
            if at < 4:
                self.plane.step(tail, (), at + 1)
            if at == 3:
                self.send_y()
            if at == 4:
                self.add_y()
                self.send_half()
        else:
            if at == 0:
                self.add_y()
            if at < 5:
                self.plane.step(tail, (), at)
            if at == 4:
                self.send_half()
        if at == 5:
            self.half.wait_recv()
            mine = pl.ds(pl.multiple_of(co["yh"] * 32, 32), 32)
            own = self.acc[co["yl"], co["x"], co["z"], :, mine, :]
            self.out_ref[:, self.i] = (own.astype(F32) + self.last[...].astype(F32)).astype(BF16)

    def drain(self):
        self.plane.drain()
        self.half.wait_send()
        for cp in self.cores + self.halves:
            cp.wait_send()


MLP = (WIDE, WIDE, TALL)
LATE = (True, False, False)


def backward_kernel(
    kv_ref, w_ref, bias_ref, m_ref, delta_ref, h_ref, dg_ref, dp_ref, dy_ref, z_ref,
    dq_ref, own_ref, mlp_ref, acc, last, *rest,
):
    bufs, (send, recv) = rest[:16], rest[16:18]
    co = coords()
    greet(co, GRAD_DIMS)
    factors = ((h_ref, dg_ref), (h_ref, dp_ref), (dy_ref, z_ref))
    slabs, at = [], 18
    for i, kind in enumerate(MLP):
        count = len(SlabSum.scratch(kind, LATE[i]))
        slabs.append(SlabSum(kind, factors[i], mlp_ref, i, rest[at:at + count], co, LATE[i]))
        at += count
    for slab in slabs:
        slab.begin()
    slabs[0].fold()
    slabs[1].fold()
    pairs = PairSum(acc, own_ref, last, bufs, Sems(send, recv), co)
    starts = (2, 4, 8)
    for g in range(KEY_VALUE_HEADS):
        w = w_ref[g]
        top, delta = m_ref[g], delta_ref[g]

        def step(i, dq):
            kv = kv_ref[i // 4, i % 4, :, g].reshape(CHUNK, 128)
            both = jnp.dot(kv, w, preferred_element_type=F32)
            b = bias_ref[pl.ds(i * CHUNK, CHUNK)]
            s = both[:, :ROWS3] + jnp.concatenate([b, b, b], axis=1)
            e = jnp.exp(s - top)
            ds = (e * (both[:, ROWS3:] - delta)).astype(BF16)
            pair = jnp.concatenate([ds, e.astype(BF16)], axis=1)
            dkv = over_lanes(pair, w)
            acc[i // 4, i % 4, :, g] = dkv.astype(BF16).reshape(4, 128, 128)
            return dq + over_dim0(kv, ds)

        dq = jnp.zeros((128, ROWS3), F32)
        for half in range(2):
            dq = lax.fori_loop(4 * half, 4 * half + 4, step, dq, unroll=4)
            if half == 1:
                dq_ref[g] = dq
                pairs.advance(g)
            now = 2 * g + half
            for early in range(g):
                if pairs.at[early] < (5 if now >= 8 else 3):
                    pairs.advance(early)
            if now == 0:
                slabs[2].fold()
            for slab, start in zip(slabs, starts):
                if now >= start and slab.at < 6:
                    slab.advance()
    for turn in range(5):
        for g in (4, 3, 2, 1, 0):
            if pairs.at[g] < 5:
                pairs.advance(g)
        for slab in slabs:
            if slab.at < 6:
                slab.advance()
    pairs.drain()
    for slab in slabs:
        slab.drain()


def backward_call(*args):
    shape = jax.ShapeDtypeStruct
    return pl.pallas_call(
        backward_kernel,
        out_shape=(
            shape((5, 128, ROWS3), F32),
            shape((5, 128, 128), BF16),
            shape((5, 3, 32, 128), BF16),
        ),
        in_specs=[INV] * 10,
        out_specs=[INV] * 3,
        scratch_shapes=[
            pltpu.VMEM((2, 4, 4, 5, 128, 128), BF16),
            pltpu.VMEM((5, 128, 128), BF16),
        ]
        + [pltpu.VMEM(s, BF16) for s in PlaneReduce.shapes("both", (5,), (32, 128))]
        + [dma_sems(128), dma_sems(128)]
        + [s for kind, late in zip(MLP, LATE) for s in SlabSum.scratch(kind, late)],
        compiler_params=params(3),
        name="attention_backward",
    )(*args)


LAST = (GAIN,)


def last_kernel(lhs_ref, rhs_ref, gain_ref, mlp_ref, out_ref, mlp_out, *rest):
    msend, mrecv, send, recv = rest[:4]
    co = coords()
    greet(co, GRAD_DIMS)
    here = (co["yh"], co["x"], co["z"])
    grad = GradSum(LAST, ((lhs_ref, rhs_ref),), gain_ref, rest[4:], co)
    mlp_out[here] = mlp_ref[...]
    mlp = AllGather(mlp_out, Sems(msend, mrecv), co)
    for part in range(5):
        mlp.start(part, 0)

    def mlp_stage(stage):
        for part in range(5):
            mlp.finish(part, stage)
            if stage < 3:
                mlp.start(part, stage + 1)

    def mlp_last(slab):
        for part in range(5):
            mlp.start(part, 4, slab)

    grad.begin(0)
    mlp_stage(0)
    mlp_stage(1)
    grad.fold(0)
    grad.launch()
    mlp_stage(2)
    grad.stage(0)
    grad.stage(1)
    mlp_stage(3)
    for i in range(3):
        mlp_last(i)
        grad.stage(2 + i)
    grad.halve()
    grad.half.wait_recv()
    for p in range(5):
        out_ref[here + (p,)] = grad.result(p)
    ag = AllGather(out_ref, Sems(send, recv), co)
    for part in range(5):
        ag.start(part, 0)
    for stage in range(5):
        for part in range(5):
            ag.finish(part, stage)
            if stage < 4:
                ag.start(part, stage + 1)
    mlp_stage(4)
    grad.drain()
    mlp.drain()
    ag.drain()


def last_call(*args):
    shape = jax.ShapeDtypeStruct
    return pl.pallas_call(
        last_kernel,
        out_shape=(
            shape((2, 4, 4, 5, 1, 32, 128), BF16),
            shape((2, 4, 4, 5, 3, 32, 128), BF16),
        ),
        in_specs=[INV] * 4,
        out_specs=[INV, INV],
        scratch_shapes=[dma_sems(64)] * 4 + grad_scratch(LAST),
        compiler_params=params(4),
        name="last_gradients",
    )(*args)


def unpack_kernel(first, second, q_ref, k_ref, v_ref, o_ref, gain_ref, *outs):
    for x in range(4):
        for yh in range(2):
            at = 64 * x + 32 * yh
            value = jnp.concatenate(
                [first[yh, x, z, p, 0].astype(F32) for p in range(5) for z in range(4)], axis=1
            )
            rows = min(32, 240 - at)
            for ref, lane in ((q_ref, 0), (k_ref, 960), (v_ref, 1280), (o_ref, 1600)):
                ref[at:at + rows] = value[:rows, lane:lane + ref.shape[1]]
            if rows < 32:
                gain_ref[...] = value[rows:, :256]
    for i, kind in enumerate(MLP):

        def part(p, carry):
            for x in range(4):
                for z in range(4):
                    for yh in range(2):
                        block = second[yh, x, z, p, i].astype(F32)
                        if kind != TALL:
                            rows = min(32, kind - 64 * x - 32 * yh)
                            lanes = pl.ds(pl.multiple_of(512 * p + 128 * z, 128), 128)
                            outs[i][pl.ds(64 * x + 32 * yh, rows), lanes] = block[:rows]
                        elif x * 4 + z < 15:
                            lanes = pl.ds(pl.multiple_of(128 * p, 128), 128)
                            outs[i][pl.ds(256 * x + 64 * z + 32 * yh, 32), lanes] = block
            return carry

        lax.fori_loop(0, 5, part, 0)


def unpack_call(first, second):
    shapes = [(240, 960), (240, 320), (240, 320), (240, 960), (16, 256)]
    shapes += [slab_shape(kind) for kind in MLP]
    return pl.pallas_call(
        unpack_kernel,
        out_shape=tuple(jax.ShapeDtypeStruct(s, F32) for s in shapes),
        in_specs=[INV, INV],
        out_specs=[INV] * len(shapes),
        compiler_params=pltpu.CompilerParams(vmem_limit_bytes=VMEM_LIMIT),
        name="unpack",
    )(first, second)


EPS = 1e-05


def turn(value):
    return value.astype(F32).T


def rms_rows(x):
    return lax.rsqrt(jnp.mean(x * x, axis=0, keepdims=True) + EPS)


def norm_back_rows(grad, x, inverse, gain):
    gain_grad = jnp.sum(grad * x * inverse, axis=1, keepdims=True)
    scaled = grad * gain
    mean = jnp.mean(scaled * x, axis=0, keepdims=True)
    return inverse * scaled - x * (inverse * inverse * inverse) * mean, gain_grad


def rotate(rows, cosine, sine):
    a, b = rows[:32], rows[32:]
    return jnp.concatenate([a * cosine - b * sine, b * cosine + a * sine], axis=0)


def head_rows(i):
    return slice(64 * i, 64 * i + 64)


def token_lanes(j):
    return slice(128 * j, 128 * j + 128)


def project_kernel(x_ref, w_ref, gain_ref, cos_ref, sin_ref, qt_ref, kv_ref, h_ref, inv_ref, raw):
    x = x_ref[...].astype(F32)
    inverse = rms_rows(x)
    inv_ref[...] = inverse
    normed = x * inverse * gain_ref[:, 0:1].astype(F32)
    h_ref[...] = normed.astype(BF16)
    rows = turn(normed).astype(BF16)
    for first, count in ((0, 512), (512, 512), (1024, 576)):
        lanes = slice(first, first + count)
        part = jnp.dot(rows, w_ref[:, lanes], preferred_element_type=F32)
        raw[lanes] = part.T
    cosine, sine = cos_ref[...], sin_ref[...]
    for g in range(KEY_VALUE_HEADS):
        for j in range(QUERY_PER_KV):
            q = rotate(raw[head_rows(3 * g + j)], cosine, sine).astype(BF16)
            qt_ref[g, 0:64, token_lanes(j)] = q * BF16(0.125)
        qt_ref[g, 64:128, :] = jnp.zeros((64, ROWS3), BF16)
        k = rotate(raw[head_rows(15 + g)], cosine, sine)
        pair = jnp.concatenate([k, raw[head_rows(20 + g)]], axis=0)
        kv_ref[g] = pair.T.astype(BF16)


def plain_params():
    return pltpu.CompilerParams(vmem_limit_bytes=VMEM_LIMIT)


def project_call(*args):
    shape = jax.ShapeDtypeStruct
    return pl.pallas_call(
        project_kernel,
        out_shape=(
            shape((5, 128, ROWS3), BF16),
            shape((5, 128, 128), BF16),
            shape((960, 128), BF16),
            shape((1, 128), F32),
        ),
        in_specs=[INV] * 5,
        out_specs=[INV] * 4,
        scratch_shapes=[pltpu.VMEM((1600, 128), F32)],
        compiler_params=plain_params(),
        name="project",
    )(*args)


def middle_kernel(
    x_ref, dy_ref, gain_ref, u_ref, l_ref, qt_ref, wo_hbm, wg_hbm, wu_hbm, wd_hbm,
    out_ref, h_ref, dg_ref, dp_ref, z_ref, dx_ref, a_ref, w_ref, delta_ref, ggain_ref,
    wo, wg, wu, wd, attended, sems,
):
    loads = []
    for i, (src, dst) in enumerate(((wo_hbm, wo), (wg_hbm, wg), (wu_hbm, wu), (wd_hbm, wd))):
        cp = pltpu.make_async_copy(src, dst, sems.at[i])
        cp.start()
        loads.append(cp)
    for g in range(KEY_VALUE_HEADS):
        for j in range(QUERY_PER_KV):
            lanes = token_lanes(j)
            attended[head_rows(3 * g + j)] = u_ref[g, 64:128, lanes] / l_ref[g, :, lanes]
    a_ref[...] = attended[...].astype(BF16)
    a_rows = attended[...].T.astype(BF16)
    dy_turned = dy_ref[...].astype(F32)
    dy_rows = dy_turned.T.astype(BF16)
    loads[0].wait()
    branch = jnp.dot(a_rows, wo[...], preferred_element_type=F32)
    x2 = x_ref[...].astype(F32) + branch.T
    inverse = rms_rows(x2)
    gain = gain_ref[:, 64:65].astype(F32)
    normed = x2 * inverse * gain
    h_ref[...] = normed.astype(BF16)
    h_rows = normed.T.astype(BF16)
    for cp in loads[1:]:
        cp.wait()

    def hidden(i, carry):
        lanes = pl.ds(pl.multiple_of(i * 512, 128), 512)
        gate = jnp.dot(h_rows, wg[:, lanes], preferred_element_type=F32)
        upper = jnp.dot(h_rows, wu[:, lanes], preferred_element_type=F32)
        dz = jnp.dot(dy_rows, wd[:, lanes], preferred_element_type=F32)
        sigma = jax.nn.sigmoid(gate)
        silu = gate * sigma
        z_ref[:, lanes] = (silu * upper).astype(BF16)
        dg_ref[:, lanes] = (dz * upper * sigma * (1.0 + gate * (1.0 - sigma))).astype(BF16)
        dp_ref[:, lanes] = (dz * silu).astype(BF16)
        return carry

    lax.fori_loop(0, 5, hidden, 0, unroll=5)

    def back(i, carry):
        out, grad = carry
        lanes = pl.ds(pl.multiple_of(i * 512, 128), 512)
        out = out + over_lanes(wd[:, lanes], z_ref[:, lanes])
        grad = grad + over_lanes(wg[:, lanes], dg_ref[:, lanes])
        grad = grad + over_lanes(wu[:, lanes], dp_ref[:, lanes])
        return out, grad

    out, grad = lax.fori_loop(
        0, 5, back, (x2, jnp.zeros((960, 128), F32)), unroll=5
    )
    out_ref[...] = out.astype(BF16)
    change, ggain_ref[...] = norm_back_rows(grad, x2, inverse, gain)
    dx = dy_turned + change
    dx_ref[...] = dx
    da = jnp.dot(wo[...], dx.astype(BF16), preferred_element_type=F32)
    for g in range(KEY_VALUE_HEADS):
        w_ref[g, :, 0:ROWS3] = qt_ref[g]
        w_ref[g, 0:64, ROWS3:] = jnp.zeros((64, ROWS3), BF16)
        for j in range(QUERY_PER_KV):
            lanes = token_lanes(j)
            rows = head_rows(3 * g + j)
            total = l_ref[g, :, lanes]
            w_ref[g, 64:128, ROWS3 + 128 * j:ROWS3 + 128 * j + 128] = (
                da[rows] / total
            ).astype(BF16)
            delta_ref[g, :, lanes] = (
                jnp.sum(da[rows] * attended[rows], axis=0, keepdims=True) / total
            )


def middle_call(*args):
    shape = jax.ShapeDtypeStruct
    return pl.pallas_call(
        middle_kernel,
        out_shape=(
            shape((960, 128), BF16),
            shape((960, 128), BF16),
            shape((128, 2560), BF16),
            shape((128, 2560), BF16),
            shape((128, 2560), BF16),
            shape((960, 128), F32),
            shape((960, 128), BF16),
            shape((5, 128, 2 * ROWS3), BF16),
            shape((5, 1, ROWS3), F32),
            shape((960, 1), F32),
        ),
        in_specs=[INV] * 6 + [ANY] * 4,
        out_specs=[INV] * 10,
        scratch_shapes=[
            pltpu.VMEM((960, 960), BF16),
            pltpu.VMEM((960, 2560), BF16),
            pltpu.VMEM((960, 2560), BF16),
            pltpu.VMEM((960, 2560), BF16),
            pltpu.VMEM((960, 128), F32),
            dma_sems(4),
        ],
        compiler_params=plain_params(),
        name="middle",
    )(*args)


def finish_kernel(
    dq_ref, pair_ref, cos_ref, sin_ref, w_ref, x_ref, inv_ref, gain_ref, h_ref, dx_ref, a_ref,
    out_ref, lhs_ref, rhs_ref, ggain_ref,
):
    cosine, sine = cos_ref[...], -sin_ref[...]
    rhs_ref[0:1600, 128:256] = jnp.zeros((1600, 128), BF16)
    rhs_ref[1600:2560, 0:128] = jnp.zeros((960, 128), BF16)
    dx = dx_ref[...]
    rhs_ref[1600:2560, 128:256] = dx.astype(BF16)
    lhs_ref[:, 0:128] = h_ref[...]
    lhs_ref[:, 128:256] = a_ref[...]
    for g in range(KEY_VALUE_HEADS):
        for j in range(QUERY_PER_KV):
            rows = rotate(dq_ref[g, 0:64, token_lanes(j)] * 0.125, cosine, sine)
            rhs_ref[head_rows(3 * g + j), 0:128] = rows.astype(BF16)
        pair = turn(pair_ref[g])
        rhs_ref[head_rows(15 + g), 0:128] = rotate(pair[:64], cosine, sine).astype(BF16)
        rhs_ref[head_rows(20 + g), 0:128] = pair[64:].astype(BF16)
    grad = jnp.dot(w_ref[...], rhs_ref[0:1600, 0:128], preferred_element_type=F32)
    change, ggain_ref[...] = norm_back_rows(
        grad, x_ref[...].astype(F32), inv_ref[...], gain_ref[:, 0:1].astype(F32)
    )
    out_ref[...] = (dx + change).astype(BF16)


def finish_call(*args):
    shape = jax.ShapeDtypeStruct
    return pl.pallas_call(
        finish_kernel,
        out_shape=(
            shape((960, 128), BF16),
            shape((960, 256), BF16),
            shape((2560, 256), BF16),
            shape((960, 1), F32),
        ),
        in_specs=[INV] * 11,
        out_specs=[INV] * 4,
        compiler_params=plain_params(),
        name="finish",
    )(*args)


def shards(
    tokens, positions, w_query, key_weight, value_weight, w_output, gain_attn,
    w_gate, w_up, w_down, gain_mlp, cotangent,
):
    owned_positions = positions[0]
    w_one = jnp.concatenate([w_query, key_weight, value_weight], axis=1)
    gains = jnp.concatenate(
        [
            jnp.broadcast_to(gain_attn[:, None], (240, 64)),
            jnp.broadcast_to(gain_mlp[:, None], (240, 64)),
        ],
        axis=1,
    )
    w_qkv, gains = first_call(w_one, gains)
    half_size = HEAD_SIZE // 2
    frequency = 100000.0 ** (-(jnp.arange(half_size, dtype=F32) * 2.0 / HEAD_SIZE))
    angles = frequency[:, None] * owned_positions.astype(F32)[None, :]
    cosine, sine = jnp.cos(angles), jnp.sin(angles)
    x_turned = tokens[0].T
    dy_turned = cotangent[0].T

    qt, kv_own, h_one, inverse_one = project_call(x_turned, w_qkv, gains, cosine, sine)
    kv_all, bias, u_all, top, total, wo_all, wg_all, wu_all, wd_turned = forward_call(
        kv_own, qt, jnp.broadcast_to(owned_positions[None], (8, 128)),
        w_output, w_gate, w_up, w_down.T,
    )
    out, h_two, dg, dp, z, dx, a, w_back, delta, gain_two = middle_call(
        x_turned, dy_turned, gains, u_all, total, qt, wo_all, wg_all, wu_all, wd_turned
    )
    dq, own_pairs, mlp_own = backward_call(
        kv_all, w_back, bias, top, delta, h_two, dg, dp, dy_turned, z
    )
    grad_in, lhs, rhs, gain_one = finish_call(
        dq, own_pairs, cosine, sine, w_qkv, x_turned, inverse_one, gains, h_one, dx, a
    )
    term_gains = jnp.concatenate([gain_one, gain_two], axis=1).astype(BF16)
    gain_rows = jnp.pad(
        term_gains.reshape(4, 240, 2).transpose(0, 2, 1), ((0, 0), (0, 14), (0, 16))
    ).reshape(64, 256)
    packed = last_call(lhs, rhs, gain_rows, mlp_own)
    (
        sum_query, sum_key, sum_value, sum_output, sum_gains, sum_gate, sum_up, sum_down
    ) = unpack_call(*packed)
    return (
        out.T[None], grad_in.T[None], sum_query, sum_key, sum_value, sum_output,
        sum_gains[0, :240], sum_gate, sum_up, sum_down.T, sum_gains[1, :240],
    )


def solution(mesh):
    in_specs = (
        P("dp", "ctx", None), P("dp", "ctx"),
        P("dp", None), P("dp", None), P("dp", None), P("dp", None), P("dp"),
        P("dp", None), P("dp", None), P("dp", None), P("dp"),
        P("dp", "ctx", None),
    )
    out_specs = (
        P("dp", "ctx", None), P("dp", "ctx", None),
        P("dp", None), P("dp", None), P("dp", None), P("dp", None), P("dp"),
        P("dp", None), P("dp", None), P("dp", None), P("dp"),
    )
    return jax.shard_map(shards, mesh=mesh, in_specs=in_specs, out_specs=out_specs, check_vma=False)
```

```python
import jax
import jax.numpy as jnp
from jax import lax
from jax.experimental import pallas as pl
from jax.experimental.pallas import tpu as pltpu
from jax.sharding import PartitionSpec as P

HQ = 15
KEY_VALUE_HEADS = 5
HEAD_SIZE = 64
QUERY_PER_KV = 3
MESH = pl.DeviceIdType.MESH
VMEM_LIMIT = 60 * 2**20
F32 = jnp.float32
BF16 = jnp.bfloat16
ROWS3 = 384


def coords():
    dp = lax.axis_index("dp")
    ctx = lax.axis_index("ctx")
    return dict(yl=dp // 2, c=dp % 2, yh=ctx // 16, x=(ctx // 4) % 4, z=ctx % 4)


def flip(t):
    return t + 1 - 2 * (t % 2)


def partner(co, d):
    new = dict(co)
    if d == "core":
        new["c"] = 1 - co["c"]
    elif d == "x1":
        new["x"] = flip(co["x"])
    elif d == "x3":
        new["x"] = 3 - co["x"]
    elif d == "z1":
        new["z"] = flip(co["z"])
    elif d == "z3":
        new["z"] = 3 - co["z"]
    else:
        if d in ("y1", "y3"):
            new["yl"] = 1 - co["yl"]
        if d in ("y2", "y3"):
            new["yh"] = 1 - co["yh"]
    return new


def device(co):
    return (co["yl"] * 2 + co["c"], co["yh"] * 16 + co["x"] * 4 + co["z"])


def spans(state, t):
    if state == "all":
        return [(0, 4)]
    if state == "both":
        return [(0, 2)]
    if state == "pair":
        return [(t - t % 2, 2)]
    if state == "anti":
        return [(t, 1), (3 - t, 1)]
    return [(t, 1)]


WIDTH = {"all": 4, "both": 2, "pair": 2, "anti": 2, "one": 1}


def less(state, d):
    new = dict(state)
    axis = d[0]
    if axis == "y":
        new["y"] = "one"
    elif state[axis] == "all":
        new[axis] = "anti" if d[1] == "1" else "pair"
    else:
        new[axis] = "one"
    return new


def more(state, d):
    new = dict(state)
    axis = d[0]
    if axis == "y":
        new["y"] = "both"
    elif state[axis] == "one":
        new[axis] = "pair" if d[1] == "1" else "anti"
    else:
        new[axis] = "all"
    return new


def boxes(state, co, ykey):
    out = []
    place_y = 0
    for ys, yn in spans(state["y"], co[ykey]):
        place_x = 0
        for xs, xn in spans(state["x"], co["x"]):
            place_z = 0
            for zs, zn in spans(state["z"], co["z"]):
                out.append(
                    (
                        (pl.ds(ys, yn), pl.ds(xs, xn), pl.ds(zs, zn)),
                        (pl.ds(place_y, yn), pl.ds(place_x, xn), pl.ds(place_z, zn)),
                        (yn, xn, zn),
                    )
                )
                place_z += zn
            place_x += xn
        place_y += yn
    return out


FULL = dict(y="both", x="all", z="all")
SINGLE = dict(y="one", x="one", z="one")


def order(ydim, part):
    dims = ["x1", "x3", "z1", "z3", ydim]
    return dims[part:] + dims[:part]


def rs_states(ydim, part):
    states = []
    state = FULL
    for d in order(ydim, part):
        state = less(state, d)
        states.append(state)
    return states


def rs_shapes(ydim, block):
    return [
        (WIDTH[s["y"]], WIDTH[s["x"]], WIDTH[s["z"]]) + block
        for part in range(5)
        for s in rs_states(ydim, part)
    ]


class Sems:
    def __init__(self, send, recv):
        self.send, self.recv, self.count = send, recv, 0

    def take(self):
        i = self.count
        self.count += 1
        return self.send.at[i], self.recv.at[i]

    def copy(self, src, dst, co):
        s, r = self.take()
        cp = pltpu.make_async_remote_copy(
            src_ref=src, dst_ref=dst, send_sem=s, recv_sem=r,
            device_id=device(co), device_id_type=MESH,
        )
        cp.start()
        return cp


def greet(co, dims):
    barrier = pltpu.get_barrier_semaphore()
    for d in dims:
        pl.semaphore_signal(
            barrier, inc=1, device_id=device(partner(co, d)), device_id_type=MESH
        )
    pl.semaphore_wait(barrier, len(dims))


def add_boxes(pairs, acc, tail, buf, head):
    for box, place, (yn, xn, zn) in pairs:
        (by, bx, bz), (py, px, pz) = box, place

        def add(i, carry):
            iy, ix = i // xn, i % xn
            here = (by.start + iy, bx.start + ix, bz) + tail
            there = head + (py.start + iy, px.start + ix, pz)
            acc[here] = acc[here] + buf[there]
            return carry

        if yn * xn == 1:
            add(0, 0)
        else:
            lax.fori_loop(0, yn * xn, add, 0)


class PlaneReduce:
    DIMS = ["x1", "x3", "z1", "z3"]

    @classmethod
    def plan(cls, part, y):
        dims = (cls.DIMS[part:] + cls.DIMS[:part])[::-1]
        states = []
        state = dict(y=y, x="all", z="all")
        for d in dims:
            state = less(state, d)
            states.append(state)
        return dims, states

    @classmethod
    def shapes(cls, y, lead, block):
        return [
            lead + (WIDTH[y], WIDTH[s["x"]], WIDTH[s["z"]]) + block
            for part in range(4)
            for s in cls.plan(part, y)[1]
        ]

    def __init__(self, acc, bufs, sems, co, y):
        self.acc, self.bufs, self.sems, self.co, self.y = acc, bufs, sems, co, y
        self.ykey = "yh" if y == "both" else "yl"
        self.quarter = acc.shape[-2] // 4
        self.flying, self.sent = {}, []

    def send(self, tail, lead, part, stage):
        dims, states = self.plan(part, self.y)
        to = partner(self.co, dims[stage])
        rows = pl.ds(self.quarter * part, self.quarter)
        buf = self.bufs[part * 4 + stage]
        out = []
        for box, place, _ in boxes(states[stage], to, self.ykey):
            src = self.acc.at[box + tail + (rows,)]
            out.append(self.sems.copy(src, buf.at[lead + place], to))
        self.flying[lead, part] = out
        self.sent += out

    def step(self, tail, lead, stage):
        for part in range(4):
            if stage > 0:
                for cp in self.flying[lead, part]:
                    cp.wait_recv()
                rows = pl.ds(self.quarter * part, self.quarter)
                add_boxes(
                    boxes(self.plan(part, self.y)[1][stage - 1], self.co, self.ykey),
                    self.acc, tail + (rows,), self.bufs[part * 4 + stage - 1], lead,
                )
            if stage < 4:
                self.send(tail, lead, part, stage)

    def drain(self):
        for cp in self.sent:
            cp.wait_send()


class PairSum:
    def __init__(self, acc, own, last, bufs, sems, co):
        self.acc, self.own, self.last, self.sems, self.co = acc, own, last, sems, co
        self.plane = PlaneReduce(acc, bufs, sems, co, "both")
        self.at, self.halves = {}, {}

    def advance(self, g):
        at = self.at[g] = self.at.get(g, -1) + 1
        co = self.co
        if at < 5:
            self.plane.step((g,), (g,), at)
        if at == 4:
            there = (1 - co["yh"], co["x"], co["z"], g)
            self.halves[g] = self.sems.copy(
                self.acc.at[there], self.last.at[g], partner(co, "y2")
            )
        elif at == 5:
            self.halves[g].wait_recv()
            here = (co["yh"], co["x"], co["z"], g)
            self.own[g] = (
                self.acc[here].astype(F32) + self.last[g].astype(F32)
            ).astype(BF16)

    def drain(self):
        self.plane.drain()
        for cp in self.halves.values():
            cp.wait_send()


class ReduceScatter:
    def __init__(self, acc, bufs, sems, co, ydim):
        self.acc, self.bufs, self.sems, self.co, self.ydim = acc, bufs, sems, co, ydim
        self.ykey = "yl" if ydim == "yl" else "yh"
        self.flying = {}
        self.sent = []

    def start(self, part, stage):
        d = order(self.ydim, part)[stage]
        state = rs_states(self.ydim, part)[stage]
        buf = self.bufs[part * 5 + stage]
        out = []
        if d == "yl":
            half = self.acc.shape[-2] // 2
            ways = [("y1", pl.ds(0, half)), ("y3", pl.ds(half, half))]
        else:
            ways = [(d, slice(None))]
        for way, rows in ways:
            to = partner(self.co, way)
            for box, place, _ in boxes(state, to, self.ykey):
                middle = (slice(None),) * (len(self.acc.shape) - 6)
                src = self.acc.at[box + (part,) + middle + (rows, slice(None))]
                dst = buf.at[place + middle + (rows, slice(None))]
                out.append(self.sems.copy(src, dst, to))
        self.flying[part, stage] = out
        self.sent += out

    def finish(self, part, stage):
        for cp in self.flying[part, stage]:
            cp.wait_recv()
        state = rs_states(self.ydim, part)[stage]
        buf = self.bufs[part * 5 + stage]
        add_boxes(
            boxes(state, self.co, self.ykey), self.acc, (part,), buf, ()
        )

    def drain(self):
        for cp in self.sent:
            cp.wait_send()


class AllGather:
    def __init__(self, buf, sems, co, ydim="y2"):
        self.buf, self.sems, self.co, self.ydim = buf, sems, co, ydim
        self.flying = {}
        self.sent = []

    def start(self, part, stage, pick=slice(None)):
        dims = order(self.ydim, part)
        state = SINGLE
        for d in dims[:stage]:
            state = more(state, d)
        to = partner(self.co, dims[stage])
        out = []
        for box, _, _ in boxes(state, self.co, "yh"):
            ref = self.buf.at[box + (part, pick)]
            out.append(self.sems.copy(ref, ref, to))
        self.flying.setdefault((part, stage), []).extend(out)
        self.sent += out

    def finish(self, part, stage):
        for cp in self.flying[part, stage]:
            cp.wait_recv()

    def drain(self):
        for cp in self.sent:
            cp.wait_send()


class PlaneGather:
    DIMS = ["x1", "x3", "z1", "z3"]

    def __init__(self, buf, places, sems, co):
        self.buf, self.places, self.sems, self.co = buf, places, sems, co
        self.flying, self.sent = {}, []

    def first(self):
        co = self.co
        out = []
        for buf in (self.places, self.buf):
            ref = buf.at[co["yh"], co["x"], co["z"]]
            out.append(self.sems.copy(ref, ref, partner(co, "y2")))
        for cp in out:
            cp.wait_recv()
        self.sent += out

    def start(self, part, stage):
        dims = self.DIMS[part:] + self.DIMS[:part]
        state = dict(y="both", x="one", z="one")
        for d in dims[:stage]:
            state = more(state, d)
        to = partner(self.co, dims[stage])
        rows = pl.ds(32 * part, 32)
        for g in range(5) if stage == 3 else [None]:
            out = []
            for box, _, _ in boxes(state, self.co, "yh"):
                if part == 0 and g in (None, 0):
                    ref = self.places.at[box]
                    out.append(self.sems.copy(ref, ref, to))
                ref = self.buf.at[box + (slice(None) if g is None else g, rows)]
                out.append(self.sems.copy(ref, ref, to))
            self.flying[part, stage, g or 0] = out
            self.sent += out

    def finish(self, part, stage, g=0):
        for cp in self.flying[part, stage, g]:
            cp.wait_recv()

    def drain(self):
        for cp in self.sent:
            cp.wait_send()


class Gather:
    def __init__(self, items, sems, local, co):
        self.items, self.sems, self.local, self.co = items, sems, local, co
        self.waits = []

    def block(self, i, q, first, count):
        src, dst, h, lanes = self.items[i]
        n, width = src.shape
        if lanes:
            where = pl.ds(pl.multiple_of(q * width, 128), width)
            return dst.at[pl.ds(first, count), where]
        return dst.at[pl.ds(pl.multiple_of(q * n + first, 16), count)]

    def start(self):
        co = self.co
        me = co["yl"] * 2 + co["c"]
        self.stage = []
        for i, (src, dst, h, lanes) in enumerate(self.items):
            n = src.shape[0]
            one = self.sems.copy(
                src.at[pl.ds(0, h)], self.block(i, me, 0, h), partner(co, "y1")
            )
            two = None
            if h < n:
                two = self.sems.copy(
                    src.at[pl.ds(h, n - h)], self.block(i, me, h, n - h), partner(co, "y3")
                )
            self.stage.append((one, two))

    def share_own(self):
        co = self.co
        me = co["yl"] * 2 + co["c"]
        for i, (src, dst, h, lanes) in enumerate(self.items):
            whole = self.block(i, me, 0, src.shape[0])
            self.waits.append(self.sems.copy(src, whole, partner(co, "core")))
            cp = pltpu.make_async_copy(src, whole, self.local.at[i])
            cp.start()
            self.waits.append(cp)

    def forward(self, i):
        co = self.co
        src, dst, h, lanes = self.items[i]
        n = src.shape[0]
        q = (1 - co["yl"]) * 2 + co["c"]
        for cp, first, count in zip(self.stage[i], (0, h), (h, n - h)):
            if cp is None:
                continue
            cp.wait_recv()
            ref = self.block(i, q, first, count)
            self.waits.append(self.sems.copy(ref, ref, partner(co, "core")))

    def finish(self):
        for one, two in self.stage:
            one.wait_send()
            if two is not None:
                two.wait_send()
        for cp in self.waits:
            cp.wait()


class Spread:
    CUTS = ((0, 128), (128, 112))

    def __init__(self, src, dst, lanes, axis, sems, local, co):
        self.src, self.dst, self.lanes, self.axis = src, dst, lanes, axis
        self.sems, self.local, self.co = sems, local, co
        self.waits = []

    def piece(self, q, t, first, count):
        rows = (t if self.lanes else q) * 240 + first
        lanes = (q if self.lanes else t) * 640
        return self.dst.at[
            pl.ds(pl.multiple_of(rows, 16), count), pl.ds(pl.multiple_of(lanes, 128), 640)
        ]

    def own(self, t, first, count):
        if self.lanes:
            return self.src.at[pl.ds(pl.multiple_of(240 * t + first, 16), count)]
        return self.src.at[pl.ds(first, count), pl.ds(pl.multiple_of(640 * t, 128), 640)]

    def block(self, q):
        if self.lanes:
            return self.dst.at[:, pl.ds(pl.multiple_of(640 * q, 128), 640)]
        return self.dst.at[pl.ds(pl.multiple_of(240 * q, 16), 240)]

    def start(self):
        co = self.co
        me, t = co["yl"] * 2 + co["c"], co[self.axis]
        self.flying = [
            self.sems.copy(self.own(t, *cut), self.piece(me, t, *cut), partner(co, way))
            for way, cut in zip(("y1", "y3"), self.CUTS)
        ]
        self.sent = list(self.flying)

    def share_own(self):
        co = self.co
        whole = self.block(co["yl"] * 2 + co["c"])
        self.waits.append(self.sems.copy(self.src, whole, partner(co, "core")))
        cp = pltpu.make_async_copy(self.src, whole, self.local)
        cp.start()
        self.waits.append(cp)

    def share(self, step):
        co = self.co
        t = co[self.axis]
        q = (1 - co["yl"]) * 2 + co["c"]
        for cp in self.flying:
            cp.wait_recv()
        self.flying = []
        for cut, edges, other in zip(self.CUTS, ("13", "31"), (flip(t), 3 - t)):
            to = partner(co, self.axis + edges[step])
            for at in (t, other)[:step + 1]:
                ref = self.piece(q, at, *cut)
                self.flying.append(self.sems.copy(ref, ref, to))
        self.sent += self.flying

    def forward(self):
        co = self.co
        for cp in self.flying:
            cp.wait_recv()
        ref = self.block((1 - co["yl"]) * 2 + co["c"])
        self.waits.append(self.sems.copy(ref, ref, partner(co, "core")))

    def finish(self):
        for cp in self.sent:
            cp.wait_send()
        for cp in self.waits:
            cp.wait()


def params(cid):
    return pltpu.CompilerParams(
        collective_id=cid, has_side_effects=True, vmem_limit_bytes=VMEM_LIMIT
    )


def dma_sems(n):
    return pltpu.SemaphoreType.DMA((n,))


ANY = pl.BlockSpec(memory_space=pl.ANY)
INV = pl.BlockSpec(memory_space=pltpu.VMEM)


def first_kernel(w_ref, gain_ref, w_out, gain_out, send, recv, local):
    co = coords()
    greet(co, ("core", "y1", "y3"))
    gather = Gather(
        [(gain_ref, gain_out, 240, False), (w_ref, w_out, 128, False)],
        Sems(send, recv), local, co,
    )
    gather.share_own()
    gather.start()
    gather.forward(0)
    gather.forward(1)
    gather.finish()


def first_call(w_one, gains):
    return pl.pallas_call(
        first_kernel,
        out_shape=(
            jax.ShapeDtypeStruct((960, 1600), BF16),
            jax.ShapeDtypeStruct((960, 128), BF16),
        ),
        in_specs=[INV] * 2,
        out_specs=[ANY] * 2,
        scratch_shapes=[dma_sems(8), dma_sems(8), dma_sems(3)],
        compiler_params=params(1),
        name="gather_first",
    )(w_one, gains)


CHUNK = 512


def over_lanes(left, right):
    return lax.dot_general(
        left, right, (((1,), (1,)), ((), ())), preferred_element_type=F32
    )


def over_dim0(left, right):
    return lax.dot_general(
        left, right, (((0,), (0,)), ((), ())), preferred_element_type=F32
    )


def forward_kernel(
    kv_ref, qt_ref, pos_ref, wo_ref, wg_ref, wu_ref, wd_ref,
    kv_all, bias_ref, u_ref, m_ref, l_ref, wo_all, wg_all, wu_all, wd_all,
    scores, places, send, recv, wsend, wrecv, local,
):
    co = coords()
    greet(co, ("x1", "x3", "z1", "z3", "y2", "core", "y1", "y3"))
    wsems = Sems(wsend, wrecv)
    weights = Gather(
        [
            (wo_ref, wo_all, 128, False),
            (wg_ref, wg_all, 128, False),
        ],
        wsems, local, co,
    )
    spreads = (
        Spread(wu_ref, wu_all, False, "x", wsems, local.at[2], co),
        Spread(wd_ref, wd_all, True, "z", wsems, local.at[3], co),
    )
    here = (co["yh"], co["x"], co["z"])
    kv_all[here] = kv_ref[...]
    places[here] = jnp.broadcast_to(pos_ref[...], (8, 128))
    ag = PlaneGather(kv_all, places, Sems(send, recv), co)
    for item in (weights,) + spreads:
        item.share_own()
    ag.first()
    for part in range(4):
        ag.start(part, 0)
    for spread in spreads:
        spread.start()
    weights.start()
    for stage in range(1, 4):
        if stage == 3:
            for spread in spreads:
                spread.share(0)
        for part in range(4):
            ag.finish(part, stage - 1)
            ag.start(part, stage)
    for part in range(4):
        ag.finish(part, 3, 0)
    steps = lax.broadcasted_iota(jnp.int32, (64, 128), 0)

    def mask(i, carry):
        row = places[i // 16, (i // 4) % 4, i % 4][0:1]
        for half in range(2):
            ahead = pos_ref[0:1] - row[:, 64 * half:64 * half + 1]
            bias_ref[pl.ds(pl.multiple_of(i * 128 + 64 * half, 64), 64)] = jnp.where(
                steps <= ahead, 0.0, -1e30
            ).astype(F32)
        return carry

    lax.fori_loop(0, 32, mask, 0)

    for g in range(KEY_VALUE_HEADS):
        qt = qt_ref[g]
        if g > 0:
            for part in range(4):
                ag.finish(part, 3, g)
        if g == 1:
            for spread in spreads:
                spread.share(1)
        if g == 4:
            weights.forward(0)
            weights.forward(1)

        def score(i, top):
            kv = kv_all[i // 4, i % 4, :, g].reshape(CHUNK, 128)
            s = jnp.dot(kv, qt, preferred_element_type=F32)
            b = bias_ref[pl.ds(i * CHUNK, CHUNK)]
            s = s + jnp.concatenate([b, b, b], axis=1)
            scores[pl.ds(i * CHUNK, CHUNK)] = s
            return jnp.maximum(top, jnp.max(s.reshape(CHUNK // 8, 8, ROWS3), axis=0))

        top = lax.fori_loop(
            0, 8, score, jnp.full((8, ROWS3), -1e30, F32), unroll=8
        )
        top = jnp.max(top, axis=0, keepdims=True)

        def weigh(i, carry):
            total, u = carry
            kv = kv_all[i // 4, i % 4, :, g].reshape(CHUNK, 128)
            e = jnp.exp(scores[pl.ds(i * CHUNK, CHUNK)] - top)
            total = total + jnp.sum(e.reshape(CHUNK // 8, 8, ROWS3), axis=0)
            return total, u + over_dim0(kv, e.astype(BF16))

        carry = (jnp.zeros((8, ROWS3), F32), jnp.zeros((128, ROWS3), F32))
        total, u = lax.fori_loop(0, 8, weigh, carry, unroll=8)
        u_ref[g] = u
        m_ref[g] = top
        l_ref[g] = jnp.sum(total, axis=0, keepdims=True)
    for spread in spreads:
        spread.forward()
    ag.drain()
    weights.finish()
    for spread in spreads:
        spread.finish()


def forward_call(kv, qt, pos, wo, wg, wu, wd):
    shape = jax.ShapeDtypeStruct
    return pl.pallas_call(
        forward_kernel,
        out_shape=(
            shape((2, 4, 4, 5, 128, 128), BF16),
            shape((4096, 128), F32),
            shape((5, 128, ROWS3), F32),
            shape((5, 1, ROWS3), F32),
            shape((5, 1, ROWS3), F32),
            shape((960, 960), BF16),
            shape((960, 2560), BF16),
            shape((960, 2560), BF16),
            shape((960, 2560), BF16),
        ),
        in_specs=[INV] * 7,
        out_specs=[INV] * 5 + [ANY] * 4,
        scratch_shapes=[
            pltpu.VMEM((4096, ROWS3), F32),
            pltpu.VMEM((2, 4, 4, 8, 128), jnp.int32),
            dma_sems(128), dma_sems(128), dma_sems(32), dma_sems(32), dma_sems(4),
        ],
        compiler_params=params(2),
        name="attention_forward",
    )(kv, qt, pos, wo, wg, wu, wd)


WIDE, TALL, GAIN = 240, 640, 256


def slab_shape(kind):
    return (960, 640) if kind == TALL else (kind, 2560)


def term(kind, lhs, rhs, q, p):
    if kind == TALL:
        lanes = pl.ds(pl.multiple_of(640 * q + 128 * p, 128), 128)
        return jnp.dot(lhs[...], rhs[:, lanes], preferred_element_type=F32)
    rows = pl.ds(pl.multiple_of(240 * q, 16), 240)
    lanes = pl.ds(pl.multiple_of(512 * p, 128), 512)
    if kind == GAIN:
        return over_lanes(lhs[rows], rhs[lanes])
    return jnp.dot(lhs[rows], rhs[:, lanes], preferred_element_type=F32)


def part_lanes(kind, p):
    width = 128 if kind == TALL else 512
    return pl.ds(pl.multiple_of(width * p, 128), width)


GRAD_DIMS = ("x1", "x3", "z1", "z3", "y1", "y2", "y3", "core")


def grad_scratch(kinds):
    n = len(kinds)
    blocks = [(2,) + slab_shape(kind) for kind in kinds]
    return (
        [pltpu.VMEM(b, BF16) for b in blocks]
        + [pltpu.VMEM(b, BF16) for b in blocks]
        + [pltpu.VMEM((2, 4, 4, 5, n, 64, 128), BF16)]
        + [pltpu.VMEM(s, BF16) for s in rs_shapes("yl", (n, 64, 128))]
        + [pltpu.VMEM((5, n, 32, 128), BF16)]
        + [dma_sems(64), dma_sems(64), dma_sems(2 * n), dma_sems(2 * n)]
    )


def send_terms(kind, factors, gains, out, got, sems, co):
    lhs, rhs = factors
    copies = []
    for yl in range(2):
        q = yl * 2 + 1 - co["c"]

        def step(p, carry):
            value = term(kind, lhs, rhs, q, p).astype(BF16)
            out[yl, pl.ds(0, value.shape[0]), part_lanes(kind, p)] = value
            return carry

        lax.fori_loop(0, 5, step, 0, unroll=5)
        if kind == GAIN:
            out[yl, 240:256, :] = jnp.zeros((16, 2560), BF16)
            rows = pl.ds(pl.multiple_of(16 * q, 16), 16)
            out[yl, 240:256, 0:256] = gains[rows]
        copies.append(sems.copy(out.at[yl], got.at[yl], partner(co, "core")))
    return copies


def fold_terms(kind, factors, gains, got, copies, put, co):
    lhs, rhs = factors
    for yl in range(2):
        q = yl * 2 + co["c"]
        copies[yl].wait_recv()

        def step(p, carry):
            value = term(kind, lhs, rhs, q, p)
            count = value.shape[0]
            value = value + got[yl, pl.ds(0, count), part_lanes(kind, p)].astype(F32)
            value = value.astype(BF16)
            if count % 64:
                pad = jnp.zeros((64 - count % 64, value.shape[1]), BF16)
                value = jnp.concatenate([value, pad], axis=0)
            for x in range(4):
                for z in range(4):
                    if kind == TALL:
                        first = min(256 * x + 64 * z, 896)
                        block = value[first:first + 64]
                    else:
                        block = value[64 * x:64 * x + 64, 128 * z:128 * z + 128]
                    put(yl, x, z, p, block)
            return carry

        lax.fori_loop(0, 5, step, 0, unroll=5)


class GradSum:
    def __init__(self, kinds, factors, gains, scratch, co):
        n = len(kinds)
        self.kinds, self.factors, self.gains, self.co = kinds, factors, gains, co
        self.outs, self.gots = scratch[:n], scratch[n:2 * n]
        self.acc = scratch[2 * n]
        bufs = scratch[2 * n + 1:2 * n + 26]
        self.last, send, recv, csend, crecv = scratch[2 * n + 26:]
        self.sems, self.core = Sems(send, recv), Sems(csend, crecv)
        self.rs = ReduceScatter(self.acc, bufs, self.sems, co, "yl")
        self.cores = []

    def begin(self, i):
        self.cores += send_terms(
            self.kinds[i], self.factors[i], self.gains, self.outs[i], self.gots[i],
            self.core, self.co,
        )

    def fold(self, i):
        co, kind, got = self.co, self.kinds[i], self.gots[i]

        def put(yl, x, z, p, block):
            self.acc[yl, x, z, p, i] = block

        copies = self.cores[2 * i:2 * i + 2]
        fold_terms(kind, self.factors[i], self.gains, got, copies, put, co)
        if kind == GAIN:
            for yl in range(2):
                q = yl * 2 + co["c"]
                rows = pl.ds(pl.multiple_of(16 * q, 16), 16)
                for z in range(2):
                    lanes = slice(128 * z, 128 * z + 128)
                    self.acc[yl, 3, z, 0, i, 48:64, :] = (
                        self.gains[rows, lanes].astype(F32)
                        + got[yl, 240:256, lanes].astype(F32)
                    ).astype(BF16)

    def launch(self):
        for part in range(5):
            self.rs.start(part, 0)

    def stage(self, stage):
        for part in range(5):
            self.rs.finish(part, stage)
            if stage < 4:
                self.rs.start(part, stage + 1)

    def halve(self):
        co = self.co
        theirs = pl.ds(pl.multiple_of((1 - co["yh"]) * 32, 32), 32)
        self.half = self.sems.copy(
            self.acc.at[co["yl"], co["x"], co["z"], :, :, theirs, :],
            self.last,
            partner(co, "y2"),
        )

    def result(self, p):
        co = self.co
        mine = pl.ds(pl.multiple_of(co["yh"] * 32, 32), 32)
        own = self.acc[co["yl"], co["x"], co["z"], p, :, mine, :]
        return (own.astype(F32) + self.last[p].astype(F32)).astype(BF16)

    def drain(self):
        self.half.wait_send()
        self.rs.drain()
        for cp in self.cores:
            cp.wait_send()


class SlabSum:
    def __init__(self, kind, factors, out_ref, i, scratch, co, late):
        self.late = late
        self.kind, self.factors, self.out_ref, self.i, self.co = kind, factors, out_ref, i, co
        self.out, self.got, self.acc, self.ybuf, self.last = scratch[:5]
        send, recv = scratch[21:]
        self.sems = Sems(send, recv)
        y = "both" if late else "one"
        self.plane = PlaneReduce(self.acc, scratch[5:21], self.sems, co, y)
        self.at = 0

    @staticmethod
    def scratch(kind, late):
        return (
            [pltpu.VMEM((2,) + slab_shape(kind), BF16)] * 2
            + [
                pltpu.VMEM((2, 4, 4, 5, 64, 128), BF16),
                pltpu.VMEM((5, 64, 128) if late else (4, 4, 5, 64, 128), BF16),
                pltpu.VMEM((5, 32, 128), BF16),
            ]
            + [pltpu.VMEM(s, BF16) for s in PlaneReduce.shapes("both" if late else "one", (), (5, 16, 128))]
            + [dma_sems(32), dma_sems(32)]
        )

    def begin(self):
        self.cores = send_terms(
            self.kind, self.factors, None, self.out, self.got, self.sems, self.co
        )

    def fold(self):
        def put(yl, x, z, p, block):
            self.acc[yl, x, z, p] = block

        fold_terms(self.kind, self.factors, None, self.got, self.cores, put, self.co)
        if self.late:
            self.plane.step((slice(None),), (), 0)
        else:
            self.send_y()

    def send_y(self):
        co = self.co
        self.halves = []
        for way, first in (("y1", 0), ("y3", 32)):
            if self.late:
                rows = (slice(None), pl.ds(first, 32))
                src = self.acc.at[(1 - co["yl"], co["x"], co["z"]) + rows]
            else:
                rows = (slice(None),) * 3 + (pl.ds(first, 32),)
                src = self.acc.at[(1 - co["yl"],) + rows]
            self.halves.append(self.sems.copy(src, self.ybuf.at[rows], partner(co, way)))

    def add_y(self):
        co = self.co
        yl = co["yl"]
        for cp in self.halves:
            cp.wait_recv()

        def add(here, there):
            self.acc[(yl,) + here] = self.acc[(yl,) + here] + self.ybuf[there]

        if self.late:
            add((co["x"], co["z"]), (slice(None),))
        else:

            def step(i, carry):
                add((i // 4, i % 4), (i // 4, i % 4))
                return carry

            lax.fori_loop(0, 16, step, 0)

    def send_half(self):
        co = self.co
        theirs = pl.ds(pl.multiple_of((1 - co["yh"]) * 32, 32), 32)
        src = self.acc.at[co["yl"], co["x"], co["z"], :, theirs, :]
        self.half = self.sems.copy(src, self.last, partner(co, "y2"))

    def advance(self):
        at, co = self.at, self.co
        self.at += 1
        tail = (slice(None),)
        if self.late:
            if at < 4:
                self.plane.step(tail, (), at + 1)
            if at == 3:
                self.send_y()
            if at == 4:
                self.add_y()
                self.send_half()
        else:
            if at == 0:
                self.add_y()
            if at < 5:
                self.plane.step(tail, (), at)
            if at == 4:
                self.send_half()
        if at == 5:
            self.half.wait_recv()
            mine = pl.ds(pl.multiple_of(co["yh"] * 32, 32), 32)
            own = self.acc[co["yl"], co["x"], co["z"], :, mine, :]
            self.out_ref[:, self.i] = (own.astype(F32) + self.last[...].astype(F32)).astype(BF16)

    def drain(self):
        self.plane.drain()
        self.half.wait_send()
        for cp in self.cores + self.halves:
            cp.wait_send()


MLP = (WIDE, WIDE, TALL)
LATE = (True, False, False)


def backward_kernel(
    kv_ref, w_ref, bias_ref, m_ref, delta_ref, h_ref, dg_ref, dp_ref, dy_ref, z_ref,
    dq_ref, own_ref, mlp_ref, acc, last, *rest,
):
    bufs, (send, recv) = rest[:16], rest[16:18]
    co = coords()
    greet(co, GRAD_DIMS)
    factors = ((h_ref, dg_ref), (h_ref, dp_ref), (dy_ref, z_ref))
    slabs, at = [], 18
    for i, kind in enumerate(MLP):
        count = len(SlabSum.scratch(kind, LATE[i]))
        slabs.append(SlabSum(kind, factors[i], mlp_ref, i, rest[at:at + count], co, LATE[i]))
        at += count
    for slab in slabs:
        slab.begin()
    slabs[0].fold()
    slabs[1].fold()
    pairs = PairSum(acc, own_ref, last, bufs, Sems(send, recv), co)
    starts = (2, 4, 8)
    for g in range(KEY_VALUE_HEADS):
        w = w_ref[g]
        top, delta = m_ref[g], delta_ref[g]

        def step(i, dq):
            kv = kv_ref[i // 4, i % 4, :, g].reshape(CHUNK, 128)
            both = jnp.dot(kv, w, preferred_element_type=F32)
            b = bias_ref[pl.ds(i * CHUNK, CHUNK)]
            s = both[:, :ROWS3] + jnp.concatenate([b, b, b], axis=1)
            e = jnp.exp(s - top)
            ds = (e * (both[:, ROWS3:] - delta)).astype(BF16)
            pair = jnp.concatenate([ds, e.astype(BF16)], axis=1)
            dkv = over_lanes(pair, w)
            acc[i // 4, i % 4, :, g] = dkv.astype(BF16).reshape(4, 128, 128)
            return dq + over_dim0(kv, ds)

        dq = jnp.zeros((128, ROWS3), F32)
        for half in range(2):
            dq = lax.fori_loop(4 * half, 4 * half + 4, step, dq, unroll=4)
            if half == 1:
                dq_ref[g] = dq
                pairs.advance(g)
            now = 2 * g + half
            for early in range(g):
                if pairs.at[early] < (5 if now >= 8 else 3):
                    pairs.advance(early)
            if now == 0:
                slabs[2].fold()
            for slab, start in zip(slabs, starts):
                if now >= start and slab.at < 6:
                    slab.advance()
    for turn in range(5):
        for g in (4, 3, 2, 1, 0):
            if pairs.at[g] < 5:
                pairs.advance(g)
        for slab in slabs:
            if slab.at < 6:
                slab.advance()
    pairs.drain()
    for slab in slabs:
        slab.drain()


def backward_call(*args):
    shape = jax.ShapeDtypeStruct
    return pl.pallas_call(
        backward_kernel,
        out_shape=(
            shape((5, 128, ROWS3), F32),
            shape((5, 128, 128), BF16),
            shape((5, 3, 32, 128), BF16),
        ),
        in_specs=[INV] * 10,
        out_specs=[INV] * 3,
        scratch_shapes=[
            pltpu.VMEM((2, 4, 4, 5, 128, 128), BF16),
            pltpu.VMEM((5, 128, 128), BF16),
        ]
        + [pltpu.VMEM(s, BF16) for s in PlaneReduce.shapes("both", (5,), (32, 128))]
        + [dma_sems(128), dma_sems(128)]
        + [s for kind, late in zip(MLP, LATE) for s in SlabSum.scratch(kind, late)],
        compiler_params=params(3),
        name="attention_backward",
    )(*args)


LAST = (GAIN,)


def last_kernel(lhs_ref, rhs_ref, gain_ref, mlp_ref, out_ref, mlp_out, *rest):
    msend, mrecv, send, recv = rest[:4]
    co = coords()
    greet(co, GRAD_DIMS)
    here = (co["yh"], co["x"], co["z"])
    grad = GradSum(LAST, ((lhs_ref, rhs_ref),), gain_ref, rest[4:], co)
    mlp_out[here] = mlp_ref[...]
    mlp = AllGather(mlp_out, Sems(msend, mrecv), co)
    for part in range(5):
        mlp.start(part, 0)

    def mlp_stage(stage):
        for part in range(5):
            mlp.finish(part, stage)
            if stage < 3:
                mlp.start(part, stage + 1)

    def mlp_last(slab):
        for part in range(5):
            mlp.start(part, 4, slab)

    grad.begin(0)
    mlp_stage(0)
    mlp_stage(1)
    grad.fold(0)
    grad.launch()
    mlp_stage(2)
    grad.stage(0)
    grad.stage(1)
    mlp_stage(3)
    for i in range(3):
        mlp_last(i)
        grad.stage(2 + i)
    grad.halve()
    grad.half.wait_recv()
    for p in range(5):
        out_ref[here + (p,)] = grad.result(p)
    ag = AllGather(out_ref, Sems(send, recv), co)
    for part in range(5):
        ag.start(part, 0)
    for stage in range(5):
        for part in range(5):
            ag.finish(part, stage)
            if stage < 4:
                ag.start(part, stage + 1)
    mlp_stage(4)
    grad.drain()
    mlp.drain()
    ag.drain()


def last_call(*args):
    shape = jax.ShapeDtypeStruct
    return pl.pallas_call(
        last_kernel,
        out_shape=(
            shape((2, 4, 4, 5, 1, 32, 128), BF16),
            shape((2, 4, 4, 5, 3, 32, 128), BF16),
        ),
        in_specs=[INV] * 4,
        out_specs=[INV, INV],
        scratch_shapes=[dma_sems(64)] * 4 + grad_scratch(LAST),
        compiler_params=params(4),
        name="last_gradients",
    )(*args)


def unpack_kernel(first, second, q_ref, k_ref, v_ref, o_ref, gain_ref, *rest):
    outs, pairs = rest[:-1], rest[-1]
    for x in range(4):
        for yh in range(2):
            at = 64 * x + 32 * yh
            value = jnp.concatenate(
                [first[yh, x, z, p, 0].astype(F32) for p in range(5) for z in range(4)], axis=1
            )
            rows = min(32, 240 - at)
            for ref, lane in ((q_ref, 0), (o_ref, 1600)):
                ref[at:at + rows] = value[:rows, lane:lane + ref.shape[1]]
            pairs[at:at + 32] = value[:, 896:1664]
            if rows < 32:
                gain_ref[...] = value[rows:, :256]
    k_ref[...] = pairs[:, 0:384].T[64:384, :240]
    v_ref[...] = pairs[:, 384:768].T[:320, :240]
    for i, kind in enumerate(MLP):

        def part(p, carry):
            for x in range(4):
                for z in range(4):
                    for yh in range(2):
                        block = second[yh, x, z, p, i].astype(F32)
                        if kind != TALL:
                            rows = min(32, kind - 64 * x - 32 * yh)
                            lanes = pl.ds(pl.multiple_of(512 * p + 128 * z, 128), 128)
                            outs[i][pl.ds(64 * x + 32 * yh, rows), lanes] = block[:rows]
                        elif x * 4 + z < 15:
                            lanes = pl.ds(pl.multiple_of(128 * p, 128), 128)
                            outs[i][pl.ds(256 * x + 64 * z + 32 * yh, 32), lanes] = block
            return carry

        lax.fori_loop(0, 5, part, 0)


def unpack_call(first, second):
    shapes = [(240, 960), (320, 240), (320, 240), (240, 960), (16, 256)]
    shapes += [slab_shape(kind) for kind in MLP]
    return pl.pallas_call(
        unpack_kernel,
        out_shape=tuple(jax.ShapeDtypeStruct(s, F32) for s in shapes),
        in_specs=[INV, INV],
        out_specs=[INV] * len(shapes),
        scratch_shapes=[pltpu.VMEM((256, 768), F32)],
        compiler_params=pltpu.CompilerParams(vmem_limit_bytes=VMEM_LIMIT),
        name="unpack",
    )(first, second)


EPS = 1e-05


def turn(value):
    return value.astype(F32).T


def rms_rows(x):
    return lax.rsqrt(jnp.mean(x * x, axis=0, keepdims=True) + EPS)


def norm_back_rows(grad, x, inverse, gain):
    gain_grad = jnp.sum(grad * x * inverse, axis=1, keepdims=True)
    scaled = grad * gain
    mean = jnp.mean(scaled * x, axis=0, keepdims=True)
    return inverse * scaled - x * (inverse * inverse * inverse) * mean, gain_grad


def rotate(rows, cosine, sine):
    a, b = rows[:32], rows[32:]
    return jnp.concatenate([a * cosine - b * sine, b * cosine + a * sine], axis=0)


def head_rows(i):
    return slice(64 * i, 64 * i + 64)


def token_lanes(j):
    return slice(128 * j, 128 * j + 128)


def project_kernel(x_ref, w_ref, gain_ref, cos_ref, sin_ref, qt_ref, kv_ref, h_ref, inv_ref, raw):
    x = x_ref[...].astype(F32)
    inverse = rms_rows(x)
    inv_ref[...] = inverse
    normed = x * inverse * gain_ref[:, 0:1].astype(F32)
    h_ref[...] = normed.astype(BF16)
    rows = turn(normed).astype(BF16)
    for first, count in ((0, 512), (512, 512), (1024, 576)):
        lanes = slice(first, first + count)
        part = jnp.dot(rows, w_ref[:, lanes], preferred_element_type=F32)
        raw[lanes] = part.T
    cosine, sine = cos_ref[...], sin_ref[...]
    for g in range(KEY_VALUE_HEADS):
        for j in range(QUERY_PER_KV):
            q = rotate(raw[head_rows(3 * g + j)], cosine, sine).astype(BF16)
            qt_ref[g, 0:64, token_lanes(j)] = q * BF16(0.125)
        qt_ref[g, 64:128, :] = jnp.zeros((64, ROWS3), BF16)
        k = rotate(raw[head_rows(15 + g)], cosine, sine)
        pair = jnp.concatenate([k, raw[head_rows(20 + g)]], axis=0)
        kv_ref[g] = pair.T.astype(BF16)


def plain_params():
    return pltpu.CompilerParams(vmem_limit_bytes=VMEM_LIMIT)


def project_call(*args):
    shape = jax.ShapeDtypeStruct
    return pl.pallas_call(
        project_kernel,
        out_shape=(
            shape((5, 128, ROWS3), BF16),
            shape((5, 128, 128), BF16),
            shape((960, 128), BF16),
            shape((1, 128), F32),
        ),
        in_specs=[INV] * 5,
        out_specs=[INV] * 4,
        scratch_shapes=[pltpu.VMEM((1600, 128), F32)],
        compiler_params=plain_params(),
        name="project",
    )(*args)


def middle_kernel(
    x_ref, dy_ref, gain_ref, u_ref, l_ref, qt_ref, wo_hbm, wg_hbm, wu_hbm, wd_hbm,
    out_ref, h_ref, dg_ref, dp_ref, z_ref, dx_ref, a_ref, w_ref, delta_ref, ggain_ref,
    wo, wg, wu, wd, attended, sems,
):
    loads = []
    for i, (src, dst) in enumerate(((wo_hbm, wo), (wg_hbm, wg), (wu_hbm, wu), (wd_hbm, wd))):
        cp = pltpu.make_async_copy(src, dst, sems.at[i])
        cp.start()
        loads.append(cp)
    for g in range(KEY_VALUE_HEADS):
        for j in range(QUERY_PER_KV):
            lanes = token_lanes(j)
            attended[head_rows(3 * g + j)] = u_ref[g, 64:128, lanes] / l_ref[g, :, lanes]
    a_ref[...] = attended[...].astype(BF16)
    a_rows = attended[...].T.astype(BF16)
    dy_turned = dy_ref[...].astype(F32)
    dy_rows = dy_turned.T.astype(BF16)
    loads[0].wait()
    branch = jnp.dot(a_rows, wo[...], preferred_element_type=F32)
    x2 = x_ref[...].astype(F32) + branch.T
    inverse = rms_rows(x2)
    gain = gain_ref[:, 64:65].astype(F32)
    normed = x2 * inverse * gain
    h_ref[...] = normed.astype(BF16)
    h_rows = normed.T.astype(BF16)
    for cp in loads[1:]:
        cp.wait()

    def hidden(i, carry):
        lanes = pl.ds(pl.multiple_of(i * 512, 128), 512)
        gate = jnp.dot(h_rows, wg[:, lanes], preferred_element_type=F32)
        upper = jnp.dot(h_rows, wu[:, lanes], preferred_element_type=F32)
        dz = jnp.dot(dy_rows, wd[:, lanes], preferred_element_type=F32)
        sigma = jax.nn.sigmoid(gate)
        silu = gate * sigma
        z_ref[:, lanes] = (silu * upper).astype(BF16)
        dg_ref[:, lanes] = (dz * upper * sigma * (1.0 + gate * (1.0 - sigma))).astype(BF16)
        dp_ref[:, lanes] = (dz * silu).astype(BF16)
        return carry

    lax.fori_loop(0, 5, hidden, 0, unroll=5)

    def back(i, carry):
        out, grad = carry
        lanes = pl.ds(pl.multiple_of(i * 512, 128), 512)
        out = out + over_lanes(wd[:, lanes], z_ref[:, lanes])
        grad = grad + over_lanes(wg[:, lanes], dg_ref[:, lanes])
        grad = grad + over_lanes(wu[:, lanes], dp_ref[:, lanes])
        return out, grad

    out, grad = lax.fori_loop(
        0, 5, back, (x2, jnp.zeros((960, 128), F32)), unroll=5
    )
    out_ref[...] = out.astype(BF16)
    change, ggain_ref[...] = norm_back_rows(grad, x2, inverse, gain)
    dx = dy_turned + change
    dx_ref[...] = dx
    da = jnp.dot(wo[...], dx.astype(BF16), preferred_element_type=F32)
    for g in range(KEY_VALUE_HEADS):
        w_ref[g, :, 0:ROWS3] = qt_ref[g]
        w_ref[g, 0:64, ROWS3:] = jnp.zeros((64, ROWS3), BF16)
        for j in range(QUERY_PER_KV):
            lanes = token_lanes(j)
            rows = head_rows(3 * g + j)
            total = l_ref[g, :, lanes]
            w_ref[g, 64:128, ROWS3 + 128 * j:ROWS3 + 128 * j + 128] = (
                da[rows] / total
            ).astype(BF16)
            delta_ref[g, :, lanes] = (
                jnp.sum(da[rows] * attended[rows], axis=0, keepdims=True) / total
            )


def middle_call(*args):
    shape = jax.ShapeDtypeStruct
    return pl.pallas_call(
        middle_kernel,
        out_shape=(
            shape((960, 128), BF16),
            shape((960, 128), BF16),
            shape((128, 2560), BF16),
            shape((128, 2560), BF16),
            shape((128, 2560), BF16),
            shape((960, 128), F32),
            shape((960, 128), BF16),
            shape((5, 128, 2 * ROWS3), BF16),
            shape((5, 1, ROWS3), F32),
            shape((960, 1), F32),
        ),
        in_specs=[INV] * 6 + [ANY] * 4,
        out_specs=[INV] * 10,
        scratch_shapes=[
            pltpu.VMEM((960, 960), BF16),
            pltpu.VMEM((960, 2560), BF16),
            pltpu.VMEM((960, 2560), BF16),
            pltpu.VMEM((960, 2560), BF16),
            pltpu.VMEM((960, 128), F32),
            dma_sems(4),
        ],
        compiler_params=plain_params(),
        name="middle",
    )(*args)


def finish_kernel(
    dq_ref, pair_ref, cos_ref, sin_ref, w_ref, x_ref, inv_ref, gain_ref, h_ref, dx_ref, a_ref,
    out_ref, lhs_ref, rhs_ref, ggain_ref,
):
    cosine, sine = cos_ref[...], -sin_ref[...]
    rhs_ref[0:1600, 128:256] = jnp.zeros((1600, 128), BF16)
    rhs_ref[1600:2560, 0:128] = jnp.zeros((960, 128), BF16)
    dx = dx_ref[...]
    rhs_ref[1600:2560, 128:256] = dx.astype(BF16)
    lhs_ref[:, 0:128] = h_ref[...]
    lhs_ref[:, 128:256] = a_ref[...]
    for g in range(KEY_VALUE_HEADS):
        for j in range(QUERY_PER_KV):
            rows = rotate(dq_ref[g, 0:64, token_lanes(j)] * 0.125, cosine, sine)
            rhs_ref[head_rows(3 * g + j), 0:128] = rows.astype(BF16)
        pair = turn(pair_ref[g])
        rhs_ref[head_rows(15 + g), 0:128] = rotate(pair[:64], cosine, sine).astype(BF16)
        rhs_ref[head_rows(20 + g), 0:128] = pair[64:].astype(BF16)
    grad = jnp.dot(w_ref[...], rhs_ref[0:1600, 0:128], preferred_element_type=F32)
    change, ggain_ref[...] = norm_back_rows(
        grad, x_ref[...].astype(F32), inv_ref[...], gain_ref[:, 0:1].astype(F32)
    )
    out_ref[...] = (dx + change).astype(BF16)


def finish_call(*args):
    shape = jax.ShapeDtypeStruct
    return pl.pallas_call(
        finish_kernel,
        out_shape=(
            shape((960, 128), BF16),
            shape((960, 256), BF16),
            shape((2560, 256), BF16),
            shape((960, 1), F32),
        ),
        in_specs=[INV] * 11,
        out_specs=[INV] * 4,
        compiler_params=plain_params(),
        name="finish",
    )(*args)


def shards(
    tokens, positions, w_query, key_weight, value_weight, w_output, gain_attn,
    w_gate, w_up, w_down, gain_mlp, cotangent,
):
    owned_positions = positions[0]
    w_one = jnp.concatenate([w_query, key_weight, value_weight], axis=1)
    gains = jnp.concatenate(
        [
            jnp.broadcast_to(gain_attn[:, None], (240, 64)),
            jnp.broadcast_to(gain_mlp[:, None], (240, 64)),
        ],
        axis=1,
    )
    w_qkv, gains = first_call(w_one, gains)
    half_size = HEAD_SIZE // 2
    frequency = 100000.0 ** (-(jnp.arange(half_size, dtype=F32) * 2.0 / HEAD_SIZE))
    angles = frequency[:, None] * owned_positions.astype(F32)[None, :]
    cosine, sine = jnp.cos(angles), jnp.sin(angles)
    x_turned = tokens[0].T
    dy_turned = cotangent[0].T

    qt, kv_own, h_one, inverse_one = project_call(x_turned, w_qkv, gains, cosine, sine)
    kv_all, bias, u_all, top, total, wo_all, wg_all, wu_all, wd_turned = forward_call(
        kv_own, qt, positions,
        w_output, w_gate, w_up, w_down.T,
    )
    out, h_two, dg, dp, z, dx, a, w_back, delta, gain_two = middle_call(
        x_turned, dy_turned, gains, u_all, total, qt, wo_all, wg_all, wu_all, wd_turned
    )
    dq, own_pairs, mlp_own = backward_call(
        kv_all, w_back, bias, top, delta, h_two, dg, dp, dy_turned, z
    )
    grad_in, lhs, rhs, gain_one = finish_call(
        dq, own_pairs, cosine, sine, w_qkv, x_turned, inverse_one, gains, h_one, dx, a
    )
    term_gains = jnp.concatenate([gain_one, gain_two], axis=1).astype(BF16)
    gain_rows = jnp.pad(
        term_gains.reshape(4, 240, 2).transpose(0, 2, 1), ((0, 0), (0, 14), (0, 16))
    ).reshape(64, 256)
    packed = last_call(lhs, rhs, gain_rows, mlp_own)
    (
        sum_query, sum_key, sum_value, sum_output, sum_gains, sum_gate, sum_up, sum_down
    ) = unpack_call(*packed)
    return (
        out.T[None], grad_in.T[None], sum_query, sum_key.T, sum_value.T, sum_output,
        sum_gains[0, :240], sum_gate, sum_up, sum_down.T, sum_gains[1, :240],
    )


def solution(mesh):
    in_specs = (
        P("dp", "ctx", None), P("dp", "ctx"),
        P("dp", None), P("dp", None), P("dp", None), P("dp", None), P("dp"),
        P("dp", None), P("dp", None), P("dp", None), P("dp"),
        P("dp", "ctx", None),
    )
    out_specs = (
        P("dp", "ctx", None), P("dp", "ctx", None),
        P("dp", None), P("dp", None), P("dp", None), P("dp", None), P("dp"),
        P("dp", None), P("dp", None), P("dp", None), P("dp"),
    )
    return jax.shard_map(shards, mesh=mesh, in_specs=in_specs, out_specs=out_specs, check_vma=False)
```
